32 devices in a mesh: groups: 2 (over x), track: 16 (over z, y, core).
Axes of the slice: x: 2, y: 2, z: 4, core: 2. Of those that a mesh axis runs over, the one named last changes fastest.
Arguments:
- volume: bfloat16 [96, 96, 8, 128], P(None, ('groups', 'track')), parts along dimension 1, may hold values from -400 to 400
- labels: int32 [96, 8, 128], P(('groups', 'track')), parts along dimension 0, may hold values from 0 to 3
- conv_taps: float32 [2, 3, 7, 96], replicated, may hold values from -2 to 2
- norm_gain: float32 [2, 96], replicated, may hold values from 0.1 to 1.9
- weight_in: bfloat16 [2, 384, 96], replicated, may hold values from -0.625 to 0.625
- bias_in: float32 [2, 384], replicated, may hold values from -3 to 3
- weight_out: bfloat16 [2, 96, 384], replicated, may hold values from -0.3125 to 0.3125
- layer_scale: float32 [2, 96], replicated, may hold values from 0.3 to 1
- head_weight: bfloat16 [4, 96], replicated, may hold values from -0.625 to 0.625
- head_bias: float32 [4], replicated, may hold values from -4 to 4
Outputs:
- input_grad: float32 [96, 96, 8, 128], P(None, ('groups', 'track')), parts along dimension 1
- grad_taps: float32 [4, 3, 7, 96], P('groups'), parts along dimension 0
- grad_gain: float32 [4, 96], P('groups'), parts along dimension 0
- grad_weight_in: float32 [4, 384, 96], P('groups'), parts along dimension 0
- grad_bias_in: float32 [4, 384], P('groups'), parts along dimension 0
- grad_weight_out: float32 [4, 96, 384], P('groups'), parts along dimension 0
- grad_scale: float32 [4, 96], P('groups'), parts along dimension 0
- grad_head_weight: float32 [8, 96], P('groups'), parts along dimension 0
- grad_head_bias: float32 [8], P('groups'), parts along dimension 0
The draws below stay inside these ranges and needn't reach their ends.
There are 2 independent parts, one for each index of `groups`. The reference program is written for one: setup_inputs(seed, part) draws one part's arguments, and reference() takes and returns one part's arrays. A program takes and returns all parts, laid end to end along the dimension named above; an argument that names none is the same for every part. Nothing has to cross between parts.
All inputs are finite; a program needn't handle non-finite values.
Results may differ from the reference program's by a relative error of at most 0.0046.
Values may be sent and summed in bfloat16 or wider, within the bound.
No kernel may reach another device: no remote copies, remote signals or barrier semaphores. Data moves between devices by JAX's collectives and lax.ppermute only.
A program may use at most 192 MiB of HBM per device.

```python
import math
import jax
import jax.numpy as jnp
from jax import lax

C = 96
FF = 384
K = 4
TAPS = 7
SECTIONS = 2
Y = 8
Z = 128
X = 48
VOXELS = 49152
N_TRACK = 16


def draw_volume(key, part):
    key = jax.random.fold_in(key, 11)
    extent = (C, X, Y, Z)
    key_base = jax.random.fold_in(key, 0)
    values = jnp.clip(jax.random.normal(key_base, extent, jnp.float32), -6.0, 6.0)
    return values.astype(jnp.bfloat16)


def touch_ends(array, rng, smallest, high):
    longest = array.shape.index(max(array.shape))
    spots = []
    for shift in (0, 1):
        where = [jax.random.randint(jax.random.fold_in(rng, axis), (), 0, length) for axis, length in enumerate(array.shape)]
        where[longest] = (where[longest] + shift) % array.shape[longest]
        spots.append(tuple(where))
    return array.at[spots[0]].set(smallest).at[spots[1]].set(high)


def bell_draw(stream_key, shape, scale, limit, kind=jnp.bfloat16):
    array = jax.random.normal(stream_key, shape, jnp.float32) * scale
    return jnp.minimum(jnp.maximum(array, -limit), limit).astype(kind)


def setup_inputs(seed: int = 0, part: int = 0) -> dict:
    key_list = jax.random.split(jax.random.key(seed), 11)
    part_keys = jax.random.split(jax.random.fold_in(key_list[10], part), 11)
    volume = draw_volume(jax.random.fold_in(jax.random.fold_in(key_list[10], part), 71), part)
    labels = touch_ends(jax.random.randint(part_keys[1], (X, Y, Z), 0, K), jax.random.fold_in(part_keys[1], 1), 0, K - 1).astype(jnp.int32)
    conv_taps = bell_draw(key_list[2], (SECTIONS, 3, TAPS, C), TAPS ** -0.5, 2.0, jnp.float32)
    norm_gain = jnp.clip(1.0 + 0.18 * jax.random.normal(key_list[3], (SECTIONS, C), jnp.float32), 0.1, 1.9)
    weight_in = bell_draw(key_list[4], (SECTIONS, FF, C), C ** -0.5, 0.625)
    bias_in = bell_draw(key_list[5], (SECTIONS, FF), 0.5, 3.0, jnp.float32)
    weight_out = bell_draw(key_list[6], (SECTIONS, C, FF), FF ** -0.5, 0.3125)
    layer_scale = jnp.clip(jnp.exp(jax.random.uniform(key_list[7], (SECTIONS, C), jnp.float32, math.log(0.3), math.log(1.0))), 0.3, 1.0)
    head_weight = bell_draw(key_list[8], (K, C), C ** -0.5, 0.625)
    head_bias = bell_draw(key_list[9], (K,), 1.0, 4.0, jnp.float32)
    return dict(volume=volume, labels=labels, conv_taps=conv_taps, norm_gain=norm_gain, weight_in=weight_in, bias_in=bias_in, weight_out=weight_out, layer_scale=layer_scale, head_weight=head_weight, head_bias=head_bias)


def sweep(field, coeffs, axis):
    radius = coeffs.shape[0] // 2
    length = field.shape[axis] - 2 * radius
    summed = None
    for offset in range(coeffs.shape[0]):
        window = lax.slice_in_dim(field, offset, offset + length, axis=axis)
        weighted = coeffs[offset][:, None, None, None] * window
        summed = weighted if summed is None else summed + weighted
    return summed

def spread(extended, conv_taps, norm_gain):
    radius = conv_taps.shape[1] // 2
    mixed = sweep(extended, conv_taps[0], 1)
    mixed = sweep(jnp.pad(mixed, ((0, 0), (0, 0), (radius, radius), (0, 0))), conv_taps[1], 2)
    mixed = sweep(jnp.pad(mixed, ((0, 0), (0, 0), (0, 0), (radius, radius))), conv_taps[2], 3)
    centred = mixed - lax.optimization_barrier(jnp.mean(mixed, axis=0, keepdims=True))
    variance = lax.optimization_barrier(jnp.mean(centred * centred, axis=0, keepdims=True))
    return centred * lax.rsqrt(variance + 1e-06) * norm_gain[:, None, None, None]

def lift(flattened, center, weight_in, bias_in, weight_out, layer_scale):
    hidden = jnp.dot(weight_in, flattened, preferred_element_type=jnp.float32) + bias_in[:, None]
    activated = jax.nn.gelu(hidden).astype(jnp.bfloat16)
    return center + layer_scale[:, None] * jnp.dot(weight_out, activated, preferred_element_type=jnp.float32)

def pointwise_back(flattened, grad_out, weight_in, bias_in, weight_out, layer_scale):
    hidden = jnp.dot(weight_in, flattened, preferred_element_type=jnp.float32) + bias_in[:, None]
    activated = jax.nn.gelu(hidden).astype(jnp.bfloat16)
    lifted = jnp.dot(weight_out, activated, preferred_element_type=jnp.float32)
    grad_scale = lax.optimization_barrier(jnp.sum(grad_out * lifted, axis=1))
    grad_lift = (grad_out * layer_scale[:, None]).astype(jnp.bfloat16)
    grad_weight_out = lax.dot_general(grad_lift, activated, (((1,), (1,)), ((), ())), preferred_element_type=jnp.float32)
    grad_act = lax.dot_general(weight_out, grad_lift, (((0,), (0,)), ((), ())), preferred_element_type=jnp.float32)
    unused, gelu_back = jax.vjp(jax.nn.gelu, hidden)
    grad_hidden = gelu_back(grad_act)[0]
    grad_bias = lax.optimization_barrier(jnp.sum(grad_hidden, axis=1))
    grad_hid = grad_hidden.astype(jnp.bfloat16)
    grad_weight_in = lax.dot_general(grad_hid, flattened, (((1,), (1,)), ((), ())), preferred_element_type=jnp.float32)
    grad_normed = lax.dot_general(weight_in, grad_hid, (((0,), (0,)), ((), ())), preferred_element_type=jnp.float32)
    return (grad_normed, (grad_weight_in, grad_bias, grad_weight_out, grad_scale))

def head_back(final, labels, head_weight, head_bias):
    logits = jnp.dot(head_weight, final, preferred_element_type=jnp.float32) + head_bias[:, None]
    probability = jax.nn.softmax(logits, axis=0)
    classes = jnp.arange(head_weight.shape[0], dtype=jnp.int32)
    onehot = (labels[None, :] == classes[:, None]).astype(jnp.float32)
    grad_logits = probability - onehot
    grad_bias = lax.optimization_barrier(jnp.sum(grad_logits, axis=1))
    grad_low = grad_logits.astype(jnp.bfloat16)
    grad_weight = lax.dot_general(grad_low, final, (((1,), (1,)), ((), ())), preferred_element_type=jnp.float32)
    grad_final = lax.dot_general(head_weight, grad_low, (((0,), (0,)), ((), ())), preferred_element_type=jnp.float32)
    return (grad_final, grad_weight, grad_bias)

def to_blocks(flattened, count):
    channels, voxels = flattened.shape
    return jnp.moveaxis(flattened.reshape(channels, count, voxels // count), 1, 0)

def from_blocks(blocks):
    count, channels, voxels = blocks.shape
    return jnp.moveaxis(blocks, 0, 1).reshape(channels, count * voxels)

def section_forward(extended, conv_taps, norm_gain, weight_in, bias_in, weight_out, layer_scale):
    radius = conv_taps.shape[1] // 2
    normed = spread(extended, conv_taps, norm_gain)
    extent = normed.shape
    flattened = normed.reshape(extent[0], -1).astype(jnp.bfloat16)
    center = extended[:, radius:radius + extent[1]].reshape(extent[0], -1)
    lifted = lax.map(lambda pieces: lift(pieces[0], pieces[1], weight_in, bias_in, weight_out, layer_scale), (to_blocks(flattened, N_TRACK), to_blocks(center, N_TRACK)))
    return from_blocks(lifted).reshape(extent)

def section_back(extended, grad_out, conv_taps, norm_gain, weight_in, bias_in, weight_out, layer_scale):
    radius = conv_taps.shape[1] // 2
    normed, pullback = jax.vjp(spread, extended, conv_taps, norm_gain)
    extent = normed.shape
    flattened = normed.reshape(extent[0], -1).astype(jnp.bfloat16)
    out_flat = grad_out.reshape(extent[0], -1)
    grad_normed, grads = lax.map(lambda pieces: pointwise_back(pieces[0], pieces[1], weight_in, bias_in, weight_out, layer_scale), (to_blocks(flattened, N_TRACK), to_blocks(out_flat, N_TRACK)))
    grad_normed = from_blocks(grad_normed).reshape(extent)
    grads = tuple((lax.optimization_barrier(jnp.sum(member, axis=0)) for member in grads))
    grad_ext, grad_taps, grad_gain = pullback(grad_normed)
    grad_ext = grad_ext.at[:, radius:radius + extent[1]].add(grad_out)
    return (grad_ext, (grad_taps, grad_gain) + grads)

def reference(volume, labels, conv_taps, norm_gain, weight_in, bias_in, weight_out, layer_scale, head_weight, head_bias):
    radius = TAPS // 2
    padding = ((0, 0), (radius, radius), (0, 0), (0, 0))
    first_ext = jnp.pad(volume.astype(jnp.float32), padding)
    middle = section_forward(first_ext, conv_taps[0], norm_gain[0], weight_in[0], bias_in[0], weight_out[0], layer_scale[0]).astype(jnp.bfloat16)
    second_ext = jnp.pad(middle.astype(jnp.float32), padding)
    final = section_forward(second_ext, conv_taps[1], norm_gain[1], weight_in[1], bias_in[1], weight_out[1], layer_scale[1]).astype(jnp.bfloat16)
    grad_final, grad_hw, grad_hb = head_back(final.reshape(final.shape[0], -1), labels.reshape(-1), head_weight, head_bias)
    grad_out = grad_final.reshape(final.shape)
    exts = (first_ext, second_ext)
    collected = [None, None]
    for section in (1, 0):
        grad_ext, grads = section_back(exts[section], grad_out, conv_taps[section], norm_gain[section], weight_in[section], bias_in[section], weight_out[section], layer_scale[section])
        collected[section] = grads
        grad_out = grad_ext[:, radius:radius + volume.shape[1]]
    stacked = tuple((jnp.stack([collected[0][index], collected[1][index]]) / VOXELS for index in range(6)))
    return (grad_out, stacked[0], stacked[1], stacked[2], stacked[3], stacked[4], stacked[5], grad_hw / VOXELS, grad_hb / VOXELS)
```

```python
import functools

import jax
import jax.numpy as jnp
from jax import lax
from jax.experimental import pallas as pl
from jax.experimental.pallas import tpu as pltpu
from jax.sharding import PartitionSpec as P

F32 = jnp.float32
BF16 = jnp.bfloat16
LANES = 128
ROWS = 8
RADIUS = 3
TAPS = 7
PLANES = 3
Y = 8
OWN = PLANES * Y
EXT = (PLANES + 2 * RADIUS) * Y
CHUNK = 4
GELU_A = 0.7978845608028654
GELU_B = 0.044715 * GELU_A
VMEM_LIMIT = 44 * 1024 * 1024


def group_rows(index):
    return pl.ds(pl.multiple_of(index * ROWS, ROWS), ROWS)


def tap_tables(taps):
    lane = jnp.arange(LANES)
    reach = jnp.arange(TAPS) - RADIUS
    inside = (lane[None] + reach[:, None] >= 0) & (lane[None] + reach[:, None] < LANES)
    inside = inside.astype(F32)[:, None, :]
    wide = jnp.broadcast_to(taps[:, :, :, None], taps.shape + (LANES,))
    return jnp.concatenate([wide[0], wide[1], wide[2] * inside, wide[2] * inside[::-1]], axis=0)


def unpack(source, wide, ext, first):
    wide[...] = source[...].astype(F32)
    channels = ext.shape[1]

    def one(group, carry):
        rows = group_rows(group)
        for tile in range(OWN):
            ext[first + tile, rows, :] = wide[pl.ds(group * ROWS * OWN + tile, ROWS, stride=OWN), :]
        return carry

    lax.fori_loop(0, channels // ROWS, one, 0)


def widen(source, ext, first, count):
    def one(tile, carry):
        ext[first + tile] = source[tile].astype(F32)
        return carry

    lax.fori_loop(0, count, one, 0, unroll=4)


def weighted(terms):
    total = None
    for coeff, value in terms:
        product = coeff * value
        total = product if total is None else total + product
    return total


def forward_x(ext, taps, rows):
    tx = [taps[k, rows, :] for k in range(TAPS)]
    out = [[None] * Y for _ in range(PLANES)]
    for y in range(Y):
        column = [ext[j * Y + y, rows, :] for j in range(PLANES + 2 * RADIUS)]
        for p in range(PLANES):
            out[p][y] = weighted([(tx[k], column[p + k]) for k in range(TAPS)])
    return out


def forward_y(field, taps, rows):
    ty = [taps[TAPS + k, rows, :] for k in range(TAPS)]
    out = [[None] * Y for _ in range(PLANES)]
    for p in range(PLANES):
        for y in range(Y):
            out[p][y] = weighted(
                [(ty[k], field[p][y + k - RADIUS]) for k in range(TAPS) if 0 <= y + k - RADIUS < Y]
            )
    return out


def turned(value, shift):
    return value if shift % LANES == 0 else pltpu.roll(value, shift % LANES, 1)


def convolve(ext, taps, mixed):
    def one(group, carry):
        rows = group_rows(group)
        field = forward_y(forward_x(ext, taps, rows), taps, rows)
        tz = [taps[2 * TAPS + k, rows, :] for k in range(TAPS)]
        for p in range(PLANES):
            for y in range(Y):
                mixed[p * Y + y, rows, :] = weighted(
                    [(tz[k], turned(field[p][y], RADIUS - k)) for k in range(TAPS)]
                )
        return carry

    lax.fori_loop(0, mixed.shape[1] // ROWS, one, 0)


def convolve_back(dmixed, taps, gext):
    def one(group, carry):
        rows = group_rows(group)
        tx = [taps[k, rows, :] for k in range(TAPS)]
        ty = [taps[TAPS + k, rows, :] for k in range(TAPS)]
        tz = [taps[3 * TAPS + k, rows, :] for k in range(TAPS)]
        along = [[None] * Y for _ in range(PLANES)]
        for p in range(PLANES):
            cross = []
            for y in range(Y):
                value = dmixed[p * Y + y, rows, :]
                cross.append(weighted([(tz[k], turned(value, k - RADIUS)) for k in range(TAPS)]))
            for y in range(Y):
                along[p][y] = weighted(
                    [(ty[k], cross[y - k + RADIUS]) for k in range(TAPS) if 0 <= y - k + RADIUS < Y]
                )
        for y in range(Y):
            for j in range(PLANES + 2 * RADIUS):
                gext[j * Y + y, rows, :] = weighted(
                    [(tx[k], along[j - k][y]) for k in range(TAPS) if 0 <= j - k < PLANES]
                )
        return carry

    lax.fori_loop(0, dmixed.shape[1] // ROWS, one, 0)


def tap_sums(ext, dmixed, taps, out):
    lane = lax.broadcasted_iota(jnp.int32, (ROWS, LANES), 1)

    def one(group, carry):
        rows = group_rows(group)
        mx = forward_x(ext, taps, rows)
        mxy = forward_y(mx, taps, rows)
        ty = [taps[TAPS + k, rows, :] for k in range(TAPS)]
        tz = [taps[3 * TAPS + k, rows, :] for k in range(TAPS)]
        sum_x, sum_y, sum_z = ([None] * TAPS for _ in range(3))

        def add(sums, k, value):
            sums[k] = value if sums[k] is None else sums[k] + value

        for p in range(PLANES):
            cross = []
            for y in range(Y):
                value = dmixed[p * Y + y, rows, :]
                spun = [turned(value, k - RADIUS) for k in range(TAPS)]
                for k in range(TAPS):
                    add(sum_z, k, spun[k] * mxy[p][y])
                cross.append(weighted([(tz[k], spun[k]) for k in range(TAPS)]))
            for y in range(Y):
                for k in range(TAPS):
                    if 0 <= y + k - RADIUS < Y:
                        add(sum_y, k, cross[y] * mx[p][y + k - RADIUS])
            for y in range(Y):
                along = weighted(
                    [(ty[k], cross[y - k + RADIUS]) for k in range(TAPS) if 0 <= y - k + RADIUS < Y]
                )
                for k in range(TAPS):
                    add(sum_x, k, along * ext[(p + k) * Y + y, rows, :])
        for k in range(TAPS):
            reach = k - RADIUS
            kept = (lane - reach >= 0) & (lane - reach < LANES)
            sum_z[k] = jnp.where(kept, sum_z[k], 0.0)
        total = jnp.zeros((ROWS, LANES), F32)
        for index, value in enumerate(sum_x + sum_y + sum_z):
            total = jnp.where(lane == index, jnp.sum(value, axis=1, keepdims=True), total)
        out[rows, :] = total
        return carry

    lax.fori_loop(0, dmixed.shape[1] // ROWS, one, 0)


def tiles(ref, first):
    return jnp.concatenate([ref[first + i] for i in range(CHUNK)], axis=1)


def put(ref, first, value):
    for i in range(CHUNK):
        ref[first + i] = value[:, i * LANES : (i + 1) * LANES].astype(ref.dtype)


def folded(value):
    total = value[:, :LANES]
    for i in range(1, CHUNK):
        total = total + value[:, i * LANES : (i + 1) * LANES]
    return total


def normalise(mixed):
    scale = 1.0 / mixed.shape[0]
    centred = mixed - jnp.sum(mixed, axis=0, keepdims=True) * scale
    variance = jnp.sum(centred * centred, axis=0, keepdims=True) * scale
    inverse = lax.rsqrt(variance + 1e-06)
    return centred * inverse, inverse


def dot(a, b):
    return jnp.dot(a, b, preferred_element_type=F32)


def dot_t(a, b):
    return lax.dot_general(a, b, (((1,), (1,)), ((), ())), preferred_element_type=F32)


def forward_kernel(
    par, vol, ha, hb, taps, gain, w_in, b_in, w_out, scale, out, wide, ext, mixed
):
    unpack(vol, wide, ext, RADIUS * Y)
    unpack(ha, wide, ext, (1 - par[0]) * 2 * RADIUS * Y)
    unpack(hb, wide, ext, par[0] * 2 * RADIUS * Y)
    convolve(ext, taps, mixed)

    def one(step, carry):
        first = step * CHUNK
        normal, inverse = normalise(tiles(mixed, first))
        normed = (normal * gain[...]).astype(BF16)
        hidden = dot(w_in[...], normed) + b_in[...]
        half = jnp.tanh(hidden * (GELU_A + GELU_B * (hidden * hidden)))
        act = (0.5 * hidden * (1.0 + half)).astype(BF16)
        put(out, first, tiles(ext, RADIUS * Y + first) + scale[...] * dot(w_out[...], act))
        return carry

    lax.fori_loop(0, OWN // CHUNK, one, 0)


def again_kernel(par, vol, ha, hb, taps, mixed, ext_low, wide, ext):
    unpack(vol, wide, ext, RADIUS * Y)
    unpack(ha, wide, ext, (1 - par[0]) * 2 * RADIUS * Y)
    unpack(hb, wide, ext, par[0] * 2 * RADIUS * Y)
    convolve(ext, taps, mixed)

    def one(tile, carry):
        ext_low[tile] = ext[tile].astype(BF16)
        return carry

    lax.fori_loop(0, EXT, one, 0, unroll=4)


def section_back(
    make_grad, par, mixed, taps, gain, w_in, w_in_t, b_in, w_out, w_out_t, scale,
    rim_a, rim_b, inner, dmixed, sums, small, gext, acc_bias, acc_gain, acc_scale,
):
    channels = gain.shape[0]
    acc_bias[...] = jnp.zeros_like(acc_bias)
    acc_gain[...] = jnp.zeros_like(acc_gain)
    acc_scale[...] = jnp.zeros_like(acc_scale)
    sums[...] = jnp.zeros_like(sums)

    def one(step, carry):
        first = step * CHUNK
        normal, inverse = normalise(tiles(mixed, first))
        normed = (normal * gain[...]).astype(BF16)
        hidden = dot(w_in[...], normed) + b_in[...]
        square = hidden * hidden
        half = jnp.tanh(hidden * (GELU_A + GELU_B * square))
        rise = 0.5 + 0.5 * half
        act = (hidden * rise).astype(BF16)
        slope = rise + (hidden * (0.5 - 0.5 * (half * half))) * (GELU_A + 3.0 * GELU_B * square)
        lifted = dot(w_out[...], act)
        grad = make_grad(step, first, lifted)
        acc_scale[...] += folded(grad * lifted)
        put(inner, first, grad)
        g_lift = (grad * scale[...]).astype(BF16)
        sums[:channels, :] += dot_t(g_lift, act)
        g_hidden = dot(w_out_t[...], g_lift) * slope
        acc_bias[...] += folded(g_hidden)
        g_hid = g_hidden.astype(BF16)
        sums[channels : 2 * channels, :] += dot_t(normed, g_hid)
        g_norm = dot(w_in_t[...], g_hid)
        acc_gain[...] += folded(g_norm * normal)
        g_normal = g_norm * gain[...]
        share = 1.0 / channels
        mean_a = jnp.sum(g_normal, axis=0, keepdims=True) * share
        mean_b = jnp.sum(g_normal * normal, axis=0, keepdims=True) * share
        put(dmixed, first, inverse * (g_normal - mean_a - normal * mean_b))
        return carry

    lax.fori_loop(0, OWN // CHUNK, one, 0)
    sums[2 * channels : 2 * channels + 1, :] = jnp.sum(acc_bias[...].T, axis=0, keepdims=True)
    lane = lax.broadcasted_iota(jnp.int32, (channels, LANES), 1)
    small[...] = jnp.where(
        lane == 3 * TAPS,
        jnp.sum(acc_gain[...], axis=1, keepdims=True),
        jnp.where(lane == 3 * TAPS + 1, jnp.sum(acc_scale[...], axis=1, keepdims=True), 0.0),
    )
    convolve_back(dmixed, taps, gext)
    first_a = (1 - par[0]) * 2 * RADIUS * Y
    first_b = par[0] * 2 * RADIUS * Y

    def finish(tile, carry):
        rim_a[tile] = gext[first_a + tile].astype(BF16)
        rim_b[tile] = gext[first_b + tile].astype(BF16)
        inner[tile] += gext[RADIUS * Y + tile]
        return carry

    lax.fori_loop(0, OWN, finish, 0, unroll=2)


def turn_kernel(
    par, mid, ma, mb, labels, taps, gain, w_in, w_in_t, b_in, w_out, w_out_t, scale,
    head, head_t, head_b,
    rim_a, rim_b, inner, dmixed, sums, small, head_sum, head_bias,
    ext, mixed, gext, acc_bias, acc_gain, acc_scale,
):
    widen(mid, ext, RADIUS * Y, OWN)
    widen(ma, ext, (1 - par[0]) * 2 * RADIUS * Y, OWN)
    widen(mb, ext, par[0] * 2 * RADIUS * Y, OWN)
    convolve(ext, taps, mixed)
    head_sum[...] = jnp.zeros_like(head_sum)
    head_bias[...] = jnp.zeros_like(head_bias)

    def make_grad(step, first, lifted):
        final = (tiles(ext, RADIUS * Y + first) + scale[...] * lifted).astype(BF16)
        logits = dot(head[...], final) + head_b[...]
        raised = jnp.exp(logits - jnp.max(logits, axis=0, keepdims=True))
        probability = raised / jnp.sum(raised, axis=0, keepdims=True)
        classes = lax.broadcasted_iota(jnp.int32, logits.shape, 0)
        g_logits = probability - (labels[step] == classes).astype(F32)
        head_bias[...] += folded(g_logits)
        g_low = g_logits.astype(BF16)
        head_sum[...] += dot_t(g_low, final)
        return dot(head_t[...], g_low)

    section_back(
        make_grad, par, mixed, taps, gain, w_in, w_in_t, b_in, w_out, w_out_t, scale,
        rim_a, rim_b, inner, dmixed, sums, small, gext, acc_bias, acc_gain, acc_scale,
    )


def back_kernel(
    par, before, ra, rb, mixed, taps, gain, w_in, w_in_t, b_in, w_out, w_out_t, scale,
    rim_a, rim_b, inner, dmixed, sums, small,
    gext, acc_bias, acc_gain, acc_scale,
):
    def make_grad(step, first, lifted):
        return tiles(before, first) + tiles(ra, first).astype(F32) + tiles(rb, first).astype(F32)

    section_back(
        make_grad, par, mixed, taps, gain, w_in, w_in_t, b_in, w_out, w_out_t, scale,
        rim_a, rim_b, inner, dmixed, sums, small, gext, acc_bias, acc_gain, acc_scale,
    )


def taps_two_kernel(par, mid, ma, mb, dmixed, taps, out, ext):
    widen(mid, ext, RADIUS * Y, OWN)
    widen(ma, ext, (1 - par[0]) * 2 * RADIUS * Y, OWN)
    widen(mb, ext, par[0] * 2 * RADIUS * Y, OWN)
    tap_sums(ext, dmixed, taps, out)


def taps_one_kernel(ext_low, dmixed, taps, out, ext):
    widen(ext_low, ext, 0, EXT)
    tap_sums(ext, dmixed, taps, out)


def last_kernel(before, ra, rb, out, total):
    def add(tile, carry):
        total[tile] = before[tile] + ra[tile].astype(F32) + rb[tile].astype(F32)
        return carry

    lax.fori_loop(0, OWN, add, 0, unroll=2)
    channels = before.shape[1]

    def one(group, carry):
        rows = group_rows(group)
        for tile in range(OWN):
            out[pl.ds(group * ROWS * OWN + tile, ROWS, stride=OWN), :] = total[tile, rows, :]
        return carry

    lax.fori_loop(0, channels // ROWS, one, 0)


def call(kernel, name, operands, outs, scratch, flops=0):
    smem = pl.BlockSpec(memory_space=pltpu.SMEM)
    vmem = pl.BlockSpec(memory_space=pltpu.VMEM)
    moved = sum(x.size * x.dtype.itemsize for x in operands) + sum(
        x.size * x.dtype.itemsize for x in outs
    )
    return pl.pallas_call(
        kernel,
        name=name,
        out_shape=tuple(outs),
        in_specs=[smem if x.dtype == jnp.int32 and x.shape == (1,) else vmem for x in operands],
        out_specs=tuple([vmem] * len(outs)),
        scratch_shapes=scratch,
        compiler_params=pltpu.CompilerParams(vmem_limit_bytes=VMEM_LIMIT),
        cost_estimate=pl.CostEstimate(flops=flops, bytes_accessed=moved, transcendentals=0),
    )(*operands)


def shape(dims, dtype):
    return jax.ShapeDtypeStruct(dims, dtype)


def swap(value_a, value_b):
    count = lax.axis_size("track")
    near = [(i, i ^ 1) for i in range(count)]
    far = []
    for i in range(1, count - 1, 2):
        far += [(i, i + 1), (i + 1, i)]
    return lax.ppermute(value_b, "track", far), lax.ppermute(value_a, "track", near)


def summed(value):
    count = lax.axis_size("track")
    if count & (count - 1):
        return lax.psum(value, "track")
    step = 1
    while step < count:
        value = value + lax.ppermute(value, "track", [(i, i ^ step) for i in range(count)])
        step *= 2
    return value


def on_device(
    volume, labels, conv_taps, norm_gain, weight_in, bias_in, weight_out, layer_scale, head_weight, head_bias
):
    channels, planes, rows, depth = volume.shape
    hidden = weight_in.shape[1]
    classes = head_weight.shape[0]
    devices = lax.axis_size("track")
    par = (lax.axis_index("track") % 2).astype(jnp.int32).reshape(1)

    flat = volume.reshape(channels * OWN, depth)
    hb, ha = swap(flat, flat)
    tables = [tap_tables(conv_taps[s]) for s in range(2)]
    params = []
    for s in range(2):
        params.append(
            dict(
                gain=norm_gain[s][:, None],
                w_in=weight_in[s],
                w_in_t=weight_in[s].T,
                b_in=bias_in[s][:, None],
                w_out=weight_out[s],
                w_out_t=weight_out[s].T,
                scale=layer_scale[s][:, None],
            )
        )
    padded = jnp.zeros((ROWS, channels), BF16).at[:classes].set(head_weight)
    padded_b = jnp.full((ROWS,), -1e30, F32).at[:classes].set(head_bias)[:, None]
    flat_labels = labels.reshape(OWN // CHUNK, 1, CHUNK * depth)

    own_low = shape((OWN, channels, depth), BF16)
    own_wide = shape((OWN, channels, depth), F32)
    s_ext = pltpu.VMEM((EXT, channels, depth), F32)
    s_own = pltpu.VMEM((OWN, channels, depth), F32)
    s_wide = pltpu.VMEM((channels * OWN, depth), F32)
    s_bias = pltpu.VMEM((hidden, LANES), F32)
    s_chan = pltpu.VMEM((channels, LANES), F32)
    voxels = OWN * depth
    point = 2 * channels * hidden * voxels

    p = params[0]
    (mid,) = call(
        forward_kernel, "forward_one",
        (par, flat, ha, hb, tables[0], p["gain"], p["w_in"], p["b_in"], p["w_out"], p["scale"]),
        [own_low], [s_wide, s_ext, s_own], 2 * point,
    )
    mb, ma = swap(mid, mid)
    mid_tied, flat_tied = lax.optimization_barrier((mid, flat))
    mixed_one, ext_one = call(
        again_kernel, "again_one", (par, flat_tied, ha, hb, tables[0]),
        [own_wide, shape((EXT, channels, depth), BF16)], [s_wide, s_ext], 2 * point,
    )
    back_outs = [
        own_low, own_low, own_wide, own_wide,
        shape((2 * channels + ROWS, hidden), F32), shape((channels, LANES), F32),
    ]
    p = params[1]
    rim_a, rim_b, inner, dmixed, sums_two, small_two, head_sum, head_lanes = call(
        turn_kernel, "turn_two",
        (par, mid, ma, mb, flat_labels, tables[1], p["gain"], p["w_in"], p["w_in_t"], p["b_in"],
         p["w_out"], p["w_out_t"], p["scale"], padded, padded.T, padded_b),
        back_outs + [shape((ROWS, channels), F32), shape((ROWS, LANES), F32)],
        [s_ext, s_own, s_ext, s_bias, s_chan, s_chan], 6 * point,
    )
    rb, ra = swap(rim_a, rim_b)
    (taps_two,) = call(
        taps_two_kernel, "taps_two", (par, mid, ma, mb, dmixed, tables[1]),
        [shape((channels, LANES), F32)], [s_ext], 2 * point,
    )
    p = params[0]
    rim_a, rim_b, inner, dmixed, sums_one, small_one = call(
        back_kernel, "back_one",
        (par, inner, ra, rb, mixed_one, tables[0], p["gain"], p["w_in"], p["w_in_t"], p["b_in"],
         p["w_out"], p["w_out_t"], p["scale"]),
        back_outs, [s_ext, s_bias, s_chan, s_chan], 6 * point,
    )
    rb, ra = swap(rim_a, rim_b)
    (taps_one,) = call(
        taps_one_kernel, "taps_one", (ext_one, dmixed, tables[0]),
        [shape((channels, LANES), F32)], [s_ext], 2 * point,
    )
    (grad,) = call(
        last_kernel, "last", (inner, ra, rb),
        [shape((channels * OWN, depth), F32)], [s_own],
    )

    total = 1.0 / float(devices * planes * rows * depth)
    sums_two = summed(sums_two) * total
    sums_one = summed(sums_one) * total
    tail = jnp.concatenate(
        [small_one + taps_one, small_two + taps_two,
         jnp.pad(head_sum, ((0, 0), (0, LANES - channels))), head_lanes], axis=0
    )
    tail = summed(tail) * total
    stats = tail[: 2 * channels].reshape(2, channels, LANES)
    grad_taps = jnp.moveaxis(stats[:, :, : 3 * TAPS], 1, 2).reshape(2, 3, TAPS, channels)
    head_rows = tail[2 * channels : 2 * channels + classes, :channels]
    head_cols = jnp.sum(tail[2 * channels + ROWS : 2 * channels + ROWS + classes], axis=1)
    both = jnp.stack([sums_one, sums_two])
    return (
        grad.reshape(volume.shape),
        grad_taps,
        stats[:, :, 3 * TAPS],
        jnp.swapaxes(both[:, channels : 2 * channels], 1, 2),
        both[:, 2 * channels],
        both[:, :channels],
        stats[:, :, 3 * TAPS + 1],
        head_rows,
        head_cols,
    )


def solution(mesh):
    placed = (
        P(None, ("groups", "track"), None, None),
        P(("groups", "track"), None, None),
        P(), P(), P(), P(), P(), P(), P(), P(),
    )
    return jax.shard_map(
        on_device,
        mesh=mesh,
        in_specs=placed,
        out_specs=(
            P(None, ("groups", "track"), None, None),
            P("groups", None, None, None),
            P("groups", None),
            P("groups", None, None),
            P("groups", None),
            P("groups", None, None),
            P("groups", None),
            P("groups", None),
            P("groups"),
        ),
        check_vma=False,
    )
```

```python
import functools

import jax
import jax.numpy as jnp
from jax import lax
from jax.experimental import pallas as pl
from jax.experimental.pallas import tpu as pltpu
from jax.sharding import PartitionSpec as P

F32 = jnp.float32
BF16 = jnp.bfloat16
LANES = 128
ROWS = 8
PAIR = 16
RADIUS = 3
TAPS = 7
PLANES = 3
Y = 8
OWN = PLANES * Y
EXT = (PLANES + 2 * RADIUS) * Y
CHUNK = 12
GELU_A = 0.7978845608028654
GELU_B = 0.044715 * GELU_A
MIB = 1024 * 1024


T_X, T_Y, T_Z, T_Z_BACK = 0, 7, 14, 21
GAIN, SCALE = 21, 22


def group_rows(index, size=ROWS):
    return pl.ds(pl.multiple_of(index * size, size), size)


def coeffs(source, rows, first, count=TAPS):
    if len(source.shape) == 3:
        return [source[k, rows, :] for k in range(first, first + count)]
    found = []
    for k in range(first, first + count):
        column = source[rows, k : k + 1]
        found.append(jnp.broadcast_to(column, (column.shape[0], LANES)))
    return found


def tables_kernel(
    cols, b_in, w_in, w_out, head, head_b, labels,
    tables, cols_out, b_out, w_in_out, w_in_t, w_out_out, w_out_t, head_out, head_t, head_b_out, labels_out,
):
    def one(group, carry):
        rows = group_rows(group)
        lane = lax.broadcasted_iota(jnp.int32, (ROWS, LANES), 1)
        for s in range(2):
            for k, value in enumerate(coeffs(cols.at[s], rows, T_X, 2 * TAPS)):
                tables[s, k, rows, :] = value
            for k, value in enumerate(coeffs(cols.at[s], rows, T_Z)):
                for first, reach in ((T_Z, k - RADIUS), (T_Z_BACK, RADIUS - k)):
                    kept = (lane + reach >= 0) & (lane + reach < LANES)
                    tables[s, first + k, rows, :] = jnp.where(kept, value, 0.0)
        return carry

    lax.fori_loop(0, tables.shape[2] // ROWS, one, 0)
    for s in range(2):
        w_in_t[s] = w_in[s].T
        w_out_t[s] = w_out[s].T
    head_t[...] = head[...].astype(F32).T.astype(BF16)
    for source, out in (
        (cols, cols_out), (b_in, b_out), (w_in, w_in_out), (w_out, w_out_out), (head, head_out),
        (head_b, head_b_out), (labels, labels_out),
    ):
        out[...] = source[...]


def rim_coeffs(par, cols, rows, low_if_even):
    tx = coeffs(cols, rows, T_X)
    zero = jnp.zeros_like(tx[0])
    low = (par[0] == 0) == low_if_even
    found = {}
    for d in range(1 - PLANES, PLANES):
        found[d] = jnp.where(low, tx[d] if d >= 0 else zero, tx[2 * RADIUS + d] if d <= 0 else zero)
    return found


def unpack(source, wide, out, first=0):
    wide[...] = source[...].astype(F32)

    def one(group, carry):
        rows = group_rows(group)
        for tile in range(OWN):
            out[first + tile, rows, :] = wide[pl.ds(group * ROWS * OWN + tile, ROWS, stride=OWN), :]
        return carry

    lax.fori_loop(0, out.shape[1] // ROWS, one, 0)


def widen(source, ext, first, count):
    def one(tile, carry):
        ext[first + tile] = source[tile].astype(F32)
        return carry

    lax.fori_loop(0, count, one, 0, unroll=4)


def weighted(terms, total=None):
    for coeff, value in terms:
        product = coeff * value
        total = product if total is None else total + product
    return total


def along_own(par, own, near, cols, out):
    def one(group, carry):
        rows = group_rows(group, PAIR)
        tx = coeffs(cols, rows, T_X)
        tn = rim_coeffs(par, cols, rows, False)
        for y in range(Y):
            mine = [own[r * Y + y, rows, :].astype(F32) for r in range(PLANES)]
            other = [near[r * Y + y, rows, :].astype(F32) for r in range(PLANES)]
            for p in range(PLANES):
                out[p * Y + y, rows, :] = weighted(
                    [(tx[RADIUS + r - p], mine[r]) for r in range(PLANES)]
                    + [(tn[q - p], other[q]) for q in range(PLANES)]
                )
        return carry

    lax.fori_loop(0, out.shape[1] // PAIR, one, 0)


def along_far(par, part, far, cols, out):
    def one(group, carry):
        rows = group_rows(group, PAIR)
        tf = rim_coeffs(par, cols, rows, True)
        for y in range(Y):
            other = [far[r * Y + y, rows, :].astype(F32) for r in range(PLANES)]
            for p in range(PLANES):
                out[p * Y + y, rows, :] = weighted(
                    [(tf[q - p], other[q]) for q in range(PLANES)], part[p * Y + y, rows, :]
                )
        return carry

    lax.fori_loop(0, out.shape[1] // PAIR, one, 0)


def across(field, ty, y):
    return weighted([(ty[k], field[y + k - RADIUS]) for k in range(TAPS) if 0 <= y + k - RADIUS < Y])


def across_back(field, ty, y):
    return weighted([(ty[k], field[y - k + RADIUS]) for k in range(TAPS) if 0 <= y - k + RADIUS < Y])


def turned(value, shift):
    return value if shift % LANES == 0 else pltpu.roll(value, shift % LANES, 1)


def rest_of_conv(field, cols, mixed):
    def one(group, carry):
        rows = group_rows(group)
        ty = coeffs(cols, rows, T_Y)
        tz = coeffs(cols, rows, T_Z)
        for p in range(PLANES):
            plane = [field[p * Y + y, rows, :] for y in range(Y)]
            for y in range(Y):
                value = across(plane, ty, y)
                mixed[p * Y + y, rows, :] = weighted(
                    [(tz[k], turned(value, RADIUS - k)) for k in range(TAPS)]
                )
        return carry

    lax.fori_loop(0, mixed.shape[1] // ROWS, one, 0)


def convolve_back(dmixed, cols, along):
    def one(group, carry):
        rows = group_rows(group)
        ty = coeffs(cols, rows, T_Y)
        tz = coeffs(cols, rows, T_Z_BACK)
        for p in range(PLANES):
            cross = []
            for y in range(Y):
                value = dmixed[p * Y + y, rows, :]
                cross.append(weighted([(tz[k], turned(value, k - RADIUS)) for k in range(TAPS)]))
            for y in range(Y):
                along[p * Y + y, rows, :] = across_back(cross, ty, y)
        return carry

    lax.fori_loop(0, dmixed.shape[1] // ROWS, one, 0)


def rim(par, along, cols, far, out):
    def one(group, carry):
        rows = group_rows(group, PAIR)
        tt = rim_coeffs(par, cols, rows, far)
        for y in range(Y):
            column = [along[p * Y + y, rows, :] for p in range(PLANES)]
            for q in range(PLANES):
                out[q * Y + y, rows, :] = weighted(
                    [(tt[q - p], column[p]) for p in range(PLANES)]
                ).astype(out.dtype)
        return carry

    lax.fori_loop(0, out.shape[1] // PAIR, one, 0)


def inside(along, cols, base, out):
    def one(group, carry):
        rows = group_rows(group)
        tx = coeffs(cols, rows, T_X)
        for y in range(Y):
            column = [along[p * Y + y, rows, :] for p in range(PLANES)]
            for r in range(PLANES):
                out[r * Y + y, rows, :] = weighted(
                    [(tx[RADIUS + r - p], column[p]) for p in range(PLANES)], base[r * Y + y, rows, :]
                )
        return carry

    lax.fori_loop(0, out.shape[1] // ROWS, one, 0)


def tap_sums(ext, dmixed, along, cols, out):
    lane = lax.broadcasted_iota(jnp.int32, (ROWS, LANES), 1)

    def one(group, carry):
        rows = group_rows(group)
        tx = coeffs(cols, rows, T_X)
        ty = coeffs(cols, rows, T_Y)
        tz = coeffs(cols, rows, T_Z_BACK)
        sum_x, sum_y, sum_z = ([None] * TAPS for _ in range(3))

        def add(sums, k, value):
            sums[k] = value if sums[k] is None else sums[k] + value

        for p in range(PLANES):
            plane = []
            for y in range(Y):
                column = [ext[(p + k) * Y + y, rows, :] for k in range(TAPS)]
                plane.append(weighted([(tx[k], column[k]) for k in range(TAPS)]))
                back = along[p * Y + y, rows, :]
                for k in range(TAPS):
                    add(sum_x, k, back * column[k])
            for y in range(Y):
                value = dmixed[p * Y + y, rows, :]
                spun = [turned(value, k - RADIUS) for k in range(TAPS)]
                field = across(plane, ty, y)
                for k in range(TAPS):
                    add(sum_z, k, spun[k] * field)
                cross = weighted([(tz[k], spun[k]) for k in range(TAPS)])
                for k in range(TAPS):
                    if 0 <= y + k - RADIUS < Y:
                        add(sum_y, k, cross * plane[y + k - RADIUS])
        for k in range(TAPS):
            reach = k - RADIUS
            kept = (lane - reach >= 0) & (lane - reach < LANES)
            sum_z[k] = jnp.where(kept, sum_z[k], 0.0)
        total = jnp.zeros((ROWS, LANES), F32)
        for index, value in enumerate(sum_x + sum_y + sum_z):
            total = jnp.where(lane == index, jnp.sum(value, axis=1, keepdims=True), total)
        out[rows, :] = total
        return carry

    lax.fori_loop(0, dmixed.shape[1] // ROWS, one, 0)


def tiles(ref, first):
    return jnp.concatenate([ref[first + i] for i in range(CHUNK)], axis=1)


def put(ref, first, value):
    for i in range(CHUNK):
        ref[first + i] = value[:, i * LANES : (i + 1) * LANES].astype(ref.dtype)


def folded(value):
    total = value[:, :LANES]
    for i in range(1, CHUNK):
        total = total + value[:, i * LANES : (i + 1) * LANES]
    return total


def normalise(mixed):
    scale = 1.0 / mixed.shape[0]
    centred = mixed - jnp.sum(mixed, axis=0, keepdims=True) * scale
    variance = jnp.sum(centred * centred, axis=0, keepdims=True) * scale
    inverse = lax.rsqrt(variance + 1e-06)
    return centred * inverse, inverse


def normalise_back(g_norm, normal, inverse, gain):
    share = 1.0 / g_norm.shape[0]
    g_normal = g_norm * gain
    mean_a = jnp.sum(g_normal, axis=0, keepdims=True) * share
    mean_b = jnp.sum(g_normal * normal, axis=0, keepdims=True) * share
    return inverse * (g_normal - mean_a - normal * mean_b)


def dot(a, b):
    return jnp.dot(a, b, preferred_element_type=F32)


def dot_t(a, b):
    return lax.dot_general(a, b, (((1,), (1,)), ((), ())), preferred_element_type=F32)


def gelu_parts(hidden):
    square = hidden * hidden
    half = jnp.tanh(hidden * (GELU_A + GELU_B * square))
    rise = 0.5 + 0.5 * half
    act = (hidden * rise).astype(BF16)
    slope = rise + (hidden * (0.5 - 0.5 * (half * half))) * (GELU_A + 3.0 * GELU_B * square)
    return act, slope


def steps():
    return [(step, step * CHUNK) for step in range(OWN // CHUNK)]


def mixed_sums(pairs):
    for have, got, out, low in pairs:
        total = have[...] + got[...].astype(F32)
        out[...] = total
        if low is not None:
            low[...] = total.astype(BF16)


def start_kernel(par, vol, near, tables, part, own, other, wide):
    unpack(vol, wide, own)
    unpack(near, wide, other)
    along_own(par, own, other, tables.at[0], part)


def forward_kernel(
    par, far, part, own_tiles, cols, tables, w_in, b_in, w_out, out, mixed, other, wide, field
):
    unpack(far, wide, other)
    along_far(par, part, other, tables.at[0], field)
    rest_of_conv(field, tables.at[0], mixed)
    gain, scale = cols[0, :, GAIN : GAIN + 1], cols[0, :, SCALE : SCALE + 1]
    for step, first in steps():
        normal, inverse = normalise(tiles(mixed, first))
        normed = (normal * gain).astype(BF16)
        hidden = dot(w_in[0], normed) + b_in[:, 0:1]
        half = jnp.tanh(hidden * (GELU_A + GELU_B * (hidden * hidden)))
        act = (hidden * (0.5 + 0.5 * half)).astype(BF16)
        put(out, first, tiles(own_tiles, first) + scale * dot(w_out[0], act))


def save_kernel(mixed, cols, w_in, b_in, normed, normal, inverse, act, slope):
    for step, first in steps():
        value, inverse[step] = normalise(tiles(mixed, first))
        put(normal, first, value)
        low = (value * cols[0, :, GAIN : GAIN + 1]).astype(BF16)
        put(normed, first, low)
        act[step], slope[step] = gelu_parts(dot(w_in[0], low) + b_in[:, 0:1])


def middle_kernel(par, mid, near, tables, part):
    along_own(par, mid, near, tables.at[1], part)


def turn_kernel(
    par, far, part, mid, labels, cols, tables, w_in, w_in_t, b_in, w_out, w_out_t, head, head_t,
    head_b, rim_far, rim_near, along, dmixed, base, keep, send, acc_gain, acc_scale, head_cols, head_bias,
    field, mixed, sums, acc_bias,
):
    channels = mid.shape[1]
    taps = tables.at[1]
    along_far(par, part, far, taps, field)
    rest_of_conv(field, taps, mixed)
    sums[...] = jnp.zeros_like(sums)
    acc_bias[...] = jnp.zeros_like(acc_bias)
    acc_gain[...] = jnp.zeros_like(acc_gain)
    acc_scale[...] = jnp.zeros_like(acc_scale)
    head_cols[...] = jnp.zeros_like(head_cols)
    head_bias[...] = jnp.zeros_like(head_bias)
    gain, scale = cols[1, :, GAIN : GAIN + 1], cols[1, :, SCALE : SCALE + 1]
    for step, first in steps():
        normal, inverse = normalise(tiles(mixed, first))
        normed = (normal * gain).astype(BF16)
        act, slope = gelu_parts(dot(w_in[1], normed) + b_in[:, 1:2])
        lifted = dot(w_out[1], act)
        final = (tiles(mid, first).astype(F32) + scale * lifted).astype(BF16)
        logits = dot(head[...], final) + head_b[...]
        raised = jnp.exp(logits - jnp.max(logits, axis=0, keepdims=True))
        probability = raised / jnp.sum(raised, axis=0, keepdims=True)
        classes = lax.broadcasted_iota(jnp.int32, logits.shape, 0)
        g_logits = probability - (labels[step] == classes).astype(F32)
        head_bias[...] += folded(g_logits)
        g_low = g_logits.astype(BF16)
        head_cols[...] += dot_t(final, g_low)
        grad = dot(head_t[...], g_low)
        acc_scale[...] += folded(grad * lifted)
        put(base, first, grad)
        g_lift = (grad * scale).astype(BF16)
        sums[0, :channels] += dot_t(g_lift, act)
        g_hidden = dot(w_out_t[1], g_lift) * slope
        acc_bias[...] += folded(g_hidden)
        g_hid = g_hidden.astype(BF16)
        sums[1, :channels] += dot_t(normed, g_hid)
        g_norm = dot(w_in_t[1], g_hid)
        acc_gain[...] += folded(g_norm * normal)
        put(dmixed, first, normalise_back(g_norm, normal, inverse, gain))
    convolve_back(dmixed, taps, along)
    rim(par, along, taps, True, rim_far)
    rim(par, along, taps, False, rim_near)
    sums[1, channels : channels + 1] = jnp.sum(acc_bias[...].T, axis=0, keepdims=True)
    keep[...] = sums[par[0]]
    send[...] = sums[1 - par[0]]


def fill(par, own, near, far, ext):
    widen(own, ext, RADIUS * Y, OWN)
    widen(near, ext, (1 - par[0]) * 2 * RADIUS * Y, OWN)
    widen(far, ext, par[0] * 2 * RADIUS * Y, OWN)


def total_of(ref):
    return jnp.sum(ref[...], axis=1, keepdims=True)


def taps_two_kernel(
    par, own, near, far, dmixed, along, base, tables, acc_gain, acc_scale, head_cols, head_bias,
    have, got, out, inner, new, new_low, ext,
):
    taps = tables.at[1]
    mixed_sums([(have, got, new, new_low)])
    fill(par, own, near, far, ext)
    inside(along, taps, base, inner)
    tap_sums(ext, dmixed, along, taps, out)
    lane = lax.broadcasted_iota(jnp.int32, out.shape, 1)
    value = jnp.where(lane == 3 * TAPS, total_of(acc_gain), out[...])
    value = jnp.where(lane == 3 * TAPS + 1, total_of(acc_scale), value)
    value = pltpu.roll(value, 32, 1)
    for k in range(ROWS):
        value = jnp.where(lane == 64 + k, head_cols[:, k : k + 1], value)
    out[...] = value
    out[:ROWS] = jnp.where(lane[:ROWS] == 72, total_of(head_bias), out[:ROWS])


def taps_one_kernel(
    par, own, near, far, dmixed, along, tables, acc_gain, gs_scale, stats_two, out, ext
):
    fill(par, own, near, far, ext)
    tap_sums(ext, dmixed, along, tables.at[0], out)
    lane = lax.broadcasted_iota(jnp.int32, out.shape, 1)
    value = jnp.where(lane == 3 * TAPS, total_of(acc_gain), out[...])
    value = jnp.where(lane == 3 * TAPS + 1, gs_scale[...], value)
    out[...] = jnp.where(lane < 32, value, stats_two[...])


def inside_kernel(along, base, tables, inner):
    inside(along, tables.at[0], base, inner)


def point_back_kernel(
    par, inner, near, far, act, slope, normed, cols, w_in_t, w_out, w_out_t, have, got,
    base, g_norm, keep, send, gs_scale, new, new_low, sums, acc_bias,
):
    channels = inner.shape[1]
    mixed_sums([(have, got, new, new_low)])
    sums[...] = jnp.zeros_like(sums)
    acc_bias[...] = jnp.zeros_like(acc_bias)
    scale = cols[0, :, SCALE : SCALE + 1]
    for step, first in steps():
        grad = tiles(inner, first) + (tiles(near, first).astype(F32) + tiles(far, first).astype(F32))
        put(base, first, grad)
        g_lift = (grad * scale).astype(BF16)
        sums[0, :channels] += dot_t(g_lift, act[step])
        g_hidden = dot(w_out_t[0], g_lift) * slope[step]
        acc_bias[...] += folded(g_hidden)
        g_hid = g_hidden.astype(BF16)
        sums[1, :channels] += dot_t(tiles(normed, first), g_hid)
        put(g_norm, first, dot(w_in_t[0], g_hid))
    sums[1, channels : channels + 1] = jnp.sum(acc_bias[...].T, axis=0, keepdims=True)
    spread = jnp.sum(sums[0, :channels] * w_out[0].astype(F32), axis=1, keepdims=True)
    gs_scale[...] = spread / scale
    keep[...] = sums[par[0]]
    send[...] = sums[1 - par[0]]


def conv_back_kernel(
    par, g_norm, normal, inverse, cols, tables, rim_far, rim_near, along, dmixed, acc_gain
):
    taps = tables.at[0]
    acc_gain[...] = jnp.zeros_like(acc_gain)
    for step, first in steps():
        value, unit = tiles(g_norm, first), tiles(normal, first)
        acc_gain[...] += folded(value * unit)
        put(dmixed, first, normalise_back(value, unit, inverse[step], cols[0, :, GAIN : GAIN + 1]))
    convolve_back(dmixed, taps, along)
    rim(par, along, taps, True, rim_far)
    rim(par, along, taps, False, rim_near)


def sums_kernel(count, *refs):
    have, got, out, low = (refs[i * count : (i + 1) * count] for i in range(4))
    mixed_sums(zip(have, got, out, low))


def gather_kernel(have, got, value, first, second, third, out, low, total):
    mixed_sums([(have, got, out, low)])
    total[...] = (value[...] + first[...]) + (second[...] + third[...])


def last_kernel(inner, near, far, out, total):
    def add(tile, carry):
        total[tile] = inner[tile] + (near[tile].astype(F32) + far[tile].astype(F32))
        return carry

    lax.fori_loop(0, OWN, add, 0, unroll=2)

    def one(group, carry):
        rows = group_rows(group)
        for tile in range(OWN):
            out[pl.ds(group * ROWS * OWN + tile, ROWS, stride=OWN), :] = total[tile, rows, :]
        return carry

    lax.fori_loop(0, inner.shape[1] // ROWS, one, 0)


def weights_kernel(share, par, one_a, one_b, two_a, two_b, g_in_t, g_bias, g_out):
    channels = g_out.shape[1]
    for s, (mine, other) in enumerate(((one_a, one_b), (two_a, two_b))):
        even = par[0] == 0
        first = jnp.where(even, mine[...], other[...]) * share
        second = jnp.where(even, other[...], mine[...]) * share
        g_out[s] = first[:channels]
        g_in_t[s] = second[:channels]
        g_bias[s : s + 1] = second[channels : channels + 1]


def stats_kernel(share, stats, g_taps, g_gain, g_scale, g_head, g_head_b):
    rows = stats[...].T * share
    for s in range(2):
        for axis in range(3):
            first = 32 * s + axis * TAPS
            g_taps[s, axis] = rows[first : first + TAPS]
        g_gain[s : s + 1] = rows[32 * s + 21 : 32 * s + 22]
        g_scale[s : s + 1] = rows[32 * s + 22 : 32 * s + 23]
    g_head[...] = rows[64 : 64 + g_head.shape[0]]
    g_head_b[...] = rows[72:73]


def call(kernel, name, operands, outs, scratch=(), room=8, after=()):
    smem = pl.BlockSpec(memory_space=pltpu.SMEM)
    vmem = pl.BlockSpec(memory_space=pltpu.VMEM)
    anywhere = pl.BlockSpec(memory_space=pl.ANY)
    count = len(operands)

    def run(*refs):
        kernel(*refs[:count], *refs[count + len(after) :])

    in_specs = [smem if x.dtype == jnp.int32 and x.shape == (1,) else vmem for x in operands]
    return pl.pallas_call(
        run,
        name=name,
        out_shape=tuple(outs),
        in_specs=in_specs + [anywhere] * len(after),
        out_specs=tuple([vmem] * len(outs)),
        scratch_shapes=list(scratch),
        compiler_params=pltpu.CompilerParams(vmem_limit_bytes=room * MIB),
        cost_estimate=pl.CostEstimate(flops=0, bytes_accessed=0, transcendentals=0),
    )(*operands, *after)


def pinned(dims, dtype=F32):
    return pltpu.VMEM(dims, dtype)


def shape(dims, dtype=F32):
    return jax.ShapeDtypeStruct(dims, dtype)


def near_swap(value):
    count = lax.axis_size("track")
    return lax.ppermute(value, "track", [(i, i ^ 1) for i in range(count)])


def far_swap(value):
    count = lax.axis_size("track")
    pairs = []
    for i in range(1, count - 1, 2):
        pairs += [(i, i + 1), (i + 1, i)]
    return lax.ppermute(value, "track", pairs)


def bit_swap(value, step):
    count = lax.axis_size("track")
    return lax.ppermute(value, "track", [(i, i ^ step) for i in range(count)])


def exchanged(value, step):
    return value + bit_swap(value.astype(BF16), step).astype(F32)


def on_device(
    volume, labels, conv_taps, norm_gain, weight_in, bias_in, weight_out, layer_scale, head_weight, head_bias
):
    channels, planes, rows, depth = volume.shape
    hidden = weight_in.shape[1]
    classes = head_weight.shape[0]
    devices = lax.axis_size("track")
    share = 1.0 / float(devices * planes * rows * depth)
    par = (lax.axis_index("track") % 2).astype(jnp.int32).reshape(1)
    parts = OWN // CHUNK

    flat = volume.reshape(channels * OWN, depth)
    near = near_swap(flat)
    far = far_swap(flat)
    cols = jnp.swapaxes(
        jnp.concatenate(
            [conv_taps.reshape(2, 3 * TAPS, channels), norm_gain[:, None], layer_scale[:, None]], axis=1
        ), 1, 2,
    )
    b_in = bias_in.T
    head = jnp.zeros((ROWS, channels), BF16).at[:classes].set(head_weight)
    head_b = jnp.full((ROWS,), -1e30, F32).at[:classes].set(head_bias)[:, None]
    flat_labels = labels.reshape(parts, 1, CHUNK * depth)

    low = shape((OWN, channels, depth), BF16)
    full = shape((OWN, channels, depth))
    half = shape((channels + ROWS, hidden))
    half_low = shape((channels + ROWS, hidden), BF16)
    stat = shape((channels, LANES))
    s_full = pltpu.VMEM((OWN, channels, depth), F32)
    s_wide = pltpu.VMEM((channels * OWN, depth), F32)
    s_ext = pltpu.VMEM((EXT, channels, depth), F32)
    s_sums = pltpu.VMEM((2, channels + ROWS, hidden), F32)
    s_bias = pltpu.VMEM((hidden, LANES), F32)
    k_full = pinned((OWN, channels, depth))
    k_half = pinned((channels + ROWS, hidden))
    k_stat = pinned((channels, LANES))

    small = (cols, b_in, weight_in, weight_out, head, head_b, flat_labels)
    (tables, cols, b_in, w_in, w_in_t, w_out, w_out_t, head, head_t, head_b, flat_labels) = call(
        tables_kernel, "tables", small,
        [pinned((2, 4 * TAPS, channels, LANES)), pinned(cols.shape), pinned(b_in.shape),
         pinned(weight_in.shape, BF16), pinned(weight_out.shape, BF16), pinned(weight_out.shape, BF16),
         pinned(weight_in.shape, BF16), pinned(head.shape, BF16), pinned((channels, ROWS), BF16),
         pinned(head_b.shape), pinned(flat_labels.shape, jnp.int32)],
    )
    part, own_kept, near_kept = call(
        start_kernel, "start_one", (par, flat, near, tables), [k_full, k_full, k_full], [s_wide],
    )
    mid, mixed_one, far_kept = call(
        forward_kernel, "forward_one", (par, far, part, own_kept, cols, tables, w_in, b_in, w_out),
        [low, k_full, k_full], [s_wide, s_full], 16,
    )
    near = near_swap(mid)
    far = far_swap(mid)
    normed, normal, inverse, act, slope = call(
        save_kernel, "save_one", (mixed_one, cols, w_in, b_in),
        [pinned((OWN, channels, depth), BF16), k_full, pinned((parts, 1, CHUNK * depth)),
         pinned((parts, hidden, CHUNK * depth), BF16), pinned((parts, hidden, CHUNK * depth))],
        (), 16,
    )
    (part,) = call(
        middle_kernel, "start_two", (par, mid, near, tables), [k_full], (), 4, after=(inverse,)
    )
    (rim_far, rim_near, along, dmixed, base, keep, send,
     acc_gain, acc_scale, head_cols, head_lanes) = call(
        turn_kernel, "turn_two",
        (par, far, part, mid, flat_labels, cols, tables, w_in, w_in_t, b_in, w_out, w_out_t,
         head, head_t, head_b),
        [low, low, k_full, k_full, k_full, k_half, half, k_stat, k_stat, pinned((channels, ROWS)),
         pinned((ROWS, LANES))],
        [s_full, s_full, s_sums, s_bias], 24,
    )
    rim_near = near_swap(rim_near)
    rim_far = far_swap(rim_far)
    got = near_swap(send)
    stats, inner, two, two_low = call(
        taps_two_kernel, "taps_two",
        (par, mid, near, far, dmixed, along, base, tables, acc_gain, acc_scale, head_cols, head_lanes,
         keep, got),
        [k_stat, k_full, k_half, half_low], [s_ext], 8, after=(rim_near,),
    )
    got = bit_swap(two_low, 2)
    base, g_norm, keep, send, gs_scale, two, two_low = call(
        point_back_kernel, "point_back_one",
        (par, inner, rim_near, rim_far, act, slope, normed, cols, w_in_t, w_out, w_out_t, two, got),
        [k_full, k_full, k_half, half, pinned((channels, 1)), k_half, half_low], [s_sums, s_bias], 16,
    )
    got_two = bit_swap(two_low, 4)
    got_one = near_swap(send)
    rim_far, rim_near, along, dmixed, acc_gain = call(
        conv_back_kernel, "conv_back_one", (par, g_norm, normal, inverse, cols, tables),
        [low, low, k_full, k_full, k_stat], (), 12,
    )
    rim_near = near_swap(rim_near)
    rim_far = far_swap(rim_far)
    one, two, one_low, two_low = call(
        functools.partial(sums_kernel, 2), "sums_a", (keep, two, got_one, got_two),
        [k_half, k_half, half_low, half_low], (), 4, after=(rim_near,),
    )
    got_one = bit_swap(one_low, 2)
    got_two = bit_swap(two_low, 8)
    (stats,) = call(
        taps_one_kernel, "taps_one",
        (par, own_kept, near_kept, far_kept, dmixed, along, tables, acc_gain, gs_scale, stats),
        [stat], [s_ext], 8, after=(one,),
    )
    one, two, one_low, two_low = call(
        functools.partial(sums_kernel, 2), "sums_b", (one, two, got_one, got_two),
        [k_half, half, half_low, half_low], (), 4, after=(stats,),
    )
    got_one = bit_swap(one_low, 4)
    got_stats = [bit_swap(stats, step) for step in (1, 2, 3)]
    (inner,) = call(inside_kernel, "inside_one", (along, base, tables), [k_full], (), 4, after=(one,))
    one, one_low, stats = call(
        gather_kernel, "sums_c", (one, got_one, stats, *got_stats), [k_half, half_low, stat], (), 4,
        after=(inner,),
    )
    got_one = bit_swap(one_low, 8)
    got_stats = [bit_swap(stats, step) for step in (4, 8, 12)]
    (grad,) = call(
        last_kernel, "last", (inner, rim_near, rim_far), [shape((channels * OWN, depth))], [s_full], 4,
        after=(one,),
    )
    one, one_low, stats = call(
        gather_kernel, "sums_d", (one, got_one, stats, *got_stats), [half, half_low, stat], (), 4,
        after=(grad,),
    )
    step = 16
    while step < devices:
        one, two, stats = exchanged(one, step), exchanged(two, step), stats + bit_swap(stats, step)
        step *= 2
    g_taps, g_gain, g_scale, g_head, g_head_b = call(
        functools.partial(stats_kernel, share), "stats", (stats,),
        [shape((2, 3, TAPS, channels)), shape((2, channels)), shape((2, channels)),
         shape((classes, channels)), shape((1, channels))],
    )
    g_in_t, g_bias, g_out = call(
        functools.partial(weights_kernel, share), "weights",
        (par, one, near_swap(one), two, near_swap(two)),
        [shape((2, channels, hidden)), shape((2, hidden)), shape((2, channels, hidden))],
    )
    return (
        grad.reshape(volume.shape), g_taps, g_gain, jnp.swapaxes(g_in_t, 1, 2), g_bias, g_out, g_scale,
        g_head, g_head_b[0, :classes],
    )


def solution(mesh):
    placed = (
        P(None, ("groups", "track"), None, None),
        P(("groups", "track"), None, None),
        P(), P(), P(), P(), P(), P(), P(), P(),
    )
    return jax.shard_map(
        on_device,
        mesh=mesh,
        in_specs=placed,
        out_specs=(
            P(None, ("groups", "track"), None, None),
            P("groups", None, None, None),
            P("groups", None),
            P("groups", None, None),
            P("groups", None),
            P("groups", None, None),
            P("groups", None),
            P("groups", None),
            P("groups"),
        ),
        check_vma=False,
    )
```

```python
import functools

import jax
import jax.numpy as jnp
from jax import lax
from jax.experimental import pallas as pl
from jax.experimental.pallas import tpu as pltpu
from jax.sharding import PartitionSpec as P

F32 = jnp.float32
BF16 = jnp.bfloat16
LANES = 128
ROWS = 8
PAIR = 16
RADIUS = 3
TAPS = 7
PLANES = 3
Y = 8
OWN = PLANES * Y
EXT = (PLANES + 2 * RADIUS) * Y
CHUNK = 12
GELU_A = 0.7978845608028654
GELU_B = 0.044715 * GELU_A
STAT = 32
MIB = 1024 * 1024


T_X, T_Y, T_Z, T_Z_BACK = 0, 7, 14, 21
GAIN, SCALE, HEAD_BIAS, HEAD = 21, 22, 23, 24


def group_rows(index, size=ROWS):
    return pl.ds(pl.multiple_of(index * size, size), size)


def coeffs(source, rows, first, count=TAPS):
    if len(source.shape) == 3:
        return [source[k, rows, :] for k in range(first, first + count)]
    found = []
    for k in range(first, first + count):
        column = source[rows, k : k + 1]
        found.append(jnp.broadcast_to(column, (column.shape[0], LANES)))
    return found


def tables_kernel(
    cols, b_in, w_in, w_out, head, head_b, labels,
    tables, cols_out, b_out, w_in_out, w_in_t, w_out_out, w_out_t, head_out, head_t, head_b_out, labels_out,
    select,
):
    def one(group, carry):
        rows = group_rows(group)
        lane = lax.broadcasted_iota(jnp.int32, (ROWS, LANES), 1)
        for s in range(2):
            for k, value in enumerate(coeffs(cols.at[s], rows, T_X, 2 * TAPS)):
                tables[s, k, rows, :] = value
            for k, value in enumerate(coeffs(cols.at[s], rows, T_Z)):
                for first, reach in ((T_Z, k - RADIUS), (T_Z_BACK, RADIUS - k)):
                    kept = (lane + reach >= 0) & (lane + reach < LANES)
                    tables[s, first + k, rows, :] = jnp.where(kept, value, 0.0)
        return carry

    lax.fori_loop(0, tables.shape[2] // ROWS, one, 0)
    lane = lax.broadcasted_iota(jnp.int32, (LANES, LANES), 1)
    for k in range(3 * TAPS):
        select[k * LANES : (k + 1) * LANES] = jnp.where(lane == k, 1.0, 0.0).astype(BF16)
    for s in range(2):
        w_in_t[s] = w_in[s].T
        w_out_t[s] = w_out[s].T
    head_t[...] = head[...].astype(F32).T.astype(BF16)
    for source, out in (
        (cols, cols_out), (b_in, b_out), (w_in, w_in_out), (w_out, w_out_out), (head, head_out),
        (head_b, head_b_out), (labels, labels_out),
    ):
        out[...] = source[...]


def rim_coeffs(par, cols, rows, low_if_even):
    tx = coeffs(cols, rows, T_X)
    zero = jnp.zeros_like(tx[0])
    low = (par[0] == 0) == low_if_even
    found = {}
    for d in range(1 - PLANES, PLANES):
        found[d] = jnp.where(low, tx[d] if d >= 0 else zero, tx[2 * RADIUS + d] if d <= 0 else zero)
    return found


def unpack(source, wide, out, first=0):
    wide[...] = source[...].astype(F32)

    def one(group, carry):
        rows = group_rows(group)
        for tile in range(OWN):
            out[first + tile, rows, :] = wide[pl.ds(group * ROWS * OWN + tile, ROWS, stride=OWN), :]
        return carry

    lax.fori_loop(0, out.shape[1] // ROWS, one, 0)


def widen(source, ext, first, count):
    def one(tile, carry):
        ext[first + tile] = source[tile].astype(F32)
        return carry

    lax.fori_loop(0, count, one, 0, unroll=4)


def weighted(terms, total=None):
    for coeff, value in terms:
        product = coeff * value
        total = product if total is None else total + product
    return total


def along_own(par, own, near, cols, out):
    def one(group, carry):
        rows = group_rows(group, PAIR)
        tx = coeffs(cols, rows, T_X)
        tn = rim_coeffs(par, cols, rows, False)
        for y in range(Y):
            mine = [own[r * Y + y, rows, :].astype(F32) for r in range(PLANES)]
            other = [near[r * Y + y, rows, :].astype(F32) for r in range(PLANES)]
            for p in range(PLANES):
                out[p * Y + y, rows, :] = weighted(
                    [(tx[RADIUS + r - p], mine[r]) for r in range(PLANES)]
                    + [(tn[q - p], other[q]) for q in range(PLANES)]
                )
        return carry

    lax.fori_loop(0, out.shape[1] // PAIR, one, 0)


def along_far(par, part, far, cols, out):
    def one(group, carry):
        rows = group_rows(group, PAIR)
        tf = rim_coeffs(par, cols, rows, True)
        for y in range(Y):
            other = [far[r * Y + y, rows, :].astype(F32) for r in range(PLANES)]
            for p in range(PLANES):
                out[p * Y + y, rows, :] = weighted(
                    [(tf[q - p], other[q]) for q in range(PLANES)], part[p * Y + y, rows, :]
                )
        return carry

    lax.fori_loop(0, out.shape[1] // PAIR, one, 0)


def across(field, ty, y):
    return weighted([(ty[k], field[y + k - RADIUS]) for k in range(TAPS) if 0 <= y + k - RADIUS < Y])


def across_back(field, ty, y):
    return weighted([(ty[k], field[y - k + RADIUS]) for k in range(TAPS) if 0 <= y - k + RADIUS < Y])


def turned(value, shift):
    return value if shift % LANES == 0 else pltpu.roll(value, shift % LANES, 1)


def rest_of_conv(field, cols, crossed, mixed):
    def one(group, carry):
        rows = group_rows(group)
        ty = coeffs(cols, rows, T_Y)
        tz = coeffs(cols, rows, T_Z)
        for p in range(PLANES):
            plane = [field[p * Y + y, rows, :] for y in range(Y)]
            for y in range(Y):
                value = across(plane, ty, y)
                crossed[p * Y + y, rows, :] = value
                mixed[p * Y + y, rows, :] = weighted(
                    [(tz[k], turned(value, RADIUS - k)) for k in range(TAPS)]
                )
        return carry

    lax.fori_loop(0, mixed.shape[1] // ROWS, one, 0)


def convolve_back(dmixed, mxy, cols, cross_out, along, sums):
    lane = lax.broadcasted_iota(jnp.int32, (ROWS, LANES), 1)

    def one(group, carry):
        rows = group_rows(group)
        ty = coeffs(cols, rows, T_Y)
        tz = coeffs(cols, rows, T_Z_BACK)
        found = [None] * TAPS
        for p in range(PLANES):
            cross = []
            for y in range(Y):
                value = dmixed[p * Y + y, rows, :]
                spun = [turned(value, k - RADIUS) for k in range(TAPS)]
                field = mxy[p * Y + y, rows, :]
                for k in range(TAPS):
                    found[k] = weighted([(spun[k], field)], found[k])
                cross.append(weighted([(tz[k], spun[k]) for k in range(TAPS)]))
                cross_out[p * Y + y, rows, :] = cross[y]
            for y in range(Y):
                along[p * Y + y, rows, :] = across_back(cross, ty, y)
        for k in range(TAPS):
            shift = k - RADIUS
            sums[k, rows, :] = jnp.where((lane - shift >= 0) & (lane - shift < LANES), found[k], 0.0)
        return carry

    lax.fori_loop(0, dmixed.shape[1] // ROWS, one, 0)


def rim(par, along, cols, far, out):
    def one(group, carry):
        rows = group_rows(group, PAIR)
        tt = rim_coeffs(par, cols, rows, far)
        for y in range(Y):
            column = [along[p * Y + y, rows, :] for p in range(PLANES)]
            for q in range(PLANES):
                out[q * Y + y, rows, :] = weighted(
                    [(tt[q - p], column[p]) for p in range(PLANES)]
                ).astype(out.dtype)
        return carry

    lax.fori_loop(0, out.shape[1] // PAIR, one, 0)


def inside(along, cols, base, out):
    def one(group, carry):
        rows = group_rows(group)
        tx = coeffs(cols, rows, T_X)
        for y in range(Y):
            column = [along[p * Y + y, rows, :] for p in range(PLANES)]
            for r in range(PLANES):
                out[r * Y + y, rows, :] = weighted(
                    [(tx[RADIUS + r - p], column[p]) for p in range(PLANES)], base[r * Y + y, rows, :]
                )
        return carry

    lax.fori_loop(0, out.shape[1] // ROWS, one, 0)


def tap_sums(par, own, near, far, mx, cross, along, z_sums, select, sums):
    reach = range(1 - PLANES, PLANES)

    def along_track(group, carry):
        rows = group_rows(group, PAIR)
        found = []
        for source in (own, near, far):
            total = dict.fromkeys(reach)
            for y in range(Y):
                back = [along[p * Y + y, rows, :] for p in range(PLANES)]
                field = [source[q * Y + y, rows, :].astype(F32) for q in range(PLANES)]
                for d in reach:
                    total[d] = weighted(
                        [(back[p], field[p + d]) for p in range(PLANES) if 0 <= p + d < PLANES], total[d]
                    )
            found.append(total)
        mine, close, away = found
        even = par[0] == 0
        low = [jnp.where(even, away[d], close[d]) for d in range(PLANES)]
        high = [jnp.where(even, close[-d], away[-d]) for d in range(PLANES)]
        resolved = [
            low[0], mine[-2] + low[1], mine[-1] + low[2], mine[0], mine[1] + high[2], mine[2] + high[1], high[0]
        ]
        for k in range(TAPS):
            sums[T_X + k, rows, :] = resolved[k]
        return carry

    lax.fori_loop(0, mx.shape[1] // PAIR, along_track, 0)

    def cross_track(group, carry):
        rows = group_rows(group)
        total = [None] * TAPS
        for p in range(PLANES):
            plane = [mx[p * Y + y, rows, :] for y in range(Y)]
            for y in range(Y):
                back = cross[p * Y + y, rows, :]
                for k in range(TAPS):
                    if 0 <= y + k - RADIUS < Y:
                        total[k] = weighted([(back, plane[y + k - RADIUS])], total[k])
        for k in range(TAPS):
            sums[T_Y + k, rows, :] = total[k]
        return carry

    lax.fori_loop(0, mx.shape[1] // ROWS, cross_track, 0)
    terms = [sums[k] for k in range(2 * TAPS)] + [z_sums[k] for k in range(TAPS)]
    wide = jnp.concatenate(terms, axis=1)
    high = wide.astype(BF16)
    rest = (wide - high.astype(F32)).astype(BF16)
    return dot(high, select[...]) + dot(rest, select[...])


def tiles(ref, first):
    return jnp.concatenate([ref[first + i] for i in range(CHUNK)], axis=1)


def put(ref, first, value):
    for i in range(CHUNK):
        ref[first + i] = value[:, i * LANES : (i + 1) * LANES].astype(ref.dtype)


def folded(value):
    total = value[:, :LANES]
    for i in range(1, CHUNK):
        total = total + value[:, i * LANES : (i + 1) * LANES]
    return total


def normalise(mixed):
    scale = 1.0 / mixed.shape[0]
    centred = mixed - jnp.sum(mixed, axis=0, keepdims=True) * scale
    variance = jnp.sum(centred * centred, axis=0, keepdims=True) * scale
    inverse = lax.rsqrt(variance + 1e-06)
    return centred * inverse, inverse


def normalise_back(g_norm, normal, inverse, gain):
    share = 1.0 / g_norm.shape[0]
    g_normal = g_norm * gain
    mean_a = jnp.sum(g_normal, axis=0, keepdims=True) * share
    mean_b = jnp.sum(g_normal * normal, axis=0, keepdims=True) * share
    return inverse * (g_normal - mean_a - normal * mean_b)


def dot(a, b):
    return jnp.dot(a, b, preferred_element_type=F32)


def dot_t(a, b):
    return lax.dot_general(a, b, (((1,), (1,)), ((), ())), preferred_element_type=F32)


def gelu_parts(hidden):
    square = hidden * hidden
    half = jnp.tanh(hidden * (GELU_A + GELU_B * square))
    rise = 0.5 + 0.5 * half
    act = (hidden * rise).astype(BF16)
    slope = rise + (hidden * (0.5 - 0.5 * (half * half))) * (GELU_A + 3.0 * GELU_B * square)
    return act, slope


def steps():
    return [(step, step * CHUNK) for step in range(OWN // CHUNK)]


def fold_stats(value):
    lane = lax.broadcasted_iota(jnp.int32, (ROWS, LANES), 1)
    parts, blocks = LANES // STAT, []
    for i in range(0, value.shape[0], ROWS):
        block = jnp.where(lane < STAT, value[i : i + ROWS], 0.0)
        shift = i // ROWS % parts * STAT
        blocks.append(pltpu.roll(block, shift, 1) if shift else block)
    sums = []
    for i in range(0, len(blocks), parts):
        total = blocks[i]
        for block in blocks[i + 1 : i + parts]:
            total = total + block
        sums.append(total)
    return jnp.concatenate(sums, axis=1)


def unfold_stats(folded_stats, channels):
    parts, blocks = LANES // STAT, []
    for i in range(channels // ROWS):
        block = folded_stats[:, i // parts * LANES : (i // parts + 1) * LANES]
        shift = (LANES - i % parts * STAT) % LANES
        blocks.append(pltpu.roll(block, shift, 1) if shift else block)
    return jnp.concatenate(blocks, axis=0)


def send_low(low, first, total):
    weights = total.shape[0] - ROWS
    low[first : first + weights] = total[:weights].astype(BF16)
    stats = total[weights:]
    high = stats.astype(BF16).astype(F32)
    low[first + weights : first + weights + PAIR] = jnp.concatenate([high, stats - high], axis=0).astype(BF16)


def take_low(low, first, height):
    weights = height - ROWS
    terms = low[first + weights : first + weights + PAIR].astype(F32)
    return jnp.concatenate(
        [low[first : first + weights].astype(F32), terms[:ROWS] + terms[ROWS:]], axis=0
    )


def pack_kernel(have, got, stats, total, low):
    both = jnp.concatenate([have[...] + got[...], fold_stats(stats[...])], axis=0)
    total[...] = both
    send_low(low, 0, both)


def gathered(have, first, second, third):
    height = have.shape[0]
    return (have[...] + take_low(first, 0, height)) + (take_low(second, 0, height) + take_low(third, 0, height))


def spread_two_kernel(have, first, second, third, total):
    total[...] = gathered(have, first, second, third)


def spread_one_kernel(have, first, second, third, two, total, low):
    out = gathered(have, first, second, third)
    height = out.shape[0]
    total[:height] = out
    total[height:] = two[...]
    send_low(low, 0, out)
    send_low(low, height + ROWS, two[...])


def joined_kernel(have, got, total):
    height = have.shape[0] // 2
    total[:height] = have[:height] + take_low(got, 0, height)
    total[height:] = have[height:] + take_low(got, height + ROWS, height)


def start_kernel(par, vol, near, tables, part, own, other, wide):
    unpack(vol, wide, own)
    unpack(near, wide, other)
    along_own(par, own, other, tables.at[0], part)


def forward_kernel(
    par, far, part, own_tiles, cols, tables, w_in, b_in, w_out, out, mixed, other, field, crossed, wide
):
    unpack(far, wide, other)
    along_far(par, part, other, tables.at[0], field)
    rest_of_conv(field, tables.at[0], crossed, mixed)
    gain, scale = cols[0, :, GAIN : GAIN + 1], cols[0, :, SCALE : SCALE + 1]
    for step, first in steps():
        normal, inverse = normalise(tiles(mixed, first))
        normed = (normal * gain).astype(BF16)
        hidden = dot(w_in[0], normed) + b_in[:, 0:1]
        half = jnp.tanh(hidden * (GELU_A + GELU_B * (hidden * hidden)))
        act = (hidden * (0.5 + 0.5 * half)).astype(BF16)
        put(out, first, tiles(own_tiles, first) + scale * dot(w_out[0], act))


def save_kernel(mixed, cols, w_in, b_in, normed, normal, inverse, act, slope):
    for step, first in steps():
        value, inverse[step] = normalise(tiles(mixed, first))
        put(normal, first, value)
        low = (value * cols[0, :, GAIN : GAIN + 1]).astype(BF16)
        put(normed, first, low)
        act[step], slope[step] = gelu_parts(dot(w_in[0], low) + b_in[:, 0:1])


def middle_kernel(par, mid, near, tables, part):
    along_own(par, mid, near, tables.at[1], part)


def turn_kernel(
    par, far, part, mid, labels, cols, tables, w_in, w_in_t, b_in, w_out, w_out_t, head, head_t,
    head_b, rim_far, rim_near, field, z_sums, cross, along, dmixed, base, keep, send, acc_gain, acc_scale, head_cols, head_bias,
    mixed, crossed, sums, acc_bias,
):
    channels = mid.shape[1]
    taps = tables.at[1]
    along_far(par, part, far, taps, field)
    rest_of_conv(field, taps, crossed, mixed)
    sums[...] = jnp.zeros_like(sums)
    acc_bias[...] = jnp.zeros_like(acc_bias)
    acc_gain[...] = jnp.zeros_like(acc_gain)
    acc_scale[...] = jnp.zeros_like(acc_scale)
    head_cols[...] = jnp.zeros_like(head_cols)
    head_bias[...] = jnp.zeros_like(head_bias)
    gain, scale = cols[1, :, GAIN : GAIN + 1], cols[1, :, SCALE : SCALE + 1]
    for step, first in steps():
        normal, inverse = normalise(tiles(mixed, first))
        normed = (normal * gain).astype(BF16)
        act, slope = gelu_parts(dot(w_in[1], normed) + b_in[:, 1:2])
        lifted = dot(w_out[1], act)
        final = (tiles(mid, first).astype(F32) + scale * lifted).astype(BF16)
        logits = dot(head[...], final) + head_b[...]
        raised = jnp.exp(logits - jnp.max(logits, axis=0, keepdims=True))
        probability = raised / jnp.sum(raised, axis=0, keepdims=True)
        classes = lax.broadcasted_iota(jnp.int32, logits.shape, 0)
        g_logits = probability - (labels[step] == classes).astype(F32)
        head_bias[...] += folded(g_logits)
        g_low = g_logits.astype(BF16)
        head_cols[...] += dot_t(final, g_low)
        grad = dot(head_t[...], g_low)
        acc_scale[...] += folded(grad * lifted)
        put(base, first, grad)
        g_lift = (grad * scale).astype(BF16)
        sums[0, :channels] += dot_t(g_lift, act)
        g_hidden = dot(w_out_t[1], g_lift) * slope
        acc_bias[...] += folded(g_hidden)
        g_hid = g_hidden.astype(BF16)
        sums[1, :channels] += dot_t(normed, g_hid)
        g_norm = dot(w_in_t[1], g_hid)
        acc_gain[...] += folded(g_norm * normal)
        put(dmixed, first, normalise_back(g_norm, normal, inverse, gain))
    convolve_back(dmixed, crossed, taps, cross, along, z_sums)
    rim(par, along, taps, True, rim_far)
    rim(par, along, taps, False, rim_near)
    sums[1, channels : channels + 1] = jnp.sum(acc_bias[...].T, axis=0, keepdims=True)
    keep[...] = sums[par[0]]
    send[...] = sums[1 - par[0]]


def total_of(ref):
    return jnp.sum(ref[...], axis=1, keepdims=True)


def taps_two_kernel(
    par, own, near, far, mx, cross, along, z_sums, select, base, tables, acc_gain, acc_scale, head_cols,
    head_bias, out, inner, sums,
):
    inside(along, tables.at[1], base, inner)
    value = tap_sums(par, own, near, far, mx, cross, along, z_sums, select, sums)
    lane = lax.broadcasted_iota(jnp.int32, out.shape, 1)
    value = jnp.where(lane == GAIN, total_of(acc_gain), value)
    value = jnp.where(lane == SCALE, total_of(acc_scale), value)
    for k in range(ROWS):
        value = jnp.where(lane == HEAD + k, head_cols[:, k : k + 1], value)
    out[...] = value
    out[:ROWS] = jnp.where(lane[:ROWS] == HEAD_BIAS, total_of(head_bias), out[:ROWS])


def taps_one_kernel(
    par, own, near, far, mx, cross, along, z_sums, select, acc_gain, gs_scale, out, sums
):
    value = tap_sums(par, own, near, far, mx, cross, along, z_sums, select, sums)
    lane = lax.broadcasted_iota(jnp.int32, out.shape, 1)
    value = jnp.where(lane == GAIN, total_of(acc_gain), value)
    out[...] = jnp.where(lane == SCALE, gs_scale[...], value)


def inside_kernel(along, base, tables, inner):
    inside(along, tables.at[0], base, inner)


def point_back_kernel(
    par, inner, near, far, act, slope, normed, cols, w_in_t, w_out, w_out_t,
    base, g_norm, keep, send, gs_scale, sums, acc_bias,
):
    channels = inner.shape[1]
    sums[...] = jnp.zeros_like(sums)
    acc_bias[...] = jnp.zeros_like(acc_bias)
    scale = cols[0, :, SCALE : SCALE + 1]
    for step, first in steps():
        grad = tiles(inner, first) + (tiles(near, first).astype(F32) + tiles(far, first).astype(F32))
        put(base, first, grad)
        g_lift = (grad * scale).astype(BF16)
        sums[0, :channels] += dot_t(g_lift, act[step])
        g_hidden = dot(w_out_t[0], g_lift) * slope[step]
        acc_bias[...] += folded(g_hidden)
        g_hid = g_hidden.astype(BF16)
        sums[1, :channels] += dot_t(tiles(normed, first), g_hid)
        put(g_norm, first, dot(w_in_t[0], g_hid))
    sums[1, channels : channels + 1] = jnp.sum(acc_bias[...].T, axis=0, keepdims=True)
    spread = jnp.sum(sums[0, :channels] * w_out[0].astype(F32), axis=1, keepdims=True)
    gs_scale[...] = spread / scale
    keep[...] = sums[par[0]]
    send[...] = sums[1 - par[0]]


def conv_back_kernel(
    par, g_norm, normal, inverse, mxy, cols, tables, rim_far, rim_near, z_sums, cross, along, acc_gain,
    dmixed,
):
    taps = tables.at[0]
    acc_gain[...] = jnp.zeros_like(acc_gain)
    for step, first in steps():
        value, unit = tiles(g_norm, first), tiles(normal, first)
        acc_gain[...] += folded(value * unit)
        put(dmixed, first, normalise_back(value, unit, inverse[step], cols[0, :, GAIN : GAIN + 1]))
    convolve_back(dmixed, mxy, taps, cross, along, z_sums)
    rim(par, along, taps, True, rim_far)
    rim(par, along, taps, False, rim_near)


def last_kernel(inner, near, far, out, token, total):
    token[...] = jnp.zeros_like(token)

    def add(tile, carry):
        total[tile] = inner[tile] + (near[tile].astype(F32) + far[tile].astype(F32))
        return carry

    lax.fori_loop(0, OWN, add, 0, unroll=2)

    def one(group, carry):
        rows = group_rows(group)
        for tile in range(OWN):
            out[pl.ds(group * ROWS * OWN + tile, ROWS, stride=OWN), :] = total[tile, rows, :]
        return carry

    lax.fori_loop(0, inner.shape[1] // ROWS, one, 0)


def final_kernel(share, par, mine, other, g_in_t, g_bias, g_out, g_taps, g_gain, g_scale, g_head, g_head_b):
    channels = g_out.shape[1]
    even = par[0] == 0
    height = mine.shape[0] // 2
    weights = height - ROWS
    for s in range(2):
        here, stop = s * height, s * height + weights
        first = jnp.where(even, mine[here:stop], other[here:stop]) * share
        second = jnp.where(even, other[here:stop], mine[here:stop]) * share
        g_out[s] = first[:channels]
        g_in_t[s] = second[:channels]
        g_bias[s : s + 1] = second[channels : channels + 1]
        stats = mine[stop : stop + ROWS] + other[stop : stop + ROWS]
        rows = unfold_stats(stats, channels).T * share
        for axis in range(3):
            for k in range(TAPS):
                g_taps[axis, k, s : s + 1] = rows[axis * TAPS + k : axis * TAPS + k + 1]
        g_gain[s : s + 1] = rows[GAIN : GAIN + 1]
        g_scale[s : s + 1] = rows[SCALE : SCALE + 1]
    g_head[...] = rows[HEAD : HEAD + g_head.shape[0]]
    g_head_b[...] = rows[HEAD_BIAS : HEAD_BIAS + 1, : g_head_b.shape[1]]


def call(kernel, name, operands, outs, scratch=(), room=8, after=()):
    smem = pl.BlockSpec(memory_space=pltpu.SMEM)
    vmem = pl.BlockSpec(memory_space=pltpu.VMEM)
    anywhere = pl.BlockSpec(memory_space=pl.ANY)
    count = len(operands)

    def run(*refs):
        kernel(*refs[:count], *refs[count + len(after) :])

    in_specs = [smem if x.dtype == jnp.int32 and x.shape == (1,) else vmem for x in operands]
    return pl.pallas_call(
        run,
        name=name,
        out_shape=tuple(outs),
        in_specs=in_specs + [anywhere] * len(after),
        out_specs=tuple([vmem] * len(outs)),
        scratch_shapes=list(scratch),
        compiler_params=pltpu.CompilerParams(vmem_limit_bytes=room * MIB),
        cost_estimate=pl.CostEstimate(flops=0, bytes_accessed=0, transcendentals=0),
    )(*operands, *after)


def pinned(dims, dtype=F32):
    return pltpu.VMEM(dims, dtype)


def shape(dims, dtype=F32):
    return jax.ShapeDtypeStruct(dims, dtype)


def near_swap(value):
    count = lax.axis_size("track")
    return lax.ppermute(value, "track", [(i, i ^ 1) for i in range(count)])


def far_swap(value):
    count = lax.axis_size("track")
    pairs = []
    for i in range(1, count - 1, 2):
        pairs += [(i, i + 1), (i + 1, i)]
    return lax.ppermute(value, "track", pairs)


def bit_swap(value, step):
    count = lax.axis_size("track")
    return lax.ppermute(value, "track", [(i, i ^ step) for i in range(count)])


def on_device(
    volume, labels, conv_taps, norm_gain, weight_in, bias_in, weight_out, layer_scale, head_weight, head_bias
):
    channels, planes, rows, depth = volume.shape
    hidden = weight_in.shape[1]
    classes = head_weight.shape[0]
    devices = lax.axis_size("track")
    share = 1.0 / float(devices * planes * rows * depth)
    par = (lax.axis_index("track") % 2).astype(jnp.int32).reshape(1)
    parts = OWN // CHUNK

    flat = volume.reshape(channels * OWN, depth)
    near = near_swap(flat)
    far = far_swap(flat)
    cols = jnp.swapaxes(
        jnp.concatenate(
            [conv_taps.reshape(2, 3 * TAPS, channels), norm_gain[:, None], layer_scale[:, None]], axis=1
        ), 1, 2,
    )
    b_in = bias_in.T
    head = jnp.zeros((ROWS, channels), BF16).at[:classes].set(head_weight)
    head_b = jnp.full((ROWS,), -1e30, F32).at[:classes].set(head_bias)[:, None]
    flat_labels = labels.reshape(parts, 1, CHUNK * depth)

    low = shape((OWN, channels, depth), BF16)
    full = shape((OWN, channels, depth))
    half = shape((channels + PAIR, hidden))
    s_full = pltpu.VMEM((OWN, channels, depth), F32)
    s_wide = pltpu.VMEM((channels * OWN, depth), F32)
    s_sums = pltpu.VMEM((2, channels + PAIR, hidden), F32)
    s_bias = pltpu.VMEM((hidden, LANES), F32)
    k_full = pinned((OWN, channels, depth))
    k_half = pinned((channels + PAIR, hidden))
    k_stat = pinned((channels, LANES))

    small = (cols, b_in, weight_in, weight_out, head, head_b, flat_labels)
    (tables, cols, b_in, w_in, w_in_t, w_out, w_out_t, head, head_t, head_b, flat_labels, select) = call(
        tables_kernel, "tables", small,
        [pinned((2, 4 * TAPS, channels, LANES)), pinned(cols.shape), pinned(b_in.shape),
         pinned(weight_in.shape, BF16), pinned(weight_out.shape, BF16), pinned(weight_out.shape, BF16),
         pinned(weight_in.shape, BF16), pinned(head.shape, BF16), pinned((channels, ROWS), BF16),
         pinned(head_b.shape), pinned(flat_labels.shape, jnp.int32),
         pinned((3 * TAPS * LANES, LANES), BF16)],
    )
    part, own_kept, near_kept = call(
        start_kernel, "start_one", (par, flat, near, tables), [k_full, k_full, k_full], [s_wide],
    )
    mid, mixed_one, far_kept, mx_one, mxy_one = call(
        forward_kernel, "forward_one", (par, far, part, own_kept, cols, tables, w_in, b_in, w_out),
        [low, k_full, k_full, k_full, k_full], [s_wide], 16,
    )
    near = near_swap(mid)
    far = far_swap(mid)
    normed, normal, inverse, act, slope = call(
        save_kernel, "save_one", (mixed_one, cols, w_in, b_in),
        [pinned((OWN, channels, depth), BF16), k_full, pinned((parts, 1, CHUNK * depth)),
         pinned((parts, hidden, CHUNK * depth), BF16), pinned((parts, hidden, CHUNK * depth))],
        (), 16,
    )
    (part,) = call(
        middle_kernel, "start_two", (par, mid, near, tables), [k_full], (), 4, after=(inverse,)
    )
    k_taps = pinned((TAPS, channels, LANES))
    s_taps = pltpu.VMEM((2 * TAPS, channels, LANES), F32)
    (rim_far, rim_near, mx, z_sums, cross, along, dmixed, base, keep, send,
     acc_gain, acc_scale, head_cols, head_lanes) = call(
        turn_kernel, "turn_two",
        (par, far, part, mid, flat_labels, cols, tables, w_in, w_in_t, b_in, w_out, w_out_t,
         head, head_t, head_b),
        [low, low, k_full, k_taps, k_full, k_full, k_full, k_full, k_half, half, k_stat, k_stat, pinned((channels, ROWS)),
         pinned((ROWS, LANES))],
        [s_full, s_full, s_sums, s_bias], 24,
    )
    rim_near = near_swap(rim_near)
    rim_far = far_swap(rim_far)
    got = near_swap(send)
    stats, inner = call(
        taps_two_kernel, "taps_two",
        (par, mid, near, far, mx, cross, along, z_sums, select, base, tables, acc_gain, acc_scale, head_cols,
         head_lanes),
        [k_stat, k_full], [s_taps], 8, after=(rim_near,),
    )
    tall = shape((channels + PAIR + ROWS, hidden))
    k_tall = pinned(tall.shape)
    tall_low = shape((channels + 2 * PAIR, hidden), BF16)
    two, two_low = call(
        pack_kernel, "pack_two", (keep, got, stats), [k_tall, tall_low], (), 4, after=(inner,)
    )
    got = [bit_swap(two_low, step) for step in (4, 8, 12)]
    base, g_norm, keep, send, gs_scale = call(
        point_back_kernel, "point_back_one",
        (par, inner, rim_near, rim_far, act, slope, normed, cols, w_in_t, w_out, w_out_t),
        [k_full, k_full, k_half, half, pinned((channels, 1))], [s_sums, s_bias], 16,
    )
    (two,) = call(spread_two_kernel, "sums_two", (two, *got), [k_tall], (), 4, after=(base,))
    got = near_swap(send)
    rim_far, rim_near, z_sums, cross, along, acc_gain = call(
        conv_back_kernel, "conv_back_one", (par, g_norm, normal, inverse, mxy_one, cols, tables),
        [low, low, k_taps, k_full, k_full, k_stat], [s_full], 12, after=(two,),
    )
    rim_near = near_swap(rim_near)
    rim_far = far_swap(rim_far)
    (stats,) = call(
        taps_one_kernel, "taps_one",
        (par, own_kept, near_kept, far_kept, mx_one, cross, along, z_sums, select, acc_gain, gs_scale),
        [k_stat], [s_taps], 8, after=(rim_near,),
    )
    one, one_low = call(pack_kernel, "pack_one", (keep, got, stats), [k_tall, tall_low], (), 4)
    got = [bit_swap(one_low, step) for step in (4, 8, 12)]
    (inner,) = call(inside_kernel, "inside_one", (along, base, tables), [k_full], (), 4, after=(one,))
    both_shape = (2 * tall.shape[0], hidden)
    both, both_low = call(
        spread_one_kernel, "sums_one", (one, *got, two),
        [pinned(both_shape), shape((2 * tall_low.shape[0], hidden), BF16)], (), 4, after=(inner,),
    )
    got = bit_swap(both_low, 2)
    grad, token = call(
        last_kernel, "last", (inner, rim_near, rim_far),
        [shape((channels * OWN, depth)), pinned((ROWS, LANES))], [s_full], 4,
        after=(both,),
    )
    (both,) = call(joined_kernel, "sums_last", (both, got), [shape(both_shape)], (), 4, after=(token,))
    step = 16
    while step < devices:
        both = both + bit_swap(both, step)
        step *= 2
    g_in_t, g_bias, g_out, g_taps, g_gain, g_scale, g_head, g_head_b = call(
        functools.partial(final_kernel, share), "final", (par, both, near_swap(both)),
        [shape((2, channels, hidden)), shape((2, hidden)), shape((2, channels, hidden)),
         shape((3, TAPS, 2, channels)), shape((2, channels)), shape((2, channels)),
         shape((classes, channels)), shape((1, classes))],
    )
    return (
        grad.reshape(volume.shape), jnp.moveaxis(g_taps, 2, 0), g_gain, jnp.swapaxes(g_in_t, 1, 2), g_bias, g_out, g_scale,
        g_head, g_head_b.reshape(classes),
    )


def solution(mesh):
    placed = (
        P(None, ("groups", "track"), None, None),
        P(("groups", "track"), None, None),
        P(), P(), P(), P(), P(), P(), P(), P(),
    )
    return jax.shard_map(
        on_device,
        mesh=mesh,
        in_specs=placed,
        out_specs=(
            P(None, ("groups", "track"), None, None),
            P("groups", None, None, None),
            P("groups", None),
            P("groups", None, None),
            P("groups", None),
            P("groups", None, None),
            P("groups", None),
            P("groups", None),
            P("groups"),
        ),
        check_vma=False,
    )
```

```python
import functools

import jax
import jax.numpy as jnp
from jax import lax
from jax.experimental import pallas as pl
from jax.experimental.pallas import tpu as pltpu
from jax.sharding import PartitionSpec as P

F32 = jnp.float32
BF16 = jnp.bfloat16
LANES = 128
ROWS = 8
PAIR = 16
RADIUS = 3
TAPS = 7
PLANES = 3
Y = 8
OWN = PLANES * Y
EXT = (PLANES + 2 * RADIUS) * Y
CHUNK = 12
GELU_A = 0.7978845608028654
GELU_B = 0.044715 * GELU_A
STAT = 32
MIB = 1024 * 1024


T_X, T_Y, T_Z, T_Z_BACK = 0, 7, 14, 21
GAIN, SCALE, HEAD_BIAS, HEAD = 21, 22, 23, 24


def group_rows(index, size=ROWS):
    return pl.ds(pl.multiple_of(index * size, size), size)


def coeffs(source, rows, first, count=TAPS):
    if len(source.shape) == 3:
        return [source[k, rows, :] for k in range(first, first + count)]
    found = []
    for k in range(first, first + count):
        column = source[rows, k : k + 1]
        found.append(jnp.broadcast_to(column, (column.shape[0], LANES)))
    return found


def tables_kernel(
    cols, b_in, w_in, w_out, head, head_b, labels,
    tables, cols_out, b_out, w_in_out, w_in_t, w_out_out, w_out_t, head_out, head_t, head_b_out, labels_out,
    select,
):
    def one(group, carry):
        rows = group_rows(group)
        lane = lax.broadcasted_iota(jnp.int32, (ROWS, LANES), 1)
        for s in range(2):
            for k, value in enumerate(coeffs(cols.at[s], rows, T_X, 2 * TAPS)):
                tables[s, k, rows, :] = value
            for k, value in enumerate(coeffs(cols.at[s], rows, T_Z)):
                for first, reach in ((T_Z, k - RADIUS), (T_Z_BACK, RADIUS - k)):
                    kept = (lane + reach >= 0) & (lane + reach < LANES)
                    tables[s, first + k, rows, :] = jnp.where(kept, value, 0.0)
        return carry

    lax.fori_loop(0, tables.shape[2] // ROWS, one, 0)
    lane = lax.broadcasted_iota(jnp.int32, (LANES, LANES), 1)
    for k in range(3 * TAPS):
        select[k * LANES : (k + 1) * LANES] = jnp.where(lane == k, 1.0, 0.0).astype(BF16)
    for s in range(2):
        w_in_t[s] = w_in[s].T
        w_out_t[s] = w_out[s].T
    head_t[...] = head[...].astype(F32).T.astype(BF16)
    for source, out in (
        (cols, cols_out), (b_in, b_out), (w_in, w_in_out), (w_out, w_out_out), (head, head_out),
        (head_b, head_b_out), (labels, labels_out),
    ):
        out[...] = source[...]


def rim_coeffs(par, cols, rows, low_if_even):
    tx = coeffs(cols, rows, T_X)
    zero = jnp.zeros_like(tx[0])
    low = (par[0] == 0) == low_if_even
    found = {}
    for d in range(1 - PLANES, PLANES):
        found[d] = jnp.where(low, tx[d] if d >= 0 else zero, tx[2 * RADIUS + d] if d <= 0 else zero)
    return found


def unpack(source, wide, out, first=0):
    wide[...] = source[...].astype(F32)

    def one(group, carry):
        rows = group_rows(group)
        for tile in range(OWN):
            out[first + tile, rows, :] = wide[pl.ds(group * ROWS * OWN + tile, ROWS, stride=OWN), :]
        return carry

    lax.fori_loop(0, out.shape[1] // ROWS, one, 0)


def widen(source, ext, first, count):
    def one(tile, carry):
        ext[first + tile] = source[tile].astype(F32)
        return carry

    lax.fori_loop(0, count, one, 0, unroll=4)


def weighted(terms, total=None):
    for coeff, value in terms:
        product = coeff * value
        total = product if total is None else total + product
    return total


def along_own(par, own, near, cols, out):
    def one(group, carry):
        rows = group_rows(group, PAIR)
        tx = coeffs(cols, rows, T_X)
        tn = rim_coeffs(par, cols, rows, False)
        for y in range(Y):
            mine = [own[r * Y + y, rows, :].astype(F32) for r in range(PLANES)]
            other = [near[r * Y + y, rows, :].astype(F32) for r in range(PLANES)]
            for p in range(PLANES):
                out[p * Y + y, rows, :] = weighted(
                    [(tx[RADIUS + r - p], mine[r]) for r in range(PLANES)]
                    + [(tn[q - p], other[q]) for q in range(PLANES)]
                )
        return carry

    lax.fori_loop(0, out.shape[1] // PAIR, one, 0)


def along_far(par, part, far, cols, out):
    def one(group, carry):
        rows = group_rows(group, PAIR)
        tf = rim_coeffs(par, cols, rows, True)
        for y in range(Y):
            other = [far[r * Y + y, rows, :].astype(F32) for r in range(PLANES)]
            for p in range(PLANES):
                out[p * Y + y, rows, :] = weighted(
                    [(tf[q - p], other[q]) for q in range(PLANES)], part[p * Y + y, rows, :]
                )
        return carry

    lax.fori_loop(0, out.shape[1] // PAIR, one, 0)


def across(field, ty, y):
    return weighted([(ty[k], field[y + k - RADIUS]) for k in range(TAPS) if 0 <= y + k - RADIUS < Y])


def across_back(field, ty, y):
    return weighted([(ty[k], field[y - k + RADIUS]) for k in range(TAPS) if 0 <= y - k + RADIUS < Y])


def turns(value, sign):
    low = value.astype(BF16)
    moved = []
    for k in range(TAPS):
        shift = sign * (k - RADIUS) % LANES
        moved.append(pltpu.roll(low, shift, 1).astype(F32) if shift else value)
    return moved


def rest_of_conv(field, cols, crossed, mixed):
    def one(group, carry):
        rows = group_rows(group, PAIR)
        ty = coeffs(cols, rows, T_Y)
        tz = coeffs(cols, rows, T_Z)
        for p in range(PLANES):
            plane = [field[p * Y + y, rows, :] for y in range(Y)]
            for y in range(Y):
                value = across(plane, ty, y)
                crossed[p * Y + y, rows, :] = value
                mixed[p * Y + y, rows, :] = weighted(zip(tz, turns(value, -1)))
        return carry

    lax.fori_loop(0, mixed.shape[1] // PAIR, one, 0)


def convolve_back(dmixed, mxy, cols, cross_out, along, sums):
    lane = lax.broadcasted_iota(jnp.int32, (PAIR, LANES), 1)

    def one(group, carry):
        rows = group_rows(group, PAIR)
        ty = coeffs(cols, rows, T_Y)
        tz = coeffs(cols, rows, T_Z_BACK)
        found = [None] * TAPS
        for p in range(PLANES):
            cross = []
            for y in range(Y):
                spun = turns(dmixed[p * Y + y, rows, :], 1)
                field = mxy[p * Y + y, rows, :]
                for k in range(TAPS):
                    found[k] = weighted([(spun[k], field)], found[k])
                cross.append(weighted(zip(tz, spun)))
                cross_out[p * Y + y, rows, :] = cross[y]
            for y in range(Y):
                along[p * Y + y, rows, :] = across_back(cross, ty, y)
        for k in range(TAPS):
            shift = k - RADIUS
            sums[k, rows, :] = jnp.where((lane - shift >= 0) & (lane - shift < LANES), found[k], 0.0)
        return carry

    lax.fori_loop(0, dmixed.shape[1] // PAIR, one, 0)


def rim(par, along, cols, far, out):
    def one(group, carry):
        rows = group_rows(group, PAIR)
        tt = rim_coeffs(par, cols, rows, far)
        for y in range(Y):
            column = [along[p * Y + y, rows, :] for p in range(PLANES)]
            for q in range(PLANES):
                out[q * Y + y, rows, :] = weighted(
                    [(tt[q - p], column[p]) for p in range(PLANES)]
                ).astype(out.dtype)
        return carry

    lax.fori_loop(0, out.shape[1] // PAIR, one, 0)


def inside(along, cols, base, out):
    def one(group, carry):
        rows = group_rows(group)
        tx = coeffs(cols, rows, T_X)
        for y in range(Y):
            column = [along[p * Y + y, rows, :] for p in range(PLANES)]
            for r in range(PLANES):
                out[r * Y + y, rows, :] = weighted(
                    [(tx[RADIUS + r - p], column[p]) for p in range(PLANES)], base[r * Y + y, rows, :]
                )
        return carry

    lax.fori_loop(0, out.shape[1] // ROWS, one, 0)


def tap_sums(par, own, near, far, mx, cross, along, z_sums, select, sums):
    reach = range(1 - PLANES, PLANES)

    def along_track(group, carry):
        rows = group_rows(group, PAIR)
        found = []
        for source in (own, near, far):
            total = dict.fromkeys(reach)
            for y in range(Y):
                back = [along[p * Y + y, rows, :] for p in range(PLANES)]
                field = [source[q * Y + y, rows, :].astype(F32) for q in range(PLANES)]
                for d in reach:
                    total[d] = weighted(
                        [(back[p], field[p + d]) for p in range(PLANES) if 0 <= p + d < PLANES], total[d]
                    )
            found.append(total)
        mine, close, away = found
        even = par[0] == 0
        low = [jnp.where(even, away[d], close[d]) for d in range(PLANES)]
        high = [jnp.where(even, close[-d], away[-d]) for d in range(PLANES)]
        resolved = [
            low[0], mine[-2] + low[1], mine[-1] + low[2], mine[0], mine[1] + high[2], mine[2] + high[1], high[0]
        ]
        for k in range(TAPS):
            sums[T_X + k, rows, :] = resolved[k]
        return carry

    lax.fori_loop(0, mx.shape[1] // PAIR, along_track, 0)

    def cross_track(group, carry):
        rows = group_rows(group)
        total = [None] * TAPS
        for p in range(PLANES):
            plane = [mx[p * Y + y, rows, :] for y in range(Y)]
            for y in range(Y):
                back = cross[p * Y + y, rows, :]
                for k in range(TAPS):
                    if 0 <= y + k - RADIUS < Y:
                        total[k] = weighted([(back, plane[y + k - RADIUS])], total[k])
        for k in range(TAPS):
            sums[T_Y + k, rows, :] = total[k]
        return carry

    lax.fori_loop(0, mx.shape[1] // ROWS, cross_track, 0)
    terms = [sums[k] for k in range(2 * TAPS)] + [z_sums[k] for k in range(TAPS)]
    wide = jnp.concatenate(terms, axis=1)
    high = wide.astype(BF16)
    rest = (wide - high.astype(F32)).astype(BF16)
    return dot(high, select[...]) + dot(rest, select[...])


def tiles(ref, first):
    return jnp.concatenate([ref[first + i] for i in range(CHUNK)], axis=1)


def put(ref, first, value):
    for i in range(CHUNK):
        ref[first + i] = value[:, i * LANES : (i + 1) * LANES].astype(ref.dtype)


def folded(value):
    total = value[:, :LANES]
    for i in range(1, CHUNK):
        total = total + value[:, i * LANES : (i + 1) * LANES]
    return total


def normalise(mixed):
    scale = 1.0 / mixed.shape[0]
    centred = mixed - jnp.sum(mixed, axis=0, keepdims=True) * scale
    variance = jnp.sum(centred * centred, axis=0, keepdims=True) * scale
    inverse = lax.rsqrt(variance + 1e-06)
    return centred * inverse, inverse


def normalise_back(g_norm, normal, inverse, gain):
    share = 1.0 / g_norm.shape[0]
    g_normal = g_norm * gain
    mean_a = jnp.sum(g_normal, axis=0, keepdims=True) * share
    mean_b = jnp.sum(g_normal * normal, axis=0, keepdims=True) * share
    return inverse * (g_normal - mean_a - normal * mean_b)


def dot(a, b):
    return jnp.dot(a, b, preferred_element_type=F32)


def dot_t(a, b):
    return lax.dot_general(a, b, (((1,), (1,)), ((), ())), preferred_element_type=F32)


def gelu_parts(hidden):
    square = hidden * hidden
    half = jnp.tanh(hidden * (GELU_A + GELU_B * square))
    rise = 0.5 + 0.5 * half
    act = (hidden * rise).astype(BF16)
    slope = rise + (hidden * (0.5 - 0.5 * (half * half))) * (GELU_A + 3.0 * GELU_B * square)
    return act, slope


def steps():
    return [(step, step * CHUNK) for step in range(OWN // CHUNK)]


def fold_stats(value):
    lane = lax.broadcasted_iota(jnp.int32, (ROWS, LANES), 1)
    parts, blocks = LANES // STAT, []
    for i in range(0, value.shape[0], ROWS):
        block = jnp.where(lane < STAT, value[i : i + ROWS], 0.0)
        shift = i // ROWS % parts * STAT
        blocks.append(pltpu.roll(block, shift, 1) if shift else block)
    sums = []
    for i in range(0, len(blocks), parts):
        total = blocks[i]
        for block in blocks[i + 1 : i + parts]:
            total = total + block
        sums.append(total)
    return jnp.concatenate(sums, axis=1)


def unfold_stats(folded_stats, channels):
    parts, blocks = LANES // STAT, []
    for i in range(channels // ROWS):
        block = folded_stats[:, i // parts * LANES : (i // parts + 1) * LANES]
        shift = (LANES - i % parts * STAT) % LANES
        blocks.append(pltpu.roll(block, shift, 1) if shift else block)
    return jnp.concatenate(blocks, axis=0)


def send_low(low, first, total):
    weights = total.shape[0] - ROWS
    low[first : first + weights] = total[:weights].astype(BF16)
    stats = total[weights:]
    high = stats.astype(BF16).astype(F32)
    low[first + weights : first + weights + PAIR] = jnp.concatenate([high, stats - high], axis=0).astype(BF16)


def take_low(low, first, height):
    weights = height - ROWS
    terms = low[first + weights : first + weights + PAIR].astype(F32)
    return jnp.concatenate(
        [low[first : first + weights].astype(F32), terms[:ROWS] + terms[ROWS:]], axis=0
    )


def pack_kernel(have, got, stats, total, low):
    both = jnp.concatenate([have[...] + got[...], fold_stats(stats[...])], axis=0)
    total[...] = both
    send_low(low, 0, both)


def gathered(have, first, second, third):
    height = have.shape[0]
    return (have[...] + take_low(first, 0, height)) + (take_low(second, 0, height) + take_low(third, 0, height))


def spread_two_kernel(have, first, second, third, total):
    total[...] = gathered(have, first, second, third)


def spread_one_kernel(have, first, second, third, two, total, low):
    out = gathered(have, first, second, third)
    height = out.shape[0]
    total[:height] = out
    total[height:] = two[...]
    send_low(low, 0, out)
    send_low(low, height + ROWS, two[...])


def joined_kernel(have, got, total):
    height = have.shape[0] // 2
    total[:height] = have[:height] + take_low(got, 0, height)
    total[height:] = have[height:] + take_low(got, height + ROWS, height)


def start_kernel(par, vol, near, tables, part, own, other, wide):
    unpack(vol, wide, own)
    unpack(near, wide, other)
    along_own(par, own, other, tables.at[0], part)


def forward_kernel(
    par, far, part, own_tiles, cols, tables, w_in, b_in, w_out, out, mixed, other, field, crossed, wide
):
    unpack(far, wide, other)
    along_far(par, part, other, tables.at[0], field)
    rest_of_conv(field, tables.at[0], crossed, mixed)
    gain, scale = cols[0, :, GAIN : GAIN + 1], cols[0, :, SCALE : SCALE + 1]
    for step, first in steps():
        normal, inverse = normalise(tiles(mixed, first))
        normed = (normal * gain).astype(BF16)
        hidden = dot(w_in[0], normed) + b_in[:, 0:1]
        half = jnp.tanh(hidden * (GELU_A + GELU_B * (hidden * hidden)))
        act = (hidden * (0.5 + 0.5 * half)).astype(BF16)
        put(out, first, tiles(own_tiles, first) + scale * dot(w_out[0], act))


def save_kernel(mixed, cols, w_in, b_in, normed, normal, inverse, act, slope):
    for step, first in steps():
        value, inverse[step] = normalise(tiles(mixed, first))
        put(normal, first, value)
        low = (value * cols[0, :, GAIN : GAIN + 1]).astype(BF16)
        put(normed, first, low)
        act[step], slope[step] = gelu_parts(dot(w_in[0], low) + b_in[:, 0:1])


def middle_kernel(par, mid, near, tables, part):
    along_own(par, mid, near, tables.at[1], part)


def turn_kernel(
    par, far, part, mid, labels, cols, tables, w_in, w_in_t, b_in, w_out, w_out_t, head, head_t,
    head_b, rim_far, rim_near, field, z_sums, cross, along, dmixed, base, keep, send, acc_gain, acc_scale, head_cols, head_bias,
    mixed, crossed, sums, acc_bias,
):
    channels = mid.shape[1]
    taps = tables.at[1]
    along_far(par, part, far, taps, field)
    rest_of_conv(field, taps, crossed, mixed)
    sums[...] = jnp.zeros_like(sums)
    acc_bias[...] = jnp.zeros_like(acc_bias)
    acc_gain[...] = jnp.zeros_like(acc_gain)
    acc_scale[...] = jnp.zeros_like(acc_scale)
    head_cols[...] = jnp.zeros_like(head_cols)
    head_bias[...] = jnp.zeros_like(head_bias)
    gain, scale = cols[1, :, GAIN : GAIN + 1], cols[1, :, SCALE : SCALE + 1]
    for step, first in steps():
        normal, inverse = normalise(tiles(mixed, first))
        normed = (normal * gain).astype(BF16)
        act, slope = gelu_parts(dot(w_in[1], normed) + b_in[:, 1:2])
        lifted = dot(w_out[1], act)
        final = (tiles(mid, first).astype(F32) + scale * lifted).astype(BF16)
        logits = dot(head[...], final) + head_b[...]
        raised = jnp.exp(logits - jnp.max(logits, axis=0, keepdims=True))
        probability = raised / jnp.sum(raised, axis=0, keepdims=True)
        classes = lax.broadcasted_iota(jnp.int32, logits.shape, 0)
        g_logits = probability - (labels[step] == classes).astype(F32)
        head_bias[...] += folded(g_logits)
        g_low = g_logits.astype(BF16)
        head_cols[...] += dot_t(final, g_low)
        grad = dot(head_t[...], g_low)
        acc_scale[...] += folded(grad * lifted)
        put(base, first, grad)
        g_lift = (grad * scale).astype(BF16)
        sums[0, :channels] += dot_t(g_lift, act)
        g_hidden = dot(w_out_t[1], g_lift) * slope
        acc_bias[...] += folded(g_hidden)
        g_hid = g_hidden.astype(BF16)
        sums[1, :channels] += dot_t(normed, g_hid)
        g_norm = dot(w_in_t[1], g_hid)
        acc_gain[...] += folded(g_norm * normal)
        put(dmixed, first, normalise_back(g_norm, normal, inverse, gain))
    convolve_back(dmixed, crossed, taps, cross, along, z_sums)
    rim(par, along, taps, True, rim_far)
    rim(par, along, taps, False, rim_near)
    sums[1, channels : channels + 1] = jnp.sum(acc_bias[...].T, axis=0, keepdims=True)
    keep[...] = sums[par[0]]
    send[...] = sums[1 - par[0]]


def total_of(ref):
    return jnp.sum(ref[...], axis=1, keepdims=True)


def taps_two_kernel(
    par, own, near, far, mx, cross, along, z_sums, select, base, tables, acc_gain, acc_scale, head_cols,
    head_bias, out, inner, sums,
):
    inside(along, tables.at[1], base, inner)
    value = tap_sums(par, own, near, far, mx, cross, along, z_sums, select, sums)
    lane = lax.broadcasted_iota(jnp.int32, out.shape, 1)
    value = jnp.where(lane == GAIN, total_of(acc_gain), value)
    value = jnp.where(lane == SCALE, total_of(acc_scale), value)
    for k in range(ROWS):
        value = jnp.where(lane == HEAD + k, head_cols[:, k : k + 1], value)
    out[...] = value
    out[:ROWS] = jnp.where(lane[:ROWS] == HEAD_BIAS, total_of(head_bias), out[:ROWS])


def taps_one_kernel(
    par, own, near, far, mx, cross, along, z_sums, select, acc_gain, gs_scale, out, sums
):
    value = tap_sums(par, own, near, far, mx, cross, along, z_sums, select, sums)
    lane = lax.broadcasted_iota(jnp.int32, out.shape, 1)
    value = jnp.where(lane == GAIN, total_of(acc_gain), value)
    out[...] = jnp.where(lane == SCALE, gs_scale[...], value)


def inside_kernel(along, base, tables, inner):
    inside(along, tables.at[0], base, inner)


def point_back_kernel(
    par, inner, near, far, act, slope, normed, cols, w_in_t, w_out, w_out_t,
    base, g_norm, keep, send, gs_scale, sums, acc_bias,
):
    channels = inner.shape[1]
    sums[...] = jnp.zeros_like(sums)
    acc_bias[...] = jnp.zeros_like(acc_bias)
    scale = cols[0, :, SCALE : SCALE + 1]
    for step, first in steps():
        grad = tiles(inner, first) + (tiles(near, first).astype(F32) + tiles(far, first).astype(F32))
        put(base, first, grad)
        g_lift = (grad * scale).astype(BF16)
        sums[0, :channels] += dot_t(g_lift, act[step])
        g_hidden = dot(w_out_t[0], g_lift) * slope[step]
        acc_bias[...] += folded(g_hidden)
        g_hid = g_hidden.astype(BF16)
        sums[1, :channels] += dot_t(tiles(normed, first), g_hid)
        put(g_norm, first, dot(w_in_t[0], g_hid))
    sums[1, channels : channels + 1] = jnp.sum(acc_bias[...].T, axis=0, keepdims=True)
    spread = jnp.sum(sums[0, :channels] * w_out[0].astype(F32), axis=1, keepdims=True)
    gs_scale[...] = spread / scale
    keep[...] = sums[par[0]]
    send[...] = sums[1 - par[0]]


def conv_back_kernel(
    par, g_norm, normal, inverse, mxy, cols, tables, rim_far, rim_near, z_sums, cross, along, acc_gain,
    dmixed,
):
    taps = tables.at[0]
    acc_gain[...] = jnp.zeros_like(acc_gain)
    for step, first in steps():
        value, unit = tiles(g_norm, first), tiles(normal, first)
        acc_gain[...] += folded(value * unit)
        put(dmixed, first, normalise_back(value, unit, inverse[step], cols[0, :, GAIN : GAIN + 1]))
    convolve_back(dmixed, mxy, taps, cross, along, z_sums)
    rim(par, along, taps, True, rim_far)
    rim(par, along, taps, False, rim_near)


def last_kernel(inner, near, far, out, token, total):
    token[...] = jnp.zeros_like(token)

    def add(tile, carry):
        total[tile] = inner[tile] + (near[tile].astype(F32) + far[tile].astype(F32))
        return carry

    lax.fori_loop(0, OWN, add, 0, unroll=2)

    def one(group, carry):
        rows = group_rows(group)
        for tile in range(OWN):
            out[pl.ds(group * ROWS * OWN + tile, ROWS, stride=OWN), :] = total[tile, rows, :]
        return carry

    lax.fori_loop(0, inner.shape[1] // ROWS, one, 0)


def final_kernel(share, par, mine, other, g_in_t, g_bias, g_out, g_taps, g_gain, g_scale, g_head, g_head_b):
    channels = g_out.shape[1]
    even = par[0] == 0
    height = mine.shape[0] // 2
    weights = height - ROWS
    for s in range(2):
        here, stop = s * height, s * height + weights
        first = jnp.where(even, mine[here:stop], other[here:stop]) * share
        second = jnp.where(even, other[here:stop], mine[here:stop]) * share
        g_out[s] = first[:channels]
        g_in_t[s] = second[:channels]
        g_bias[s : s + 1] = second[channels : channels + 1]
        stats = mine[stop : stop + ROWS] + other[stop : stop + ROWS]
        rows = unfold_stats(stats, channels).T * share
        for axis in range(3):
            for k in range(TAPS):
                g_taps[axis, k, s : s + 1] = rows[axis * TAPS + k : axis * TAPS + k + 1]
        g_gain[s : s + 1] = rows[GAIN : GAIN + 1]
        g_scale[s : s + 1] = rows[SCALE : SCALE + 1]
    g_head[...] = rows[HEAD : HEAD + g_head.shape[0]]
    g_head_b[...] = rows[HEAD_BIAS : HEAD_BIAS + 1, : g_head_b.shape[1]]


def call(kernel, name, operands, outs, scratch=(), room=8, after=()):
    smem = pl.BlockSpec(memory_space=pltpu.SMEM)
    vmem = pl.BlockSpec(memory_space=pltpu.VMEM)
    anywhere = pl.BlockSpec(memory_space=pl.ANY)
    count = len(operands)

    def run(*refs):
        kernel(*refs[:count], *refs[count + len(after) :])

    in_specs = [smem if x.dtype == jnp.int32 and x.shape == (1,) else vmem for x in operands]
    return pl.pallas_call(
        run,
        name=name,
        out_shape=tuple(outs),
        in_specs=in_specs + [anywhere] * len(after),
        out_specs=tuple([vmem] * len(outs)),
        scratch_shapes=list(scratch),
        compiler_params=pltpu.CompilerParams(vmem_limit_bytes=room * MIB),
        cost_estimate=pl.CostEstimate(flops=0, bytes_accessed=0, transcendentals=0),
    )(*operands, *after)


def pinned(dims, dtype=F32):
    return pltpu.VMEM(dims, dtype)


def shape(dims, dtype=F32):
    return jax.ShapeDtypeStruct(dims, dtype)


def near_swap(value):
    count = lax.axis_size("track")
    return lax.ppermute(value, "track", [(i, i ^ 1) for i in range(count)])


def far_swap(value):
    count = lax.axis_size("track")
    pairs = []
    for i in range(1, count - 1, 2):
        pairs += [(i, i + 1), (i + 1, i)]
    return lax.ppermute(value, "track", pairs)


def bit_swap(value, step):
    count = lax.axis_size("track")
    return lax.ppermute(value, "track", [(i, i ^ step) for i in range(count)])


def on_device(
    volume, labels, conv_taps, norm_gain, weight_in, bias_in, weight_out, layer_scale, head_weight, head_bias
):
    channels, planes, rows, depth = volume.shape
    hidden = weight_in.shape[1]
    classes = head_weight.shape[0]
    devices = lax.axis_size("track")
    share = 1.0 / float(devices * planes * rows * depth)
    par = (lax.axis_index("track") % 2).astype(jnp.int32).reshape(1)
    parts = OWN // CHUNK

    flat = volume.reshape(channels * OWN, depth)
    near = near_swap(flat)
    far = far_swap(flat)
    cols = jnp.swapaxes(
        jnp.concatenate(
            [conv_taps.reshape(2, 3 * TAPS, channels), norm_gain[:, None], layer_scale[:, None]], axis=1
        ), 1, 2,
    )
    b_in = bias_in.T
    head = jnp.zeros((ROWS, channels), BF16).at[:classes].set(head_weight)
    head_b = jnp.full((ROWS,), -1e30, F32).at[:classes].set(head_bias)[:, None]
    flat_labels = labels.reshape(parts, 1, CHUNK * depth)

    low = shape((OWN, channels, depth), BF16)
    full = shape((OWN, channels, depth))
    half = shape((channels + PAIR, hidden))
    s_full = pltpu.VMEM((OWN, channels, depth), F32)
    s_wide = pltpu.VMEM((channels * OWN, depth), F32)
    s_sums = pltpu.VMEM((2, channels + PAIR, hidden), F32)
    s_bias = pltpu.VMEM((hidden, LANES), F32)
    k_full = pinned((OWN, channels, depth))
    k_half = pinned((channels + PAIR, hidden))
    k_stat = pinned((channels, LANES))

    small = (cols, b_in, weight_in, weight_out, head, head_b, flat_labels)
    (tables, cols, b_in, w_in, w_in_t, w_out, w_out_t, head, head_t, head_b, flat_labels, select) = call(
        tables_kernel, "tables", small,
        [pinned((2, 4 * TAPS, channels, LANES)), pinned(cols.shape), pinned(b_in.shape),
         pinned(weight_in.shape, BF16), pinned(weight_out.shape, BF16), pinned(weight_out.shape, BF16),
         pinned(weight_in.shape, BF16), pinned(head.shape, BF16), pinned((channels, ROWS), BF16),
         pinned(head_b.shape), pinned(flat_labels.shape, jnp.int32),
         pinned((3 * TAPS * LANES, LANES), BF16)],
    )
    part, own_kept, near_kept = call(
        start_kernel, "start_one", (par, flat, near, tables), [k_full, k_full, k_full], [s_wide],
    )
    mid, mixed_one, far_kept, mx_one, mxy_one = call(
        forward_kernel, "forward_one", (par, far, part, own_kept, cols, tables, w_in, b_in, w_out),
        [low, k_full, k_full, k_full, k_full], [s_wide], 8,
    )
    near = near_swap(mid)
    far = far_swap(mid)
    normed, normal, inverse, act, slope = call(
        save_kernel, "save_one", (mixed_one, cols, w_in, b_in),
        [pinned((OWN, channels, depth), BF16), k_full, pinned((parts, 1, CHUNK * depth)),
         pinned((parts, hidden, CHUNK * depth), BF16), pinned((parts, hidden, CHUNK * depth))],
        (), 16,
    )
    (part,) = call(
        middle_kernel, "start_two", (par, mid, near, tables), [k_full], (), 4, after=(inverse,)
    )
    k_taps = pinned((TAPS, channels, LANES))
    s_taps = pltpu.VMEM((2 * TAPS, channels, LANES), F32)
    (rim_far, rim_near, mx, z_sums, cross, along, dmixed, base, keep, send,
     acc_gain, acc_scale, head_cols, head_lanes) = call(
        turn_kernel, "turn_two",
        (par, far, part, mid, flat_labels, cols, tables, w_in, w_in_t, b_in, w_out, w_out_t,
         head, head_t, head_b),
        [low, low, k_full, k_taps, k_full, k_full, k_full, k_full, k_half, half, k_stat, k_stat, pinned((channels, ROWS)),
         pinned((ROWS, LANES))],
        [s_full, s_full, s_sums, s_bias], 24,
    )
    rim_near = near_swap(rim_near)
    rim_far = far_swap(rim_far)
    got = near_swap(send)
    stats, inner = call(
        taps_two_kernel, "taps_two",
        (par, mid, near, far, mx, cross, along, z_sums, select, base, tables, acc_gain, acc_scale, head_cols,
         head_lanes),
        [k_stat, k_full], [s_taps], 8, after=(rim_near,),
    )
    tall = shape((channels + PAIR + ROWS, hidden))
    k_tall = pinned(tall.shape)
    tall_low = shape((channels + 2 * PAIR, hidden), BF16)
    two, two_low = call(
        pack_kernel, "pack_two", (keep, got, stats), [k_tall, tall_low], (), 4, after=(inner,)
    )
    got = [bit_swap(two_low, step) for step in (4, 8, 12)]
    base, g_norm, keep, send, gs_scale = call(
        point_back_kernel, "point_back_one",
        (par, inner, rim_near, rim_far, act, slope, normed, cols, w_in_t, w_out, w_out_t),
        [k_full, k_full, k_half, half, pinned((channels, 1))], [s_sums, s_bias], 8,
    )
    (two,) = call(spread_two_kernel, "sums_two", (two, *got), [k_tall], (), 4, after=(base,))
    got = near_swap(send)
    rim_far, rim_near, z_sums, cross, along, acc_gain = call(
        conv_back_kernel, "conv_back_one", (par, g_norm, normal, inverse, mxy_one, cols, tables),
        [low, low, k_taps, k_full, k_full, k_stat], [s_full], 8, after=(two,),
    )
    rim_near = near_swap(rim_near)
    rim_far = far_swap(rim_far)
    (stats,) = call(
        taps_one_kernel, "taps_one",
        (par, own_kept, near_kept, far_kept, mx_one, cross, along, z_sums, select, acc_gain, gs_scale),
        [k_stat], [s_taps], 8, after=(rim_near,),
    )
    one, one_low = call(pack_kernel, "pack_one", (keep, got, stats), [k_tall, tall_low], (), 4)
    got = [bit_swap(one_low, step) for step in (4, 8, 12)]
    (inner,) = call(inside_kernel, "inside_one", (along, base, tables), [k_full], (), 4, after=(one,))
    both_shape = (2 * tall.shape[0], hidden)
    both, both_low = call(
        spread_one_kernel, "sums_one", (one, *got, two),
        [pinned(both_shape), shape((2 * tall_low.shape[0], hidden), BF16)], (), 4, after=(inner,),
    )
    got = bit_swap(both_low, 2)
    grad, token = call(
        last_kernel, "last", (inner, rim_near, rim_far),
        [shape((channels * OWN, depth)), pinned((ROWS, LANES))], [s_full], 4,
        after=(both,),
    )
    (both,) = call(joined_kernel, "sums_last", (both, got), [shape(both_shape)], (), 4, after=(token,))
    step = 16
    while step < devices:
        both = both + bit_swap(both, step)
        step *= 2
    g_in_t, g_bias, g_out, g_taps, g_gain, g_scale, g_head, g_head_b = call(
        functools.partial(final_kernel, share), "final", (par, both, near_swap(both)),
        [shape((2, channels, hidden)), shape((2, hidden)), shape((2, channels, hidden)),
         shape((3, TAPS, 2, channels)), shape((2, channels)), shape((2, channels)),
         shape((classes, channels)), shape((1, classes))],
    )
    return (
        grad.reshape(volume.shape), jnp.moveaxis(g_taps, 2, 0), g_gain, jnp.swapaxes(g_in_t, 1, 2), g_bias, g_out, g_scale,
        g_head, g_head_b.reshape(classes),
    )


def solution(mesh):
    placed = (
        P(None, ("groups", "track"), None, None),
        P(("groups", "track"), None, None),
        P(), P(), P(), P(), P(), P(), P(), P(),
    )
    return jax.shard_map(
        on_device,
        mesh=mesh,
        in_specs=placed,
        out_specs=(
            P(None, ("groups", "track"), None, None),
            P("groups", None, None, None),
            P("groups", None),
            P("groups", None, None),
            P("groups", None),
            P("groups", None, None),
            P("groups", None),
            P("groups", None),
            P("groups"),
        ),
        check_vma=False,
    )
```

```python
import functools

import jax
import jax.numpy as jnp
from jax import lax
from jax.experimental import pallas as pl
from jax.experimental.pallas import tpu as pltpu
from jax.sharding import PartitionSpec as P

F32 = jnp.float32
BF16 = jnp.bfloat16
LANES = 128
ROWS = 8
PAIR = 16
RADIUS = 3
TAPS = 7
PLANES = 3
Y = 8
OWN = PLANES * Y
EXT = (PLANES + 2 * RADIUS) * Y
CHUNK = 12
GELU_A = 0.7978845608028654
GELU_B = 0.044715 * GELU_A
STAT = 32
MIB = 1024 * 1024


T_X, T_Y, T_Z, T_Z_BACK = 0, 7, 14, 21
GAIN, SCALE, HEAD_BIAS, HEAD = 21, 22, 23, 24


def group_rows(index, size=ROWS):
    return pl.ds(pl.multiple_of(index * size, size), size)


def coeffs(source, rows, first, count=TAPS):
    if len(source.shape) == 3:
        return [source[k, rows, :] for k in range(first, first + count)]
    found = []
    for k in range(first, first + count):
        column = source[rows, k : k + 1]
        found.append(jnp.broadcast_to(column, (column.shape[0], LANES)))
    return found


def tables_kernel(
    cols, b_in, w_in, w_out, head, head_b, labels,
    tables, cols_out, b_out, w_in_out, w_in_t, w_out_out, w_out_t, head_out, head_t, head_b_out, labels_out,
    select,
):
    def one(group, carry):
        rows = group_rows(group)
        lane = lax.broadcasted_iota(jnp.int32, (ROWS, LANES), 1)
        for s in range(2):
            for k, value in enumerate(coeffs(cols.at[s], rows, T_X, 2 * TAPS)):
                tables[s, k, rows, :] = value
            for k, value in enumerate(coeffs(cols.at[s], rows, T_Z)):
                for first, reach in ((T_Z, k - RADIUS), (T_Z_BACK, RADIUS - k)):
                    kept = (lane + reach >= 0) & (lane + reach < LANES)
                    tables[s, first + k, rows, :] = jnp.where(kept, value, 0.0)
        return carry

    lax.fori_loop(0, tables.shape[2] // ROWS, one, 0)
    lane = lax.broadcasted_iota(jnp.int32, (LANES, LANES), 1)
    for k in range(3 * TAPS):
        select[k * LANES : (k + 1) * LANES] = jnp.where(lane == k, 1.0, 0.0).astype(BF16)
    for s in range(2):
        w_in_t[s] = w_in[s].T
        w_out_t[s] = w_out[s].T
    head_t[...] = head[...].astype(F32).T.astype(BF16)
    for source, out in (
        (cols, cols_out), (b_in, b_out), (w_in, w_in_out), (w_out, w_out_out), (head, head_out),
        (head_b, head_b_out), (labels, labels_out),
    ):
        out[...] = source[...]


def rim_coeffs(par, cols, rows, low_if_even):
    tx = coeffs(cols, rows, T_X)
    zero = jnp.zeros_like(tx[0])
    low = (par[0] == 0) == low_if_even
    found = {}
    for d in range(1 - PLANES, PLANES):
        found[d] = jnp.where(low, tx[d] if d >= 0 else zero, tx[2 * RADIUS + d] if d <= 0 else zero)
    return found


def unpack(source, wide, out, first=0):
    wide[...] = source[...].astype(F32)

    def one(group, carry):
        rows = group_rows(group)
        for tile in range(OWN):
            out[first + tile, rows, :] = wide[pl.ds(group * ROWS * OWN + tile, ROWS, stride=OWN), :]
        return carry

    lax.fori_loop(0, out.shape[1] // ROWS, one, 0)


def widen(source, ext, first, count):
    def one(tile, carry):
        ext[first + tile] = source[tile].astype(F32)
        return carry

    lax.fori_loop(0, count, one, 0, unroll=4)


def weighted(terms, total=None):
    for coeff, value in terms:
        product = coeff * value
        total = product if total is None else total + product
    return total


def along_own(par, own, near, cols, out):
    def one(group, carry):
        rows = group_rows(group, PAIR)
        tx = coeffs(cols, rows, T_X)
        tn = rim_coeffs(par, cols, rows, False)
        for y in range(Y):
            mine = [own[r * Y + y, rows, :].astype(F32) for r in range(PLANES)]
            other = [near[r * Y + y, rows, :].astype(F32) for r in range(PLANES)]
            for p in range(PLANES):
                out[p * Y + y, rows, :] = weighted(
                    [(tx[RADIUS + r - p], mine[r]) for r in range(PLANES)]
                    + [(tn[q - p], other[q]) for q in range(PLANES)]
                )
        return carry

    lax.fori_loop(0, out.shape[1] // PAIR, one, 0)


def along_far(par, part, far, cols, out):
    def one(group, carry):
        rows = group_rows(group, PAIR)
        tf = rim_coeffs(par, cols, rows, True)
        for y in range(Y):
            other = [far[r * Y + y, rows, :].astype(F32) for r in range(PLANES)]
            for p in range(PLANES):
                out[p * Y + y, rows, :] = weighted(
                    [(tf[q - p], other[q]) for q in range(PLANES)], part[p * Y + y, rows, :]
                )
        return carry

    lax.fori_loop(0, out.shape[1] // PAIR, one, 0)


def across(field, ty, y):
    return weighted([(ty[k], field[y + k - RADIUS]) for k in range(TAPS) if 0 <= y + k - RADIUS < Y])


def across_back(field, ty, y):
    return weighted([(ty[k], field[y - k + RADIUS]) for k in range(TAPS) if 0 <= y - k + RADIUS < Y])


def turns(value, sign):
    low = value.astype(BF16)
    moved = []
    for k in range(TAPS):
        shift = sign * (k - RADIUS) % LANES
        moved.append(pltpu.roll(low, shift, 1).astype(F32) if shift else value)
    return moved


def rest_of_conv(field, cols, crossed, mixed):
    def one(group, carry):
        rows = group_rows(group, PAIR)
        ty = coeffs(cols, rows, T_Y)
        tz = coeffs(cols, rows, T_Z)
        for p in range(PLANES):
            plane = [field[p * Y + y, rows, :] for y in range(Y)]
            for y in range(Y):
                value = across(plane, ty, y)
                crossed[p * Y + y, rows, :] = value
                mixed[p * Y + y, rows, :] = weighted(zip(tz, turns(value, -1)))
        return carry

    lax.fori_loop(0, mixed.shape[1] // PAIR, one, 0)


def convolve_back(dmixed, mxy, cols, cross_out, along, sums):
    lane = lax.broadcasted_iota(jnp.int32, (PAIR, LANES), 1)

    def one(group, carry):
        rows = group_rows(group, PAIR)
        ty = coeffs(cols, rows, T_Y)
        tz = coeffs(cols, rows, T_Z_BACK)
        found = [None] * TAPS
        for p in range(PLANES):
            cross = []
            for y in range(Y):
                spun = turns(dmixed[p * Y + y, rows, :], 1)
                field = mxy[p * Y + y, rows, :]
                for k in range(TAPS):
                    found[k] = weighted([(spun[k], field)], found[k])
                cross.append(weighted(zip(tz, spun)))
                cross_out[p * Y + y, rows, :] = cross[y]
            for y in range(Y):
                along[p * Y + y, rows, :] = across_back(cross, ty, y)
        for k in range(TAPS):
            shift = k - RADIUS
            sums[k, rows, :] = jnp.where((lane - shift >= 0) & (lane - shift < LANES), found[k], 0.0)
        return carry

    lax.fori_loop(0, dmixed.shape[1] // PAIR, one, 0)


def rim(par, along, cols, far, out):
    def one(group, carry):
        rows = group_rows(group, PAIR)
        tt = rim_coeffs(par, cols, rows, far)
        for y in range(Y):
            column = [along[p * Y + y, rows, :] for p in range(PLANES)]
            for q in range(PLANES):
                out[q * Y + y, rows, :] = weighted(
                    [(tt[q - p], column[p]) for p in range(PLANES)]
                ).astype(out.dtype)
        return carry

    lax.fori_loop(0, out.shape[1] // PAIR, one, 0)


def inside(along, cols, base, out):
    def one(group, carry):
        rows = group_rows(group)
        tx = coeffs(cols, rows, T_X)
        for y in range(Y):
            column = [along[p * Y + y, rows, :] for p in range(PLANES)]
            for r in range(PLANES):
                out[r * Y + y, rows, :] = weighted(
                    [(tx[RADIUS + r - p], column[p]) for p in range(PLANES)], base[r * Y + y, rows, :]
                )
        return carry

    lax.fori_loop(0, out.shape[1] // ROWS, one, 0)


def tap_sums(par, own, near, far, mx, cross, along, z_sums, select, sums):
    reach = range(1 - PLANES, PLANES)

    def along_track(group, carry):
        rows = group_rows(group, PAIR)
        found = []
        for source in (own, near, far):
            total = dict.fromkeys(reach)
            for y in range(Y):
                back = [along[p * Y + y, rows, :] for p in range(PLANES)]
                field = [source[q * Y + y, rows, :].astype(F32) for q in range(PLANES)]
                for d in reach:
                    total[d] = weighted(
                        [(back[p], field[p + d]) for p in range(PLANES) if 0 <= p + d < PLANES], total[d]
                    )
            found.append(total)
        mine, close, away = found
        even = par[0] == 0
        low = [jnp.where(even, away[d], close[d]) for d in range(PLANES)]
        high = [jnp.where(even, close[-d], away[-d]) for d in range(PLANES)]
        resolved = [
            low[0], mine[-2] + low[1], mine[-1] + low[2], mine[0], mine[1] + high[2], mine[2] + high[1], high[0]
        ]
        for k in range(TAPS):
            sums[T_X + k, rows, :] = resolved[k]
        return carry

    lax.fori_loop(0, mx.shape[1] // PAIR, along_track, 0)

    def cross_track(group, carry):
        rows = group_rows(group)
        total = [None] * TAPS
        for p in range(PLANES):
            plane = [mx[p * Y + y, rows, :] for y in range(Y)]
            for y in range(Y):
                back = cross[p * Y + y, rows, :]
                for k in range(TAPS):
                    if 0 <= y + k - RADIUS < Y:
                        total[k] = weighted([(back, plane[y + k - RADIUS])], total[k])
        for k in range(TAPS):
            sums[T_Y + k, rows, :] = total[k]
        return carry

    lax.fori_loop(0, mx.shape[1] // ROWS, cross_track, 0)
    terms = [sums[k] for k in range(2 * TAPS)] + [z_sums[k] for k in range(TAPS)]
    wide = jnp.concatenate(terms, axis=1)
    high = wide.astype(BF16)
    rest = (wide - high.astype(F32)).astype(BF16)
    return dot(high, select[...]) + dot(rest, select[...])


def tiles(ref, first):
    return jnp.concatenate([ref[first + i] for i in range(CHUNK)], axis=1)


def put(ref, first, value):
    for i in range(CHUNK):
        ref[first + i] = value[:, i * LANES : (i + 1) * LANES].astype(ref.dtype)


def folded(value):
    total = value[:, :LANES]
    for i in range(1, CHUNK):
        total = total + value[:, i * LANES : (i + 1) * LANES]
    return total


def normalise(mixed):
    scale = 1.0 / mixed.shape[0]
    centred = mixed - jnp.sum(mixed, axis=0, keepdims=True) * scale
    variance = jnp.sum(centred * centred, axis=0, keepdims=True) * scale
    inverse = lax.rsqrt(variance + 1e-06)
    return centred * inverse, inverse


def normalise_back(g_norm, normal, inverse, gain):
    share = 1.0 / g_norm.shape[0]
    g_normal = g_norm * gain
    mean_a = jnp.sum(g_normal, axis=0, keepdims=True) * share
    mean_b = jnp.sum(g_normal * normal, axis=0, keepdims=True) * share
    return inverse * (g_normal - mean_a - normal * mean_b)


def dot(a, b):
    return jnp.dot(a, b, preferred_element_type=F32)


def dot_t(a, b):
    return lax.dot_general(a, b, (((1,), (1,)), ((), ())), preferred_element_type=F32)


def with_ones(normed):
    row = lax.broadcasted_iota(jnp.int32, (PAIR, normed.shape[1]), 0)
    return jnp.concatenate([normed, jnp.where(row == 0, 1.0, 0.0).astype(BF16)], axis=0)


def gelu_parts(hidden):
    square = hidden * hidden
    half = jnp.tanh(hidden * (GELU_A + GELU_B * square))
    rise = 0.5 + 0.5 * half
    act = (hidden * rise).astype(BF16)
    slope = rise + (hidden * (0.5 - 0.5 * (half * half))) * (GELU_A + 3.0 * GELU_B * square)
    return act, slope


def steps():
    return [(step, step * CHUNK) for step in range(OWN // CHUNK)]


def fold_stats(value):
    lane = lax.broadcasted_iota(jnp.int32, (ROWS, LANES), 1)
    parts, blocks = LANES // STAT, []
    for i in range(0, value.shape[0], ROWS):
        block = jnp.where(lane < STAT, value[i : i + ROWS], 0.0)
        shift = i // ROWS % parts * STAT
        blocks.append(pltpu.roll(block, shift, 1) if shift else block)
    sums = []
    for i in range(0, len(blocks), parts):
        total = blocks[i]
        for block in blocks[i + 1 : i + parts]:
            total = total + block
        sums.append(total)
    return jnp.concatenate(sums, axis=1)


def unfold_stats(folded_stats, channels):
    parts, blocks = LANES // STAT, []
    for i in range(channels // ROWS):
        block = folded_stats[:, i // parts * LANES : (i // parts + 1) * LANES]
        shift = (LANES - i % parts * STAT) % LANES
        blocks.append(pltpu.roll(block, shift, 1) if shift else block)
    return jnp.concatenate(blocks, axis=0)


def send_low(low, first, total):
    weights = total.shape[0] - ROWS
    low[first : first + weights] = total[:weights].astype(BF16)
    stats = total[weights:]
    high = stats.astype(BF16).astype(F32)
    low[first + weights : first + weights + PAIR] = jnp.concatenate([high, stats - high], axis=0).astype(BF16)


def take_low(low, first, height):
    weights = height - ROWS
    terms = low[first + weights : first + weights + PAIR].astype(F32)
    return jnp.concatenate(
        [low[first : first + weights].astype(F32), terms[:ROWS] + terms[ROWS:]], axis=0
    )


def pack_kernel(have, got, stats, total, low):
    both = jnp.concatenate([have[...] + got[...], fold_stats(stats[...])], axis=0)
    total[...] = both
    send_low(low, 0, both)


def gathered(have, first, second, third):
    height = have.shape[0]
    return (have[...] + take_low(first, 0, height)) + (take_low(second, 0, height) + take_low(third, 0, height))


def first_kernel(have, got, total, low):
    out = have[...] + got[...]
    total[...] = out
    low[...] = out.astype(BF16)


def spread_two_kernel(have, first, second, third, total):
    total[...] = gathered(have, first, second, third)


def spread_kernel(have, first, second, third, total):
    total[...] = (have[...] + first[...].astype(F32)) + (second[...].astype(F32) + third[...].astype(F32))


def stats_pack_kernel(stats, total, low):
    out = fold_stats(stats[...])
    high = out.astype(BF16).astype(F32)
    total[...] = out
    low[...] = jnp.concatenate([high, out - high], axis=0).astype(BF16)


def spread_one_kernel(one, stats, first, second, third, two, total, low):
    terms = [ref[...].astype(F32) for ref in (first, second, third)]
    first, second, third = (term[:ROWS] + term[ROWS:] for term in terms)
    out = jnp.concatenate([one[...], (stats[...] + first) + (second + third)], axis=0)
    height = out.shape[0]
    total[:height] = out
    total[height:] = two[...]
    send_low(low, 0, out)
    send_low(low, height + ROWS, two[...])


def joined_kernel(have, got, total):
    height = have.shape[0] // 2
    total[:height] = have[:height] + take_low(got, 0, height)
    total[height:] = have[height:] + take_low(got, height + ROWS, height)


def start_kernel(par, vol, near, tables, part, own, other, wide):
    unpack(vol, wide, own)
    unpack(near, wide, other)
    along_own(par, own, other, tables.at[0], part)


def forward_kernel(
    par, far, part, own_tiles, cols, tables, w_in, b_in, w_out, out, mixed, other, field, crossed, wide
):
    unpack(far, wide, other)
    along_far(par, part, other, tables.at[0], field)
    rest_of_conv(field, tables.at[0], crossed, mixed)
    gain, scale = cols[0, :, GAIN : GAIN + 1], cols[0, :, SCALE : SCALE + 1]
    for step, first in steps():
        normal, inverse = normalise(tiles(mixed, first))
        normed = (normal * gain).astype(BF16)
        hidden = dot(w_in[0], normed) + b_in[:, 0:1]
        half = jnp.tanh(hidden * (GELU_A + GELU_B * (hidden * hidden)))
        act = (hidden * (0.5 + 0.5 * half)).astype(BF16)
        put(out, first, tiles(own_tiles, first) + scale * dot(w_out[0], act))


def save_kernel(mixed, cols, w_in, b_in, normed, normal, inverse, act, slope):
    for step, first in steps():
        value, inverse[step] = normalise(tiles(mixed, first))
        put(normal, first, value)
        low = (value * cols[0, :, GAIN : GAIN + 1]).astype(BF16)
        put(normed, first, low)
        act[step], slope[step] = gelu_parts(dot(w_in[0], low) + b_in[:, 0:1])


def middle_kernel(par, mid, near, tables, part):
    along_own(par, mid, near, tables.at[1], part)


def turn_kernel(
    par, far, part, mid, labels, cols, tables, w_in, w_in_t, b_in, w_out, w_out_t, head, head_t,
    head_b, rim_far, field, z_sums, cross, along, dmixed, base, keep, send, acc_gain, acc_scale, head_cols, head_bias,
    mixed, crossed, sums,
):
    channels = mid.shape[1]
    taps = tables.at[1]
    along_far(par, part, far, taps, field)
    rest_of_conv(field, taps, crossed, mixed)
    sums[...] = jnp.zeros_like(sums)
    acc_gain[...] = jnp.zeros_like(acc_gain)
    acc_scale[...] = jnp.zeros_like(acc_scale)
    head_cols[...] = jnp.zeros_like(head_cols)
    head_bias[...] = jnp.zeros_like(head_bias)
    gain, scale = cols[1, :, GAIN : GAIN + 1], cols[1, :, SCALE : SCALE + 1]
    for step, first in steps():
        normal, inverse = normalise(tiles(mixed, first))
        normed = (normal * gain).astype(BF16)
        act, slope = gelu_parts(dot(w_in[1], normed) + b_in[:, 1:2])
        lifted = dot(w_out[1], act)
        final = (tiles(mid, first).astype(F32) + scale * lifted).astype(BF16)
        logits = dot(head[...], final) + head_b[...]
        raised = jnp.exp(logits - jnp.max(logits, axis=0, keepdims=True))
        probability = raised / jnp.sum(raised, axis=0, keepdims=True)
        classes = lax.broadcasted_iota(jnp.int32, logits.shape, 0)
        g_logits = probability - (labels[step] == classes).astype(F32)
        head_bias[...] += folded(g_logits)
        g_low = g_logits.astype(BF16)
        head_cols[...] += dot_t(final, g_low)
        grad = dot(head_t[...], g_low)
        acc_scale[...] += folded(grad * lifted)
        put(base, first, grad)
        g_lift = (grad * scale).astype(BF16)
        sums[0, :channels] += dot_t(g_lift, act)
        g_hid = (dot(w_out_t[1], g_lift) * slope).astype(BF16)
        sums[1] += dot_t(with_ones(normed), g_hid)
        g_norm = dot(w_in_t[1], g_hid)
        acc_gain[...] += folded(g_norm * normal)
        put(dmixed, first, normalise_back(g_norm, normal, inverse, gain))
    convolve_back(dmixed, crossed, taps, cross, along, z_sums)
    rim(par, along, taps, True, rim_far)
    keep[...] = sums[par[0]]
    send[...] = sums[1 - par[0]]


def total_of(ref):
    return jnp.sum(ref[...], axis=1, keepdims=True)


def taps_two_kernel(
    par, own, near, far, mx, cross, along, z_sums, select, base, tables, acc_gain, acc_scale, head_cols,
    head_bias, out, inner, rim_near, sums,
):
    rim(par, along, tables.at[1], False, rim_near)
    inside(along, tables.at[1], base, inner)
    value = tap_sums(par, own, near, far, mx, cross, along, z_sums, select, sums)
    lane = lax.broadcasted_iota(jnp.int32, out.shape, 1)
    value = jnp.where(lane == GAIN, total_of(acc_gain), value)
    value = jnp.where(lane == SCALE, total_of(acc_scale), value)
    for k in range(ROWS):
        value = jnp.where(lane == HEAD + k, head_cols[:, k : k + 1], value)
    out[...] = value
    out[:ROWS] = jnp.where(lane[:ROWS] == HEAD_BIAS, total_of(head_bias), out[:ROWS])


def taps_one_kernel(
    par, own, near, far, mx, cross, along, z_sums, select, acc_gain, gs_scale, out, sums
):
    value = tap_sums(par, own, near, far, mx, cross, along, z_sums, select, sums)
    lane = lax.broadcasted_iota(jnp.int32, out.shape, 1)
    value = jnp.where(lane == GAIN, total_of(acc_gain), value)
    out[...] = jnp.where(lane == SCALE, gs_scale[...], value)


def inside_kernel(par, along, base, tables, inner, rim_near):
    rim(par, along, tables.at[0], False, rim_near)
    inside(along, tables.at[0], base, inner)


def point_back_kernel(
    par, inner, near, far, act, slope, normed, cols, w_in_t, w_out, w_out_t,
    base, g_norm, keep, send, gs_scale, sums,
):
    channels = inner.shape[1]
    sums[...] = jnp.zeros_like(sums)
    scale = cols[0, :, SCALE : SCALE + 1]
    for step, first in steps():
        grad = tiles(inner, first) + (tiles(near, first).astype(F32) + tiles(far, first).astype(F32))
        put(base, first, grad)
        g_lift = (grad * scale).astype(BF16)
        sums[0, :channels] += dot_t(g_lift, act[step])
        g_hid = (dot(w_out_t[0], g_lift) * slope[step]).astype(BF16)
        sums[1] += dot_t(with_ones(tiles(normed, first)), g_hid)
        put(g_norm, first, dot(w_in_t[0], g_hid))
    spread = jnp.sum(sums[0, :channels] * w_out[0].astype(F32), axis=1, keepdims=True)
    gs_scale[...] = spread / scale
    keep[...] = sums[par[0]]
    send[...] = sums[1 - par[0]]


def conv_back_kernel(
    par, g_norm, normal, inverse, mxy, cols, tables, rim_far, z_sums, cross, along, acc_gain,
    dmixed,
):
    taps = tables.at[0]
    acc_gain[...] = jnp.zeros_like(acc_gain)
    for step, first in steps():
        value, unit = tiles(g_norm, first), tiles(normal, first)
        acc_gain[...] += folded(value * unit)
        put(dmixed, first, normalise_back(value, unit, inverse[step], cols[0, :, GAIN : GAIN + 1]))
    convolve_back(dmixed, mxy, taps, cross, along, z_sums)
    rim(par, along, taps, True, rim_far)


def last_kernel(inner, near, far, out, token, total):
    token[...] = jnp.zeros_like(token)

    def add(tile, carry):
        total[tile] = inner[tile] + (near[tile].astype(F32) + far[tile].astype(F32))
        return carry

    lax.fori_loop(0, OWN, add, 0, unroll=2)

    def one(group, carry):
        rows = group_rows(group)
        for tile in range(OWN):
            out[pl.ds(group * ROWS * OWN + tile, ROWS, stride=OWN), :] = total[tile, rows, :]
        return carry

    lax.fori_loop(0, inner.shape[1] // ROWS, one, 0)


def final_kernel(share, par, mine, other, g_in_t, g_bias, g_out, g_taps, g_gain, g_scale, g_head, g_head_b):
    channels = g_out.shape[1]
    even = par[0] == 0
    height = mine.shape[0] // 2
    weights = height - ROWS
    for s in range(2):
        here, stop = s * height, s * height + weights
        first = jnp.where(even, mine[here:stop], other[here:stop]) * share
        second = jnp.where(even, other[here:stop], mine[here:stop]) * share
        g_out[s] = first[:channels]
        g_in_t[s] = second[:channels]
        g_bias[s : s + 1] = second[channels : channels + 1]
        stats = mine[stop : stop + ROWS] + other[stop : stop + ROWS]
        rows = unfold_stats(stats, channels).T * share
        for axis in range(3):
            for k in range(TAPS):
                g_taps[axis, k, s : s + 1] = rows[axis * TAPS + k : axis * TAPS + k + 1]
        g_gain[s : s + 1] = rows[GAIN : GAIN + 1]
        g_scale[s : s + 1] = rows[SCALE : SCALE + 1]
    g_head[...] = rows[HEAD : HEAD + g_head.shape[0]]
    g_head_b[...] = rows[HEAD_BIAS : HEAD_BIAS + 1, : g_head_b.shape[1]]


def call(kernel, name, operands, outs, scratch=(), room=8, after=(), flops=0):
    smem = pl.BlockSpec(memory_space=pltpu.SMEM)
    vmem = pl.BlockSpec(memory_space=pltpu.VMEM)
    anywhere = pl.BlockSpec(memory_space=pl.ANY)
    count = len(operands)

    def run(*refs):
        kernel(*refs[:count], *refs[count + len(after) :])

    in_specs = [smem if x.dtype == jnp.int32 and x.shape == (1,) else vmem for x in operands]
    return pl.pallas_call(
        run,
        name=name,
        out_shape=tuple(outs),
        in_specs=in_specs + [anywhere] * len(after),
        out_specs=tuple([vmem] * len(outs)),
        scratch_shapes=list(scratch),
        compiler_params=pltpu.CompilerParams(vmem_limit_bytes=room * MIB),
        cost_estimate=pl.CostEstimate(flops=flops, bytes_accessed=0, transcendentals=0),
    )(*operands, *after)


def pinned(dims, dtype=F32):
    return pltpu.VMEM(dims, dtype)


def shape(dims, dtype=F32):
    return jax.ShapeDtypeStruct(dims, dtype)


def near_swap(value):
    count = lax.axis_size("track")
    return lax.ppermute(value, "track", [(i, i ^ 1) for i in range(count)])


def far_swap(value):
    count = lax.axis_size("track")
    pairs = []
    for i in range(1, count - 1, 2):
        pairs += [(i, i + 1), (i + 1, i)]
    return lax.ppermute(value, "track", pairs)


def bit_swap(value, step):
    count = lax.axis_size("track")
    return lax.ppermute(value, "track", [(i, i ^ step) for i in range(count)])


def on_device(
    volume, labels, conv_taps, norm_gain, weight_in, bias_in, weight_out, layer_scale, head_weight, head_bias
):
    channels, planes, rows, depth = volume.shape
    hidden = weight_in.shape[1]
    classes = head_weight.shape[0]
    devices = lax.axis_size("track")
    share = 1.0 / float(devices * planes * rows * depth)
    par = (lax.axis_index("track") % 2).astype(jnp.int32).reshape(1)
    parts = OWN // CHUNK

    flat = volume.reshape(channels * OWN, depth)
    near = near_swap(flat)
    far = far_swap(flat)
    cols = jnp.swapaxes(
        jnp.concatenate(
            [conv_taps.reshape(2, 3 * TAPS, channels), norm_gain[:, None], layer_scale[:, None]], axis=1
        ), 1, 2,
    )
    b_in = bias_in.T
    head = jnp.zeros((ROWS, channels), BF16).at[:classes].set(head_weight)
    head_b = jnp.full((ROWS,), -1e30, F32).at[:classes].set(head_bias)[:, None]
    flat_labels = labels.reshape(parts, 1, CHUNK * depth)

    low = shape((OWN, channels, depth), BF16)
    full = shape((OWN, channels, depth))
    half = shape((channels + PAIR, hidden))
    s_full = pltpu.VMEM((OWN, channels, depth), F32)
    s_wide = pltpu.VMEM((channels * OWN, depth), F32)
    s_sums = pltpu.VMEM((2, channels + PAIR, hidden), F32)
    k_full = pinned((OWN, channels, depth))
    k_half = pinned((channels + PAIR, hidden))
    k_stat = pinned((channels, LANES))

    small = (cols, b_in, weight_in, weight_out, head, head_b, flat_labels)
    (tables, cols, b_in, w_in, w_in_t, w_out, w_out_t, head, head_t, head_b, flat_labels, select) = call(
        tables_kernel, "tables", small,
        [pinned((2, 4 * TAPS, channels, LANES)), pinned(cols.shape), pinned(b_in.shape),
         pinned(weight_in.shape, BF16), pinned(weight_out.shape, BF16), pinned(weight_out.shape, BF16),
         pinned(weight_in.shape, BF16), pinned(head.shape, BF16), pinned((channels, ROWS), BF16),
         pinned(head_b.shape), pinned(flat_labels.shape, jnp.int32),
         pinned((3 * TAPS * LANES, LANES), BF16)],
    )
    part, own_kept, near_kept = call(
        start_kernel, "start_one", (par, flat, near, tables), [k_full, k_full, k_full], [s_wide],
    )
    mid, mixed_one, far_kept, mx_one, mxy_one = call(
        forward_kernel, "forward_one", (par, far, part, own_kept, cols, tables, w_in, b_in, w_out),
        [low, k_full, k_full, k_full, k_full], [s_wide], 8,
    )
    near = near_swap(mid)
    far = far_swap(mid)
    normed, normal, inverse, act, slope = call(
        save_kernel, "save_one", (mixed_one, cols, w_in, b_in),
        [pinned((OWN, channels, depth), BF16), k_full, pinned((parts, 1, CHUNK * depth)),
         pinned((parts, hidden, CHUNK * depth), BF16), pinned((parts, hidden, CHUNK * depth))],
        (), 16,
    )
    (part,) = call(
        middle_kernel, "start_two", (par, mid, near, tables), [k_full], (), 4, after=(inverse,)
    )
    k_taps = pinned((TAPS, channels, LANES))
    s_taps = pltpu.VMEM((2 * TAPS, channels, LANES), F32)
    (rim_far, mx, z_sums, cross, along, dmixed, base, keep, send,
     acc_gain, acc_scale, head_cols, head_lanes) = call(
        turn_kernel, "turn_two",
        (par, far, part, mid, flat_labels, cols, tables, w_in, w_in_t, b_in, w_out, w_out_t,
         head, head_t, head_b),
        [low, k_full, k_taps, k_full, k_full, k_full, k_full, k_half, half, k_stat, k_stat, pinned((channels, ROWS)),
         pinned((ROWS, LANES))],
        [s_full, s_full, s_sums], 24,
    )
    rim_far = far_swap(rim_far)
    got = near_swap(send)
    stats, inner, rim_near = call(
        taps_two_kernel, "taps_two",
        (par, mid, near, far, mx, cross, along, z_sums, select, base, tables, acc_gain, acc_scale, head_cols,
         head_lanes),
        [k_stat, k_full, low], [s_taps], 8, after=(got,),
    )
    rim_near = near_swap(rim_near)
    tall = shape((channels + PAIR + ROWS, hidden))
    k_tall = pinned(tall.shape)
    tall_low = shape((channels + 2 * PAIR, hidden), BF16)
    two, two_low = call(
        pack_kernel, "pack_two", (keep, got, stats), [k_tall, tall_low], (), 4, after=(inner,)
    )
    got = [bit_swap(two_low, step) for step in (4, 8, 12)]
    base, g_norm, keep, send, gs_scale = call(
        point_back_kernel, "point_back_one",
        (par, inner, rim_near, rim_far, act, slope, normed, cols, w_in_t, w_out, w_out_t),
        [k_full, k_full, k_half, half, pinned((channels, 1))], [s_sums], 8,
    )
    got_two, got = got, near_swap(send)
    rim_far, z_sums, cross, along, acc_gain = call(
        conv_back_kernel, "conv_back_one", (par, g_norm, normal, inverse, mxy_one, cols, tables),
        [low, k_taps, k_full, k_full, k_stat], [s_full], 8,
    )
    rim_far = far_swap(rim_far)
    half_low = shape((channels + PAIR, hidden), BF16)
    (two,) = call(
        spread_two_kernel, "sums_two", (two, *got_two), [k_tall], (), 4, after=(along,), flops=4 * 10**10
    )
    one, one_low = call(first_kernel, "sums_one_a", (keep, got), [k_half, half_low], (), 4, after=(two,))
    got = [bit_swap(one_low, step) for step in (4, 8, 12)]
    (stats,) = call(
        taps_one_kernel, "taps_one",
        (par, own_kept, near_kept, far_kept, mx_one, cross, along, z_sums, select, acc_gain, gs_scale),
        [k_stat], [s_taps], 8, after=(two,),
    )
    (one,) = call(spread_kernel, "sums_one_b", (one, *got), [k_half], (), 4, after=(stats,), flops=4 * 10**9)
    stats, stats_low = call(
        stats_pack_kernel, "pack_stats", (stats,), [pinned((ROWS, hidden)), shape((PAIR, hidden), BF16)], (), 4
    )
    got_stats = [bit_swap(stats_low, step) for step in (4, 8, 12)]
    inner, rim_near = call(
        inside_kernel, "inside_one", (par, along, base, tables), [k_full, low], (), 4
    )
    rim_near = near_swap(rim_near)
    both_shape = (2 * tall.shape[0], hidden)
    both, both_low = call(
        spread_one_kernel, "sums_one", (one, stats, *got_stats, two),
        [pinned(both_shape), shape((2 * tall_low.shape[0], hidden), BF16)], (), 4, after=(inner,),
    )
    got = bit_swap(both_low, 2)
    grad, token = call(
        last_kernel, "last", (inner, rim_near, rim_far),
        [shape((channels * OWN, depth)), pinned((ROWS, LANES))], [s_full], 4,
        after=(both,),
    )
    (both,) = call(joined_kernel, "sums_last", (both, got), [shape(both_shape)], (), 4, after=(token,))
    step = 16
    while step < devices:
        both = both + bit_swap(both, step)
        step *= 2
    g_in_t, g_bias, g_out, g_taps, g_gain, g_scale, g_head, g_head_b = call(
        functools.partial(final_kernel, share), "final", (par, both, near_swap(both)),
        [shape((2, channels, hidden)), shape((2, hidden)), shape((2, channels, hidden)),
         shape((3, TAPS, 2, channels)), shape((2, channels)), shape((2, channels)),
         shape((classes, channels)), shape((1, classes))],
    )
    return (
        grad.reshape(volume.shape), jnp.moveaxis(g_taps, 2, 0), g_gain, jnp.swapaxes(g_in_t, 1, 2), g_bias, g_out, g_scale,
        g_head, g_head_b.reshape(classes),
    )


def solution(mesh):
    placed = (
        P(None, ("groups", "track"), None, None),
        P(("groups", "track"), None, None),
        P(), P(), P(), P(), P(), P(), P(), P(),
    )
    return jax.shard_map(
        on_device,
        mesh=mesh,
        in_specs=placed,
        out_specs=(
            P(None, ("groups", "track"), None, None),
            P("groups", None, None, None),
            P("groups", None),
            P("groups", None, None),
            P("groups", None),
            P("groups", None, None),
            P("groups", None),
            P("groups", None),
            P("groups"),
        ),
        check_vma=False,
    )
```

```python
import functools

import jax
import jax.numpy as jnp
from jax import lax
from jax.experimental import pallas as pl
from jax.experimental.pallas import tpu as pltpu
from jax.sharding import PartitionSpec as P

F32 = jnp.float32
BF16 = jnp.bfloat16
LANES = 128
ROWS = 8
PAIR = 16
RADIUS = 3
TAPS = 7
PLANES = 3
Y = 8
OWN = PLANES * Y
EXT = (PLANES + 2 * RADIUS) * Y
CHUNK = 12
GELU_A = 0.7978845608028654
GELU_B = 0.044715 * GELU_A
STAT = 32
MIB = 1024 * 1024


T_X, T_Y, T_Z, T_Z_BACK = 0, 7, 14, 21
GAIN, SCALE, HEAD_BIAS, HEAD = 21, 22, 23, 24


def group_rows(index, size=ROWS):
    return pl.ds(pl.multiple_of(index * size, size), size)


def coeffs(source, rows, first, count=TAPS):
    if len(source.shape) == 3:
        return [source[k, rows, :] for k in range(first, first + count)]
    found = []
    for k in range(first, first + count):
        column = source[rows, k : k + 1]
        found.append(jnp.broadcast_to(column, (column.shape[0], LANES)))
    return found


def tables_kernel(
    cols, b_in, w_in, w_out, head, head_b, labels,
    tables, cols_out, b_out, w_in_out, w_in_t, w_out_out, w_out_t, head_out, head_t, head_b_out, labels_out,
    select,
):
    def one(group, carry):
        rows = group_rows(group)
        lane = lax.broadcasted_iota(jnp.int32, (ROWS, LANES), 1)
        for s in range(2):
            for k, value in enumerate(coeffs(cols.at[s], rows, T_X, 2 * TAPS)):
                tables[s, k, rows, :] = value
            for k, value in enumerate(coeffs(cols.at[s], rows, T_Z)):
                for first, reach in ((T_Z, k - RADIUS), (T_Z_BACK, RADIUS - k)):
                    kept = (lane + reach >= 0) & (lane + reach < LANES)
                    tables[s, first + k, rows, :] = jnp.where(kept, value, 0.0)
        return carry

    lax.fori_loop(0, tables.shape[2] // ROWS, one, 0)
    lane = lax.broadcasted_iota(jnp.int32, (LANES, LANES), 1)
    for k in range(3 * TAPS):
        select[k * LANES : (k + 1) * LANES] = jnp.where(lane == k, 1.0, 0.0).astype(BF16)
    for s in range(2):
        w_in_t[s] = w_in[s].T
        w_out_t[s] = w_out[s].T
    head_t[...] = head[...].astype(F32).T.astype(BF16)
    for source, out in (
        (cols, cols_out), (b_in, b_out), (w_in, w_in_out), (w_out, w_out_out), (head, head_out),
        (head_b, head_b_out), (labels, labels_out),
    ):
        out[...] = source[...]


def rim_coeffs(par, cols, rows, low_if_even):
    tx = coeffs(cols, rows, T_X)
    zero = jnp.zeros_like(tx[0])
    low = (par[0] == 0) == low_if_even
    found = {}
    for d in range(1 - PLANES, PLANES):
        found[d] = jnp.where(low, tx[d] if d >= 0 else zero, tx[2 * RADIUS + d] if d <= 0 else zero)
    return found


def unpack(source, wide, out, first=0):
    wide[...] = source[...].astype(F32)

    def one(group, carry):
        rows = group_rows(group)
        for tile in range(OWN):
            out[first + tile, rows, :] = wide[pl.ds(group * ROWS * OWN + tile, ROWS, stride=OWN), :]
        return carry

    lax.fori_loop(0, out.shape[1] // ROWS, one, 0)


def widen(source, ext, first, count):
    def one(tile, carry):
        ext[first + tile] = source[tile].astype(F32)
        return carry

    lax.fori_loop(0, count, one, 0, unroll=4)


def weighted(terms, total=None):
    for coeff, value in terms:
        product = coeff * value
        total = product if total is None else total + product
    return total


def along_own(par, own, near, cols, out):
    def one(group, carry):
        rows = group_rows(group, PAIR)
        tx = coeffs(cols, rows, T_X)
        tn = rim_coeffs(par, cols, rows, False)
        for y in range(Y):
            mine = [own[r * Y + y, rows, :].astype(F32) for r in range(PLANES)]
            other = [near[r * Y + y, rows, :].astype(F32) for r in range(PLANES)]
            for p in range(PLANES):
                out[p * Y + y, rows, :] = weighted(
                    [(tx[RADIUS + r - p], mine[r]) for r in range(PLANES)]
                    + [(tn[q - p], other[q]) for q in range(PLANES)]
                )
        return carry

    lax.fori_loop(0, out.shape[1] // PAIR, one, 0)


def along_far(par, part, far, cols, out):
    def one(group, carry):
        rows = group_rows(group, PAIR)
        tf = rim_coeffs(par, cols, rows, True)
        for y in range(Y):
            other = [far[r * Y + y, rows, :].astype(F32) for r in range(PLANES)]
            for p in range(PLANES):
                out[p * Y + y, rows, :] = weighted(
                    [(tf[q - p], other[q]) for q in range(PLANES)], part[p * Y + y, rows, :]
                )
        return carry

    lax.fori_loop(0, out.shape[1] // PAIR, one, 0)


def across(field, ty, y):
    return weighted([(ty[k], field[y + k - RADIUS]) for k in range(TAPS) if 0 <= y + k - RADIUS < Y])


def across_back(field, ty, y):
    return weighted([(ty[k], field[y - k + RADIUS]) for k in range(TAPS) if 0 <= y - k + RADIUS < Y])


def turns(value, sign):
    low = value.astype(BF16)
    moved = []
    for k in range(TAPS):
        shift = sign * (k - RADIUS) % LANES
        moved.append(pltpu.roll(low, shift, 1).astype(F32) if shift else value)
    return moved


def rest_of_conv(field, cols, crossed, mixed):
    def one(group, carry):
        rows = group_rows(group, PAIR)
        ty = coeffs(cols, rows, T_Y)
        tz = coeffs(cols, rows, T_Z)
        for p in range(PLANES):
            plane = [field[p * Y + y, rows, :] for y in range(Y)]
            for y in range(Y):
                value = across(plane, ty, y)
                crossed[p * Y + y, rows, :] = value
                mixed[p * Y + y, rows, :] = weighted(zip(tz, turns(value, -1)))
        return carry

    lax.fori_loop(0, mixed.shape[1] // PAIR, one, 0, unroll=3)


def convolve_back(dmixed, mxy, cols, cross_out, along, sums):
    lane = lax.broadcasted_iota(jnp.int32, (PAIR, LANES), 1)

    def one(group, carry):
        rows = group_rows(group, PAIR)
        ty = coeffs(cols, rows, T_Y)
        tz = coeffs(cols, rows, T_Z_BACK)
        found = [None] * TAPS
        for p in range(PLANES):
            cross = []
            for y in range(Y):
                spun = turns(dmixed[p * Y + y, rows, :], 1)
                field = mxy[p * Y + y, rows, :]
                for k in range(TAPS):
                    found[k] = weighted([(spun[k], field)], found[k])
                cross.append(weighted(zip(tz, spun)))
                cross_out[p * Y + y, rows, :] = cross[y]
            for y in range(Y):
                along[p * Y + y, rows, :] = across_back(cross, ty, y)
        for k in range(TAPS):
            shift = k - RADIUS
            sums[k, rows, :] = jnp.where((lane - shift >= 0) & (lane - shift < LANES), found[k], 0.0)
        return carry

    lax.fori_loop(0, dmixed.shape[1] // PAIR, one, 0, unroll=6)


def rim(par, along, cols, far, out):
    def one(group, carry):
        rows = group_rows(group, PAIR)
        tt = rim_coeffs(par, cols, rows, far)
        for y in range(Y):
            column = [along[p * Y + y, rows, :] for p in range(PLANES)]
            for q in range(PLANES):
                out[q * Y + y, rows, :] = weighted(
                    [(tt[q - p], column[p]) for p in range(PLANES)]
                ).astype(out.dtype)
        return carry

    lax.fori_loop(0, out.shape[1] // PAIR, one, 0)


def inside(along, cols, base, out):
    def one(group, carry):
        rows = group_rows(group)
        tx = coeffs(cols, rows, T_X)
        for y in range(Y):
            column = [along[p * Y + y, rows, :] for p in range(PLANES)]
            for r in range(PLANES):
                out[r * Y + y, rows, :] = weighted(
                    [(tx[RADIUS + r - p], column[p]) for p in range(PLANES)], base[r * Y + y, rows, :]
                )
        return carry

    lax.fori_loop(0, out.shape[1] // ROWS, one, 0)


def tap_sums(par, own, near, far, mx, cross, along, z_sums, select, sums):
    reach = range(1 - PLANES, PLANES)

    def along_track(group, carry):
        rows = group_rows(group, PAIR)
        found = []
        for source in (own, near, far):
            total = dict.fromkeys(reach)
            for y in range(Y):
                back = [along[p * Y + y, rows, :] for p in range(PLANES)]
                field = [source[q * Y + y, rows, :].astype(F32) for q in range(PLANES)]
                for d in reach:
                    total[d] = weighted(
                        [(back[p], field[p + d]) for p in range(PLANES) if 0 <= p + d < PLANES], total[d]
                    )
            found.append(total)
        mine, close, away = found
        even = par[0] == 0
        low = [jnp.where(even, away[d], close[d]) for d in range(PLANES)]
        high = [jnp.where(even, close[-d], away[-d]) for d in range(PLANES)]
        resolved = [
            low[0], mine[-2] + low[1], mine[-1] + low[2], mine[0], mine[1] + high[2], mine[2] + high[1], high[0]
        ]
        for k in range(TAPS):
            sums[T_X + k, rows, :] = resolved[k]
        return carry

    lax.fori_loop(0, mx.shape[1] // PAIR, along_track, 0, unroll=3)

    def cross_track(group, carry):
        rows = group_rows(group)
        total = [None] * TAPS
        for p in range(PLANES):
            plane = [mx[p * Y + y, rows, :] for y in range(Y)]
            for y in range(Y):
                back = cross[p * Y + y, rows, :]
                for k in range(TAPS):
                    if 0 <= y + k - RADIUS < Y:
                        total[k] = weighted([(back, plane[y + k - RADIUS])], total[k])
        for k in range(TAPS):
            sums[T_Y + k, rows, :] = total[k]
        return carry

    lax.fori_loop(0, mx.shape[1] // ROWS, cross_track, 0, unroll=3)
    terms = [sums[k] for k in range(2 * TAPS)] + [z_sums[k] for k in range(TAPS)]
    wide = jnp.concatenate(terms, axis=1)
    high = wide.astype(BF16)
    rest = (wide - high.astype(F32)).astype(BF16)
    return dot(high, select[...]) + dot(rest, select[...])


def tiles(ref, first):
    return jnp.concatenate([ref[first + i] for i in range(CHUNK)], axis=1)


def put(ref, first, value):
    for i in range(CHUNK):
        ref[first + i] = value[:, i * LANES : (i + 1) * LANES].astype(ref.dtype)


def folded(value):
    total = value[:, :LANES]
    for i in range(1, CHUNK):
        total = total + value[:, i * LANES : (i + 1) * LANES]
    return total


def normalise(mixed):
    scale = 1.0 / mixed.shape[0]
    centred = mixed - jnp.sum(mixed, axis=0, keepdims=True) * scale
    variance = jnp.sum(centred * centred, axis=0, keepdims=True) * scale
    inverse = lax.rsqrt(variance + 1e-06)
    return centred * inverse, inverse


def normalise_back(g_norm, normal, inverse, gain):
    share = 1.0 / g_norm.shape[0]
    g_normal = g_norm * gain
    mean_a = jnp.sum(g_normal, axis=0, keepdims=True) * share
    mean_b = jnp.sum(g_normal * normal, axis=0, keepdims=True) * share
    return inverse * (g_normal - mean_a - normal * mean_b)


def dot(a, b):
    return jnp.dot(a, b, preferred_element_type=F32)


def dot_t(a, b):
    return lax.dot_general(a, b, (((1,), (1,)), ((), ())), preferred_element_type=F32)


def with_ones(normed):
    row = lax.broadcasted_iota(jnp.int32, (PAIR, normed.shape[1]), 0)
    return jnp.concatenate([normed, jnp.where(row == 0, 1.0, 0.0).astype(BF16)], axis=0)


def gelu_parts(hidden):
    square = hidden * hidden
    half = jnp.tanh(hidden * (GELU_A + GELU_B * square))
    rise = 0.5 + 0.5 * half
    act = (hidden * rise).astype(BF16)
    slope = rise + (hidden * (0.5 - 0.5 * (half * half))) * (GELU_A + 3.0 * GELU_B * square)
    return act, slope


def steps():
    return [(step, step * CHUNK) for step in range(OWN // CHUNK)]


def fold_stats(value):
    lane = lax.broadcasted_iota(jnp.int32, (ROWS, LANES), 1)
    parts, blocks = LANES // STAT, []
    for i in range(0, value.shape[0], ROWS):
        block = jnp.where(lane < STAT, value[i : i + ROWS], 0.0)
        shift = i // ROWS % parts * STAT
        blocks.append(pltpu.roll(block, shift, 1) if shift else block)
    sums = []
    for i in range(0, len(blocks), parts):
        total = blocks[i]
        for block in blocks[i + 1 : i + parts]:
            total = total + block
        sums.append(total)
    return jnp.concatenate(sums, axis=1)


def unfold_stats(folded_stats, channels):
    parts, blocks = LANES // STAT, []
    for i in range(channels // ROWS):
        block = folded_stats[:, i // parts * LANES : (i // parts + 1) * LANES]
        shift = (LANES - i % parts * STAT) % LANES
        blocks.append(pltpu.roll(block, shift, 1) if shift else block)
    return jnp.concatenate(blocks, axis=0)


def send_low(low, first, total):
    weights = total.shape[0] - ROWS
    low[first : first + weights] = total[:weights].astype(BF16)
    stats = total[weights:]
    high = stats.astype(BF16).astype(F32)
    low[first + weights : first + weights + PAIR] = jnp.concatenate([high, stats - high], axis=0).astype(BF16)


def take_low(low, first, height):
    weights = height - ROWS
    terms = low[first + weights : first + weights + PAIR].astype(F32)
    return jnp.concatenate(
        [low[first : first + weights].astype(F32), terms[:ROWS] + terms[ROWS:]], axis=0
    )


def pack_kernel(have, got, stats, total, low):
    both = jnp.concatenate([have[...] + got[...], fold_stats(stats[...])], axis=0)
    total[...] = both
    send_low(low, 0, both)


def gathered(have, first, second, third):
    height = have.shape[0]
    return (have[...] + take_low(first, 0, height)) + (take_low(second, 0, height) + take_low(third, 0, height))


def first_kernel(have, got, total, low):
    out = have[...] + got[...]
    total[...] = out
    low[...] = out.astype(BF16)


def spread_two_kernel(have, first, second, third, total):
    total[...] = gathered(have, first, second, third)


def spread_kernel(have, first, second, third, total):
    total[...] = (have[...] + first[...].astype(F32)) + (second[...].astype(F32) + third[...].astype(F32))


def stats_pack_kernel(stats, total, low):
    out = fold_stats(stats[...])
    high = out.astype(BF16).astype(F32)
    total[...] = out
    low[...] = jnp.concatenate([high, out - high], axis=0).astype(BF16)


def spread_one_kernel(one, stats, first, second, third, two, total, low):
    terms = [ref[...].astype(F32) for ref in (first, second, third)]
    first, second, third = (term[:ROWS] + term[ROWS:] for term in terms)
    out = jnp.concatenate([one[...], (stats[...] + first) + (second + third)], axis=0)
    height = out.shape[0]
    total[:height] = out
    total[height:] = two[...]
    send_low(low, 0, out)
    send_low(low, height + ROWS, two[...])


def joined_kernel(have, got, total):
    height = have.shape[0] // 2
    total[:height] = have[:height] + take_low(got, 0, height)
    total[height:] = have[height:] + take_low(got, height + ROWS, height)


def start_kernel(par, vol, near, tables, part, own, other, wide):
    unpack(vol, wide, own)
    unpack(near, wide, other)
    along_own(par, own, other, tables.at[0], part)


def forward_kernel(
    par, far, part, own_tiles, cols, tables, w_in, b_in, w_out, out, mixed, other, field, crossed, wide
):
    unpack(far, wide, other)
    along_far(par, part, other, tables.at[0], field)
    rest_of_conv(field, tables.at[0], crossed, mixed)
    gain, scale = cols[0, :, GAIN : GAIN + 1], cols[0, :, SCALE : SCALE + 1]
    for step, first in steps():
        normal, inverse = normalise(tiles(mixed, first))
        normed = (normal * gain).astype(BF16)
        hidden = dot(w_in[0], normed) + b_in[:, 0:1]
        half = jnp.tanh(hidden * (GELU_A + GELU_B * (hidden * hidden)))
        act = (hidden * (0.5 + 0.5 * half)).astype(BF16)
        put(out, first, tiles(own_tiles, first) + scale * dot(w_out[0], act))


def save_kernel(mixed, cols, w_in, b_in, normed, normal, inverse, act, slope):
    for step, first in steps():
        value, inverse[step] = normalise(tiles(mixed, first))
        put(normal, first, value)
        low = (value * cols[0, :, GAIN : GAIN + 1]).astype(BF16)
        put(normed, first, low)
        act[step], slope[step] = gelu_parts(dot(w_in[0], low) + b_in[:, 0:1])


def middle_kernel(par, mid, near, tables, part):
    along_own(par, mid, near, tables.at[1], part)


def turn_kernel(
    par, far, part, mid, labels, cols, tables, w_in, w_in_t, b_in, w_out, w_out_t, head, head_t,
    head_b, rim_far, field, z_sums, cross, along, dmixed, base, keep, send, acc_gain, acc_scale, head_cols, head_bias,
    mixed, crossed, sums,
):
    channels = mid.shape[1]
    taps = tables.at[1]
    along_far(par, part, far, taps, field)
    rest_of_conv(field, taps, crossed, mixed)
    sums[...] = jnp.zeros_like(sums)
    acc_gain[...] = jnp.zeros_like(acc_gain)
    acc_scale[...] = jnp.zeros_like(acc_scale)
    head_cols[...] = jnp.zeros_like(head_cols)
    head_bias[...] = jnp.zeros_like(head_bias)
    gain, scale = cols[1, :, GAIN : GAIN + 1], cols[1, :, SCALE : SCALE + 1]
    for step, first in steps():
        normal, inverse = normalise(tiles(mixed, first))
        normed = (normal * gain).astype(BF16)
        act, slope = gelu_parts(dot(w_in[1], normed) + b_in[:, 1:2])
        lifted = dot(w_out[1], act)
        final = (tiles(mid, first).astype(F32) + scale * lifted).astype(BF16)
        logits = dot(head[...], final) + head_b[...]
        raised = jnp.exp(logits - jnp.max(logits, axis=0, keepdims=True))
        probability = raised / jnp.sum(raised, axis=0, keepdims=True)
        classes = lax.broadcasted_iota(jnp.int32, logits.shape, 0)
        g_logits = probability - (labels[step] == classes).astype(F32)
        head_bias[...] += folded(g_logits)
        g_low = g_logits.astype(BF16)
        head_cols[...] += dot_t(final, g_low)
        grad = dot(head_t[...], g_low)
        acc_scale[...] += folded(grad * lifted)
        put(base, first, grad)
        g_lift = (grad * scale).astype(BF16)
        sums[0, :channels] += dot_t(g_lift, act)
        g_hid = (dot(w_out_t[1], g_lift) * slope).astype(BF16)
        sums[1] += dot_t(with_ones(normed), g_hid)
        g_norm = dot(w_in_t[1], g_hid)
        acc_gain[...] += folded(g_norm * normal)
        put(dmixed, first, normalise_back(g_norm, normal, inverse, gain))
    convolve_back(dmixed, crossed, taps, cross, along, z_sums)
    rim(par, along, taps, True, rim_far)
    keep[...] = sums[par[0]]
    send[...] = sums[1 - par[0]]


def total_of(ref):
    return jnp.sum(ref[...], axis=1, keepdims=True)


def taps_two_kernel(
    par, own, near, far, mx, cross, along, z_sums, select, base, tables, acc_gain, acc_scale, head_cols,
    head_bias, out, inner, rim_near, sums,
):
    rim(par, along, tables.at[1], False, rim_near)
    inside(along, tables.at[1], base, inner)
    value = tap_sums(par, own, near, far, mx, cross, along, z_sums, select, sums)
    lane = lax.broadcasted_iota(jnp.int32, out.shape, 1)
    value = jnp.where(lane == GAIN, total_of(acc_gain), value)
    value = jnp.where(lane == SCALE, total_of(acc_scale), value)
    for k in range(ROWS):
        value = jnp.where(lane == HEAD + k, head_cols[:, k : k + 1], value)
    out[...] = value
    out[:ROWS] = jnp.where(lane[:ROWS] == HEAD_BIAS, total_of(head_bias), out[:ROWS])


def taps_one_kernel(
    par, own, near, far, mx, cross, along, z_sums, select, acc_gain, gs_scale, out, sums
):
    value = tap_sums(par, own, near, far, mx, cross, along, z_sums, select, sums)
    lane = lax.broadcasted_iota(jnp.int32, out.shape, 1)
    value = jnp.where(lane == GAIN, total_of(acc_gain), value)
    out[...] = jnp.where(lane == SCALE, gs_scale[...], value)


def inside_kernel(par, along, base, tables, inner, rim_near):
    rim(par, along, tables.at[0], False, rim_near)
    inside(along, tables.at[0], base, inner)


def point_back_kernel(
    par, inner, near, far, act, slope, normed, cols, w_in_t, w_out, w_out_t,
    base, g_norm, keep, send, gs_scale, sums,
):
    channels = inner.shape[1]
    sums[...] = jnp.zeros_like(sums)
    scale = cols[0, :, SCALE : SCALE + 1]
    for step, first in steps():
        grad = tiles(inner, first) + (tiles(near, first).astype(F32) + tiles(far, first).astype(F32))
        put(base, first, grad)
        g_lift = (grad * scale).astype(BF16)
        sums[0, :channels] += dot_t(g_lift, act[step])
        g_hid = (dot(w_out_t[0], g_lift) * slope[step]).astype(BF16)
        sums[1] += dot_t(with_ones(tiles(normed, first)), g_hid)
        put(g_norm, first, dot(w_in_t[0], g_hid))
    spread = jnp.sum(sums[0, :channels] * w_out[0].astype(F32), axis=1, keepdims=True)
    gs_scale[...] = spread / scale
    keep[...] = sums[par[0]]
    send[...] = sums[1 - par[0]]


def conv_back_kernel(
    par, g_norm, normal, inverse, mxy, cols, tables, rim_far, z_sums, cross, along, acc_gain,
    dmixed,
):
    taps = tables.at[0]
    acc_gain[...] = jnp.zeros_like(acc_gain)
    for step, first in steps():
        value, unit = tiles(g_norm, first), tiles(normal, first)
        acc_gain[...] += folded(value * unit)
        put(dmixed, first, normalise_back(value, unit, inverse[step], cols[0, :, GAIN : GAIN + 1]))
    convolve_back(dmixed, mxy, taps, cross, along, z_sums)
    rim(par, along, taps, True, rim_far)


def last_kernel(inner, near, far, out, token, total):
    token[...] = jnp.zeros_like(token)

    def add(tile, carry):
        total[tile] = inner[tile] + (near[tile].astype(F32) + far[tile].astype(F32))
        return carry

    lax.fori_loop(0, OWN, add, 0, unroll=2)

    def one(group, carry):
        rows = group_rows(group)
        for tile in range(OWN):
            out[pl.ds(group * ROWS * OWN + tile, ROWS, stride=OWN), :] = total[tile, rows, :]
        return carry

    lax.fori_loop(0, inner.shape[1] // ROWS, one, 0)


def final_kernel(share, par, mine, other, g_in_t, g_bias, g_out, g_taps, g_gain, g_scale, g_head, g_head_b):
    channels = g_out.shape[1]
    even = par[0] == 0
    height = mine.shape[0] // 2
    weights = height - ROWS
    for s in range(2):
        here, stop = s * height, s * height + weights
        first = jnp.where(even, mine[here:stop], other[here:stop]) * share
        second = jnp.where(even, other[here:stop], mine[here:stop]) * share
        g_out[s] = first[:channels]
        g_in_t[s] = second[:channels]
        g_bias[s : s + 1] = second[channels : channels + 1]
        stats = mine[stop : stop + ROWS] + other[stop : stop + ROWS]
        rows = unfold_stats(stats, channels).T * share
        for axis in range(3):
            for k in range(TAPS):
                g_taps[axis, k, s : s + 1] = rows[axis * TAPS + k : axis * TAPS + k + 1]
        g_gain[s : s + 1] = rows[GAIN : GAIN + 1]
        g_scale[s : s + 1] = rows[SCALE : SCALE + 1]
    g_head[...] = rows[HEAD : HEAD + g_head.shape[0]]
    g_head_b[...] = rows[HEAD_BIAS : HEAD_BIAS + 1, : g_head_b.shape[1]]


def call(kernel, name, operands, outs, scratch=(), room=8, after=(), flops=0):
    smem = pl.BlockSpec(memory_space=pltpu.SMEM)
    vmem = pl.BlockSpec(memory_space=pltpu.VMEM)
    anywhere = pl.BlockSpec(memory_space=pl.ANY)
    count = len(operands)

    def run(*refs):
        kernel(*refs[:count], *refs[count + len(after) :])

    in_specs = [smem if x.dtype == jnp.int32 and x.shape == (1,) else vmem for x in operands]
    return pl.pallas_call(
        run,
        name=name,
        out_shape=tuple(outs),
        in_specs=in_specs + [anywhere] * len(after),
        out_specs=tuple([vmem] * len(outs)),
        scratch_shapes=list(scratch),
        compiler_params=pltpu.CompilerParams(vmem_limit_bytes=room * MIB),
        cost_estimate=pl.CostEstimate(flops=flops, bytes_accessed=0, transcendentals=0),
    )(*operands, *after)


def pinned(dims, dtype=F32):
    return pltpu.VMEM(dims, dtype)


def shape(dims, dtype=F32):
    return jax.ShapeDtypeStruct(dims, dtype)


def near_swap(value):
    count = lax.axis_size("track")
    return lax.ppermute(value, "track", [(i, i ^ 1) for i in range(count)])


def far_swap(value):
    count = lax.axis_size("track")
    pairs = []
    for i in range(1, count - 1, 2):
        pairs += [(i, i + 1), (i + 1, i)]
    return lax.ppermute(value, "track", pairs)


def bit_swap(value, step):
    count = lax.axis_size("track")
    return lax.ppermute(value, "track", [(i, i ^ step) for i in range(count)])


def on_device(
    volume, labels, conv_taps, norm_gain, weight_in, bias_in, weight_out, layer_scale, head_weight, head_bias
):
    channels, planes, rows, depth = volume.shape
    hidden = weight_in.shape[1]
    classes = head_weight.shape[0]
    devices = lax.axis_size("track")
    share = 1.0 / float(devices * planes * rows * depth)
    par = (lax.axis_index("track") % 2).astype(jnp.int32).reshape(1)
    parts = OWN // CHUNK

    flat = volume.reshape(channels * OWN, depth)
    near = near_swap(flat)
    far = far_swap(flat)
    cols = jnp.swapaxes(
        jnp.concatenate(
            [conv_taps.reshape(2, 3 * TAPS, channels), norm_gain[:, None], layer_scale[:, None]], axis=1
        ), 1, 2,
    )
    b_in = bias_in.T
    head = jnp.zeros((ROWS, channels), BF16).at[:classes].set(head_weight)
    head_b = jnp.full((ROWS,), -1e30, F32).at[:classes].set(head_bias)[:, None]
    flat_labels = labels.reshape(parts, 1, CHUNK * depth)

    low = shape((OWN, channels, depth), BF16)
    full = shape((OWN, channels, depth))
    half = shape((channels + PAIR, hidden))
    s_full = pltpu.VMEM((OWN, channels, depth), F32)
    s_wide = pltpu.VMEM((channels * OWN, depth), F32)
    s_sums = pltpu.VMEM((2, channels + PAIR, hidden), F32)
    k_full = pinned((OWN, channels, depth))
    k_half = pinned((channels + PAIR, hidden))
    k_stat = pinned((channels, LANES))

    small = (cols, b_in, weight_in, weight_out, head, head_b, flat_labels)
    (tables, cols, b_in, w_in, w_in_t, w_out, w_out_t, head, head_t, head_b, flat_labels, select) = call(
        tables_kernel, "tables", small,
        [pinned((2, 4 * TAPS, channels, LANES)), pinned(cols.shape), pinned(b_in.shape),
         pinned(weight_in.shape, BF16), pinned(weight_out.shape, BF16), pinned(weight_out.shape, BF16),
         pinned(weight_in.shape, BF16), pinned(head.shape, BF16), pinned((channels, ROWS), BF16),
         pinned(head_b.shape), pinned(flat_labels.shape, jnp.int32),
         pinned((3 * TAPS * LANES, LANES), BF16)],
    )
    part, own_kept, near_kept = call(
        start_kernel, "start_one", (par, flat, near, tables), [k_full, k_full, k_full], [s_wide],
    )
    mid, mixed_one, far_kept, mx_one, mxy_one = call(
        forward_kernel, "forward_one", (par, far, part, own_kept, cols, tables, w_in, b_in, w_out),
        [low, k_full, k_full, k_full, k_full], [s_wide], 8,
    )
    near = near_swap(mid)
    far = far_swap(mid)
    normed, normal, inverse, act, slope = call(
        save_kernel, "save_one", (mixed_one, cols, w_in, b_in),
        [pinned((OWN, channels, depth), BF16), k_full, pinned((parts, 1, CHUNK * depth)),
         pinned((parts, hidden, CHUNK * depth), BF16), pinned((parts, hidden, CHUNK * depth))],
        (), 16,
    )
    (part,) = call(
        middle_kernel, "start_two", (par, mid, near, tables), [k_full], (), 4, after=(inverse,)
    )
    k_taps = pinned((TAPS, channels, LANES))
    s_taps = pltpu.VMEM((2 * TAPS, channels, LANES), F32)
    (rim_far, mx, z_sums, cross, along, dmixed, base, keep, send,
     acc_gain, acc_scale, head_cols, head_lanes) = call(
        turn_kernel, "turn_two",
        (par, far, part, mid, flat_labels, cols, tables, w_in, w_in_t, b_in, w_out, w_out_t,
         head, head_t, head_b),
        [low, k_full, k_taps, k_full, k_full, k_full, k_full, k_half, half, k_stat, k_stat, pinned((channels, ROWS)),
         pinned((ROWS, LANES))],
        [s_full, s_full, s_sums], 24,
    )
    rim_far = far_swap(rim_far)
    got = near_swap(send)
    stats, inner, rim_near = call(
        taps_two_kernel, "taps_two",
        (par, mid, near, far, mx, cross, along, z_sums, select, base, tables, acc_gain, acc_scale, head_cols,
         head_lanes),
        [k_stat, k_full, low], [s_taps], 8, after=(got,),
    )
    rim_near = near_swap(rim_near)
    tall = shape((channels + PAIR + ROWS, hidden))
    k_tall = pinned(tall.shape)
    tall_low = shape((channels + 2 * PAIR, hidden), BF16)
    two, two_low = call(
        pack_kernel, "pack_two", (keep, got, stats), [k_tall, tall_low], (), 4, after=(inner,)
    )
    got = [bit_swap(two_low, step) for step in (4, 8, 12)]
    base, g_norm, keep, send, gs_scale = call(
        point_back_kernel, "point_back_one",
        (par, inner, rim_near, rim_far, act, slope, normed, cols, w_in_t, w_out, w_out_t),
        [k_full, k_full, k_half, half, pinned((channels, 1))], [s_sums], 8,
    )
    got_two, got = got, near_swap(send)
    rim_far, z_sums, cross, along, acc_gain = call(
        conv_back_kernel, "conv_back_one", (par, g_norm, normal, inverse, mxy_one, cols, tables),
        [low, k_taps, k_full, k_full, k_stat], [s_full], 8,
    )
    rim_far = far_swap(rim_far)
    half_low = shape((channels + PAIR, hidden), BF16)
    (two,) = call(
        spread_two_kernel, "sums_two", (two, *got_two), [k_tall], (), 4, after=(along,), flops=4 * 10**10
    )
    one, one_low = call(first_kernel, "sums_one_a", (keep, got), [k_half, half_low], (), 4, after=(two,))
    got = [bit_swap(one_low, step) for step in (4, 8, 12)]
    (stats,) = call(
        taps_one_kernel, "taps_one",
        (par, own_kept, near_kept, far_kept, mx_one, cross, along, z_sums, select, acc_gain, gs_scale),
        [k_stat], [s_taps], 8, after=(two,),
    )
    (one,) = call(spread_kernel, "sums_one_b", (one, *got), [k_half], (), 4, after=(stats,), flops=4 * 10**9)
    stats, stats_low = call(
        stats_pack_kernel, "pack_stats", (stats,), [pinned((ROWS, hidden)), shape((PAIR, hidden), BF16)], (), 4
    )
    got_stats = [bit_swap(stats_low, step) for step in (4, 8, 12)]
    inner, rim_near = call(
        inside_kernel, "inside_one", (par, along, base, tables), [k_full, low], (), 4
    )
    rim_near = near_swap(rim_near)
    both_shape = (2 * tall.shape[0], hidden)
    both, both_low = call(
        spread_one_kernel, "sums_one", (one, stats, *got_stats, two),
        [pinned(both_shape), shape((2 * tall_low.shape[0], hidden), BF16)], (), 4, after=(inner,),
    )
    got = bit_swap(both_low, 2)
    grad, token = call(
        last_kernel, "last", (inner, rim_near, rim_far),
        [shape((channels * OWN, depth)), pinned((ROWS, LANES))], [s_full], 4,
        after=(both,),
    )
    (both,) = call(joined_kernel, "sums_last", (both, got), [shape(both_shape)], (), 4, after=(token,))
    step = 16
    while step < devices:
        both = both + bit_swap(both, step)
        step *= 2
    g_in_t, g_bias, g_out, g_taps, g_gain, g_scale, g_head, g_head_b = call(
        functools.partial(final_kernel, share), "final", (par, both, near_swap(both)),
        [shape((2, channels, hidden)), shape((2, hidden)), shape((2, channels, hidden)),
         shape((3, TAPS, 2, channels)), shape((2, channels)), shape((2, channels)),
         shape((classes, channels)), shape((1, classes))],
    )
    return (
        grad.reshape(volume.shape), jnp.moveaxis(g_taps, 2, 0), g_gain, jnp.swapaxes(g_in_t, 1, 2), g_bias, g_out, g_scale,
        g_head, g_head_b.reshape(classes),
    )


def solution(mesh):
    placed = (
        P(None, ("groups", "track"), None, None),
        P(("groups", "track"), None, None),
        P(), P(), P(), P(), P(), P(), P(), P(),
    )
    return jax.shard_map(
        on_device,
        mesh=mesh,
        in_specs=placed,
        out_specs=(
            P(None, ("groups", "track"), None, None),
            P("groups", None, None, None),
            P("groups", None),
            P("groups", None, None),
            P("groups", None),
            P("groups", None, None),
            P("groups", None),
            P("groups", None),
            P("groups"),
        ),
        check_vma=False,
    )
```

```python
import functools

import jax
import jax.numpy as jnp
from jax import lax
from jax.experimental import pallas as pl
from jax.experimental.pallas import tpu as pltpu
from jax.sharding import PartitionSpec as P

F32 = jnp.float32
BF16 = jnp.bfloat16
LANES = 128
ROWS = 8
PAIR = 16
RADIUS = 3
TAPS = 7
PLANES = 3
Y = 8
OWN = PLANES * Y
EXT = (PLANES + 2 * RADIUS) * Y
CHUNK = 12
GELU_A = 0.7978845608028654
GELU_B = 0.044715 * GELU_A
STAT = 32
MIB = 1024 * 1024


T_X, T_Y, T_Z, T_Z_BACK = 0, 7, 14, 21
GAIN, SCALE, HEAD_BIAS, HEAD = 21, 22, 23, 24


def group_rows(index, size=ROWS):
    return pl.ds(pl.multiple_of(index * size, size), size)


def coeffs(source, rows, first, count=TAPS):
    if len(source.shape) == 3:
        return [source[k, rows, :] for k in range(first, first + count)]
    found = []
    for k in range(first, first + count):
        column = source[rows, k : k + 1]
        found.append(jnp.broadcast_to(column, (column.shape[0], LANES)))
    return found


def tables_kernel(
    cols, b_in, w_in, w_out, head, head_b, labels,
    tables, cols_out, b_out, w_in_out, w_in_t, w_out_out, w_out_t, head_out, head_t, head_b_out, labels_out,
    select,
):
    def one(group, carry):
        rows = group_rows(group)
        lane = lax.broadcasted_iota(jnp.int32, (ROWS, LANES), 1)
        for s in range(2):
            for k, value in enumerate(coeffs(cols.at[s], rows, T_X, 2 * TAPS)):
                tables[s, k, rows, :] = value
            for k, value in enumerate(coeffs(cols.at[s], rows, T_Z)):
                for first, reach in ((T_Z, k - RADIUS), (T_Z_BACK, RADIUS - k)):
                    kept = (lane + reach >= 0) & (lane + reach < LANES)
                    tables[s, first + k, rows, :] = jnp.where(kept, value, 0.0)
        return carry

    lax.fori_loop(0, tables.shape[2] // ROWS, one, 0)
    lane = lax.broadcasted_iota(jnp.int32, (LANES, LANES), 1)
    for k in range(3 * TAPS):
        select[k * LANES : (k + 1) * LANES] = jnp.where(lane == k, 1.0, 0.0).astype(BF16)
    for s in range(2):
        w_in_t[s] = w_in[s].T
        w_out_t[s] = w_out[s].T
    head_t[...] = head[...].astype(F32).T.astype(BF16)
    for source, out in (
        (cols, cols_out), (b_in, b_out), (w_in, w_in_out), (w_out, w_out_out), (head, head_out),
        (head_b, head_b_out), (labels, labels_out),
    ):
        out[...] = source[...]


def rim_coeffs(par, cols, rows, low_if_even):
    tx = coeffs(cols, rows, T_X)
    zero = jnp.zeros_like(tx[0])
    low = (par[0] == 0) == low_if_even
    found = {}
    for d in range(1 - PLANES, PLANES):
        found[d] = jnp.where(low, tx[d] if d >= 0 else zero, tx[2 * RADIUS + d] if d <= 0 else zero)
    return found


def unpack(source, wide, out):
    wide[...] = source[...].astype(F32)
    for first in range(0, out.shape[1], ROWS):
        for tile in range(OWN):
            out[tile, first : first + ROWS, :] = wide[pl.ds(first * OWN + tile, ROWS, stride=OWN), :]


def widen(source, ext, first, count):
    def one(tile, carry):
        ext[first + tile] = source[tile].astype(F32)
        return carry

    lax.fori_loop(0, count, one, 0, unroll=4)


def weighted(terms, total=None):
    for coeff, value in terms:
        product = coeff * value
        total = product if total is None else total + product
    return total


def along_own(par, own, near, cols, out):
    def one(group, carry):
        rows = group_rows(group, PAIR)
        tx = coeffs(cols, rows, T_X)
        tn = rim_coeffs(par, cols, rows, False)
        for y in range(Y):
            mine = [own[r * Y + y, rows, :].astype(F32) for r in range(PLANES)]
            other = [near[r * Y + y, rows, :].astype(F32) for r in range(PLANES)]
            for p in range(PLANES):
                out[p * Y + y, rows, :] = weighted(
                    [(tx[RADIUS + r - p], mine[r]) for r in range(PLANES)]
                    + [(tn[q - p], other[q]) for q in range(PLANES)]
                )
        return carry

    lax.fori_loop(0, out.shape[1] // PAIR, one, 0)


def along_far(par, part, far, cols, out):
    def one(group, carry):
        rows = group_rows(group, PAIR)
        tf = rim_coeffs(par, cols, rows, True)
        for y in range(Y):
            other = [far[r * Y + y, rows, :].astype(F32) for r in range(PLANES)]
            for p in range(PLANES):
                out[p * Y + y, rows, :] = weighted(
                    [(tf[q - p], other[q]) for q in range(PLANES)], part[p * Y + y, rows, :]
                )
        return carry

    lax.fori_loop(0, out.shape[1] // PAIR, one, 0)


def across(field, ty, y):
    return weighted([(ty[k], field[y + k - RADIUS]) for k in range(TAPS) if 0 <= y + k - RADIUS < Y])


def across_back(field, ty, y):
    return weighted([(ty[k], field[y - k + RADIUS]) for k in range(TAPS) if 0 <= y - k + RADIUS < Y])


def turns(value, sign):
    low = value.astype(BF16)
    moved = []
    for k in range(TAPS):
        shift = sign * (k - RADIUS) % LANES
        moved.append(pltpu.roll(low, shift, 1).astype(F32) if shift else value)
    return moved


def rest_of_conv(field, cols, crossed, mixed):
    def one(group, carry):
        rows = group_rows(group, PAIR)
        ty = coeffs(cols, rows, T_Y)
        tz = coeffs(cols, rows, T_Z)
        for p in range(PLANES):
            plane = [field[p * Y + y, rows, :] for y in range(Y)]
            for y in range(Y):
                value = across(plane, ty, y)
                crossed[p * Y + y, rows, :] = value
                mixed[p * Y + y, rows, :] = weighted(zip(tz, turns(value, -1)))
        return carry

    lax.fori_loop(0, mixed.shape[1] // PAIR, one, 0, unroll=3)


def convolve_back(dmixed, mxy, cols, cross_out, along, sums):
    lane = lax.broadcasted_iota(jnp.int32, (PAIR, LANES), 1)

    def one(group, carry):
        rows = group_rows(group, PAIR)
        ty = coeffs(cols, rows, T_Y)
        tz = coeffs(cols, rows, T_Z_BACK)
        found = [None] * TAPS
        for p in range(PLANES):
            cross = []
            for y in range(Y):
                spun = turns(dmixed[p * Y + y, rows, :], 1)
                field = mxy[p * Y + y, rows, :]
                for k in range(TAPS):
                    found[k] = weighted([(spun[k], field)], found[k])
                cross.append(weighted(zip(tz, spun)))
                cross_out[p * Y + y, rows, :] = cross[y]
            for y in range(Y):
                along[p * Y + y, rows, :] = across_back(cross, ty, y)
        for k in range(TAPS):
            shift = k - RADIUS
            sums[k, rows, :] = jnp.where((lane - shift >= 0) & (lane - shift < LANES), found[k], 0.0)
        return carry

    lax.fori_loop(0, dmixed.shape[1] // PAIR, one, 0, unroll=6)


def rim(par, along, cols, far, out):
    def one(group, carry):
        rows = group_rows(group, PAIR)
        tt = rim_coeffs(par, cols, rows, far)
        for y in range(Y):
            column = [along[p * Y + y, rows, :] for p in range(PLANES)]
            for q in range(PLANES):
                out[q * Y + y, rows, :] = weighted(
                    [(tt[q - p], column[p]) for p in range(PLANES)]
                ).astype(out.dtype)
        return carry

    lax.fori_loop(0, out.shape[1] // PAIR, one, 0)


def inside(along, cols, base, out):
    def one(group, carry):
        rows = group_rows(group)
        tx = coeffs(cols, rows, T_X)
        for y in range(Y):
            column = [along[p * Y + y, rows, :] for p in range(PLANES)]
            for r in range(PLANES):
                out[r * Y + y, rows, :] = weighted(
                    [(tx[RADIUS + r - p], column[p]) for p in range(PLANES)], base[r * Y + y, rows, :]
                )
        return carry

    lax.fori_loop(0, out.shape[1] // ROWS, one, 0)


def tap_sums(par, own, near, far, mx, cross, along, z_sums, select, sums):
    reach = range(1 - PLANES, PLANES)

    def along_track(group, carry):
        rows = group_rows(group, PAIR)
        found = []
        for source in (own, near, far):
            total = dict.fromkeys(reach)
            for y in range(Y):
                back = [along[p * Y + y, rows, :] for p in range(PLANES)]
                field = [source[q * Y + y, rows, :].astype(F32) for q in range(PLANES)]
                for d in reach:
                    total[d] = weighted(
                        [(back[p], field[p + d]) for p in range(PLANES) if 0 <= p + d < PLANES], total[d]
                    )
            found.append(total)
        mine, close, away = found
        even = par[0] == 0
        low = [jnp.where(even, away[d], close[d]) for d in range(PLANES)]
        high = [jnp.where(even, close[-d], away[-d]) for d in range(PLANES)]
        resolved = [
            low[0], mine[-2] + low[1], mine[-1] + low[2], mine[0], mine[1] + high[2], mine[2] + high[1], high[0]
        ]
        for k in range(TAPS):
            sums[T_X + k, rows, :] = resolved[k]
        return carry

    lax.fori_loop(0, mx.shape[1] // PAIR, along_track, 0, unroll=3)

    def cross_track(group, carry):
        rows = group_rows(group)
        total = [None] * TAPS
        for p in range(PLANES):
            plane = [mx[p * Y + y, rows, :] for y in range(Y)]
            for y in range(Y):
                back = cross[p * Y + y, rows, :]
                for k in range(TAPS):
                    if 0 <= y + k - RADIUS < Y:
                        total[k] = weighted([(back, plane[y + k - RADIUS])], total[k])
        for k in range(TAPS):
            sums[T_Y + k, rows, :] = total[k]
        return carry

    lax.fori_loop(0, mx.shape[1] // ROWS, cross_track, 0, unroll=3)
    terms = [sums[k] for k in range(2 * TAPS)] + [z_sums[k] for k in range(TAPS)]
    wide = jnp.concatenate(terms, axis=1)
    high = wide.astype(BF16)
    rest = (wide - high.astype(F32)).astype(BF16)
    return dot(high, select[...]) + dot(rest, select[...])


def tiles(ref, first):
    return jnp.concatenate([ref[first + i] for i in range(CHUNK)], axis=1)


def put(ref, first, value):
    for i in range(CHUNK):
        ref[first + i] = value[:, i * LANES : (i + 1) * LANES].astype(ref.dtype)


def folded(value):
    total = value[:, :LANES]
    for i in range(1, CHUNK):
        total = total + value[:, i * LANES : (i + 1) * LANES]
    return total


def normalise(mixed):
    scale = 1.0 / mixed.shape[0]
    centred = mixed - jnp.sum(mixed, axis=0, keepdims=True) * scale
    variance = jnp.sum(centred * centred, axis=0, keepdims=True) * scale
    inverse = lax.rsqrt(variance + 1e-06)
    return centred * inverse, inverse


def normalise_back(g_norm, normal, inverse, gain):
    share = 1.0 / g_norm.shape[0]
    g_normal = g_norm * gain
    mean_a = jnp.sum(g_normal, axis=0, keepdims=True) * share
    mean_b = jnp.sum(g_normal * normal, axis=0, keepdims=True) * share
    return inverse * (g_normal - mean_a - normal * mean_b)


def dot(a, b):
    return jnp.dot(a, b, preferred_element_type=F32)


def dot_t(a, b):
    return lax.dot_general(a, b, (((1,), (1,)), ((), ())), preferred_element_type=F32)


def with_ones(normed):
    row = lax.broadcasted_iota(jnp.int32, (PAIR, normed.shape[1]), 0)
    return jnp.concatenate([normed, jnp.where(row == 0, 1.0, 0.0).astype(BF16)], axis=0)


def gelu_parts(hidden):
    square = hidden * hidden
    half = jnp.tanh(hidden * (GELU_A + GELU_B * square))
    rise = 0.5 + 0.5 * half
    act = (hidden * rise).astype(BF16)
    slope = rise + (hidden * (0.5 - 0.5 * (half * half))) * (GELU_A + 3.0 * GELU_B * square)
    return act, slope


def steps():
    return [(step, step * CHUNK) for step in range(OWN // CHUNK)]


def fold_stats(value):
    lane = lax.broadcasted_iota(jnp.int32, (ROWS, LANES), 1)
    parts, blocks = LANES // STAT, []
    for i in range(0, value.shape[0], ROWS):
        block = jnp.where(lane < STAT, value[i : i + ROWS], 0.0)
        shift = i // ROWS % parts * STAT
        blocks.append(pltpu.roll(block, shift, 1) if shift else block)
    sums = []
    for i in range(0, len(blocks), parts):
        total = blocks[i]
        for block in blocks[i + 1 : i + parts]:
            total = total + block
        sums.append(total)
    return jnp.concatenate(sums, axis=1)


def unfold_stats(folded_stats, channels):
    parts, blocks = LANES // STAT, []
    for i in range(channels // ROWS):
        block = folded_stats[:, i // parts * LANES : (i // parts + 1) * LANES]
        shift = (LANES - i % parts * STAT) % LANES
        blocks.append(pltpu.roll(block, shift, 1) if shift else block)
    return jnp.concatenate(blocks, axis=0)


def send_low(low, first, total):
    weights = total.shape[0] - ROWS
    low[first : first + weights] = total[:weights].astype(BF16)
    stats = total[weights:]
    high = stats.astype(BF16).astype(F32)
    low[first + weights : first + weights + PAIR] = jnp.concatenate([high, stats - high], axis=0).astype(BF16)


def take_low(low, first, height):
    weights = height - ROWS
    terms = low[first + weights : first + weights + PAIR].astype(F32)
    return jnp.concatenate(
        [low[first : first + weights].astype(F32), terms[:ROWS] + terms[ROWS:]], axis=0
    )


def pack_kernel(have, got, stats, total, low):
    both = jnp.concatenate([have[...] + got[...], fold_stats(stats[...])], axis=0)
    total[...] = both
    send_low(low, 0, both)


def gathered(have, first, second, third):
    height = have.shape[0]
    return (have[...] + take_low(first, 0, height)) + (take_low(second, 0, height) + take_low(third, 0, height))


def first_kernel(have, got, total, low):
    out = have[...] + got[...]
    total[...] = out
    low[...] = out.astype(BF16)


def spread_two_kernel(have, first, second, third, total):
    total[...] = gathered(have, first, second, third)


def spread_kernel(have, first, second, third, total):
    total[...] = (have[...] + first[...].astype(F32)) + (second[...].astype(F32) + third[...].astype(F32))


def stats_pack_kernel(stats, total, low):
    out = fold_stats(stats[...])
    high = out.astype(BF16).astype(F32)
    total[...] = out
    low[...] = jnp.concatenate([high, out - high], axis=0).astype(BF16)


def spread_one_kernel(one, stats, first, second, third, two, total, low):
    terms = [ref[...].astype(F32) for ref in (first, second, third)]
    first, second, third = (term[:ROWS] + term[ROWS:] for term in terms)
    out = jnp.concatenate([one[...], (stats[...] + first) + (second + third)], axis=0)
    height = out.shape[0]
    total[:height] = out
    total[height:] = two[...]
    send_low(low, 0, out)
    send_low(low, height + ROWS, two[...])


def joined_kernel(have, got, total):
    height = have.shape[0] // 2
    total[:height] = have[:height] + take_low(got, 0, height)
    total[height:] = have[height:] + take_low(got, height + ROWS, height)


def start_kernel(par, vol, near, tables, part, own, other, wide):
    unpack(vol, wide, own)
    unpack(near, wide, other)
    along_own(par, own, other, tables.at[0], part)


def forward_kernel(
    par, far, part, own_tiles, cols, tables, w_in, b_in, w_out, out, mixed, other, field, crossed, wide
):
    unpack(far, wide, other)
    along_far(par, part, other, tables.at[0], field)
    rest_of_conv(field, tables.at[0], crossed, mixed)
    gain, scale = cols[0, :, GAIN : GAIN + 1], cols[0, :, SCALE : SCALE + 1]
    for step, first in steps():
        normal, inverse = normalise(tiles(mixed, first))
        normed = (normal * gain).astype(BF16)
        hidden = dot(w_in[0], normed) + b_in[:, 0:1]
        half = jnp.tanh(hidden * (GELU_A + GELU_B * (hidden * hidden)))
        act = (hidden * (0.5 + 0.5 * half)).astype(BF16)
        put(out, first, tiles(own_tiles, first) + scale * dot(w_out[0], act))


def save_kernel(mixed, cols, w_in, b_in, normed, normal, inverse, act, slope):
    for step, first in steps():
        value, inverse[step] = normalise(tiles(mixed, first))
        put(normal, first, value)
        low = (value * cols[0, :, GAIN : GAIN + 1]).astype(BF16)
        put(normed, first, low)
        act[step], slope[step] = gelu_parts(dot(w_in[0], low) + b_in[:, 0:1])


def middle_kernel(par, mid, near, tables, part):
    along_own(par, mid, near, tables.at[1], part)


def turn_kernel(
    par, far, part, mid, labels, cols, tables, w_in, w_in_t, b_in, w_out, w_out_t, head, head_t,
    head_b, rim_far, field, z_sums, cross, along, dmixed, base, keep, send, acc_gain, acc_scale, head_cols, head_bias,
    mixed, crossed, sums,
):
    channels = mid.shape[1]
    taps = tables.at[1]
    along_far(par, part, far, taps, field)
    rest_of_conv(field, taps, crossed, mixed)
    sums[...] = jnp.zeros_like(sums)
    acc_gain[...] = jnp.zeros_like(acc_gain)
    acc_scale[...] = jnp.zeros_like(acc_scale)
    head_cols[...] = jnp.zeros_like(head_cols)
    head_bias[...] = jnp.zeros_like(head_bias)
    gain, scale = cols[1, :, GAIN : GAIN + 1], cols[1, :, SCALE : SCALE + 1]
    for step, first in steps():
        normal, inverse = normalise(tiles(mixed, first))
        normed = (normal * gain).astype(BF16)
        act, slope = gelu_parts(dot(w_in[1], normed) + b_in[:, 1:2])
        lifted = dot(w_out[1], act)
        final = (tiles(mid, first).astype(F32) + scale * lifted).astype(BF16)
        logits = dot(head[...], final) + head_b[...]
        raised = jnp.exp(logits - jnp.max(logits, axis=0, keepdims=True))
        probability = raised / jnp.sum(raised, axis=0, keepdims=True)
        classes = lax.broadcasted_iota(jnp.int32, logits.shape, 0)
        g_logits = probability - (labels[step] == classes).astype(F32)
        head_bias[...] += folded(g_logits)
        g_low = g_logits.astype(BF16)
        head_cols[...] += dot_t(final, g_low)
        grad = dot(head_t[...], g_low)
        acc_scale[...] += folded(grad * lifted)
        put(base, first, grad)
        g_lift = (grad * scale).astype(BF16)
        sums[0, :channels] += dot_t(g_lift, act)
        g_hid = (dot(w_out_t[1], g_lift) * slope).astype(BF16)
        sums[1] += dot_t(with_ones(normed), g_hid)
        g_norm = dot(w_in_t[1], g_hid)
        acc_gain[...] += folded(g_norm * normal)
        put(dmixed, first, normalise_back(g_norm, normal, inverse, gain))
    convolve_back(dmixed, crossed, taps, cross, along, z_sums)
    rim(par, along, taps, True, rim_far)
    keep[...] = sums[par[0]]
    send[...] = sums[1 - par[0]]


def total_of(ref):
    return jnp.sum(ref[...], axis=1, keepdims=True)


def taps_two_kernel(
    par, own, near, far, mx, cross, along, z_sums, select, base, tables, acc_gain, acc_scale, head_cols,
    head_bias, out, inner, rim_near, sums,
):
    rim(par, along, tables.at[1], False, rim_near)
    inside(along, tables.at[1], base, inner)
    value = tap_sums(par, own, near, far, mx, cross, along, z_sums, select, sums)
    lane = lax.broadcasted_iota(jnp.int32, out.shape, 1)
    value = jnp.where(lane == GAIN, total_of(acc_gain), value)
    value = jnp.where(lane == SCALE, total_of(acc_scale), value)
    for k in range(ROWS):
        value = jnp.where(lane == HEAD + k, head_cols[:, k : k + 1], value)
    out[...] = value
    out[:ROWS] = jnp.where(lane[:ROWS] == HEAD_BIAS, total_of(head_bias), out[:ROWS])


def taps_one_kernel(
    par, own, near, far, mx, cross, along, z_sums, select, acc_gain, gs_scale, out, sums
):
    value = tap_sums(par, own, near, far, mx, cross, along, z_sums, select, sums)
    lane = lax.broadcasted_iota(jnp.int32, out.shape, 1)
    value = jnp.where(lane == GAIN, total_of(acc_gain), value)
    out[...] = jnp.where(lane == SCALE, gs_scale[...], value)


def inside_kernel(par, along, base, tables, inner, rim_near):
    rim(par, along, tables.at[0], False, rim_near)
    inside(along, tables.at[0], base, inner)


def point_back_kernel(
    par, inner, near, far, act, slope, normed, cols, w_in_t, w_out, w_out_t,
    base, g_norm, keep, send, gs_scale, sums,
):
    channels = inner.shape[1]
    sums[...] = jnp.zeros_like(sums)
    scale = cols[0, :, SCALE : SCALE + 1]
    for step, first in steps():
        grad = tiles(inner, first) + (tiles(near, first).astype(F32) + tiles(far, first).astype(F32))
        put(base, first, grad)
        g_lift = (grad * scale).astype(BF16)
        sums[0, :channels] += dot_t(g_lift, act[step])
        g_hid = (dot(w_out_t[0], g_lift) * slope[step]).astype(BF16)
        sums[1] += dot_t(with_ones(tiles(normed, first)), g_hid)
        put(g_norm, first, dot(w_in_t[0], g_hid))
    spread = jnp.sum(sums[0, :channels] * w_out[0].astype(F32), axis=1, keepdims=True)
    gs_scale[...] = spread / scale
    keep[...] = sums[par[0]]
    send[...] = sums[1 - par[0]]


def conv_back_kernel(
    par, g_norm, normal, inverse, mxy, cols, tables, rim_far, z_sums, cross, along, acc_gain,
    dmixed,
):
    taps = tables.at[0]
    acc_gain[...] = jnp.zeros_like(acc_gain)
    for step, first in steps():
        value, unit = tiles(g_norm, first), tiles(normal, first)
        acc_gain[...] += folded(value * unit)
        put(dmixed, first, normalise_back(value, unit, inverse[step], cols[0, :, GAIN : GAIN + 1]))
    convolve_back(dmixed, mxy, taps, cross, along, z_sums)
    rim(par, along, taps, True, rim_far)


def last_kernel(inner, near, far, out, token, total):
    token[...] = jnp.zeros_like(token)

    def add(tile, carry):
        total[tile] = inner[tile] + (near[tile].astype(F32) + far[tile].astype(F32))
        return carry

    lax.fori_loop(0, OWN, add, 0, unroll=2)

    for first in range(0, inner.shape[1], ROWS):
        for tile in range(OWN):
            out[pl.ds(first * OWN + tile, ROWS, stride=OWN), :] = total[tile, first : first + ROWS, :]


def final_kernel(share, par, mine, other, g_in_t, g_bias, g_out, g_taps, g_gain, g_scale, g_head, g_head_b):
    channels = g_out.shape[1]
    even = par[0] == 0
    height = mine.shape[0] // 2
    weights = height - ROWS
    for s in range(2):
        here, stop = s * height, s * height + weights
        first = jnp.where(even, mine[here:stop], other[here:stop]) * share
        second = jnp.where(even, other[here:stop], mine[here:stop]) * share
        g_out[s] = first[:channels]
        g_in_t[s] = second[:channels]
        g_bias[s : s + 1] = second[channels : channels + 1]
        stats = mine[stop : stop + ROWS] + other[stop : stop + ROWS]
        rows = unfold_stats(stats, channels).T * share
        for axis in range(3):
            for k in range(TAPS):
                g_taps[axis, k, s : s + 1] = rows[axis * TAPS + k : axis * TAPS + k + 1]
        g_gain[s : s + 1] = rows[GAIN : GAIN + 1]
        g_scale[s : s + 1] = rows[SCALE : SCALE + 1]
    g_head[...] = rows[HEAD : HEAD + g_head.shape[0]]
    g_head_b[...] = rows[HEAD_BIAS : HEAD_BIAS + 1, : g_head_b.shape[1]]


def call(kernel, name, operands, outs, scratch=(), room=8, after=(), flops=0):
    smem = pl.BlockSpec(memory_space=pltpu.SMEM)
    vmem = pl.BlockSpec(memory_space=pltpu.VMEM)
    anywhere = pl.BlockSpec(memory_space=pl.ANY)
    count = len(operands)

    def run(*refs):
        kernel(*refs[:count], *refs[count + len(after) :])

    in_specs = [smem if x.dtype == jnp.int32 and x.shape == (1,) else vmem for x in operands]
    return pl.pallas_call(
        run,
        name=name,
        out_shape=tuple(outs),
        in_specs=in_specs + [anywhere] * len(after),
        out_specs=tuple([vmem] * len(outs)),
        scratch_shapes=list(scratch),
        compiler_params=pltpu.CompilerParams(vmem_limit_bytes=room * MIB),
        cost_estimate=pl.CostEstimate(flops=flops, bytes_accessed=0, transcendentals=0),
    )(*operands, *after)


def pinned(dims, dtype=F32):
    return pltpu.VMEM(dims, dtype)


def shape(dims, dtype=F32):
    return jax.ShapeDtypeStruct(dims, dtype)


def near_swap(value):
    count = lax.axis_size("track")
    return lax.ppermute(value, "track", [(i, i ^ 1) for i in range(count)])


def far_swap(value):
    count = lax.axis_size("track")
    pairs = []
    for i in range(1, count - 1, 2):
        pairs += [(i, i + 1), (i + 1, i)]
    return lax.ppermute(value, "track", pairs)


def bit_swap(value, step):
    count = lax.axis_size("track")
    return lax.ppermute(value, "track", [(i, i ^ step) for i in range(count)])


def on_device(
    volume, labels, conv_taps, norm_gain, weight_in, bias_in, weight_out, layer_scale, head_weight, head_bias
):
    channels, planes, rows, depth = volume.shape
    hidden = weight_in.shape[1]
    classes = head_weight.shape[0]
    devices = lax.axis_size("track")
    share = 1.0 / float(devices * planes * rows * depth)
    par = (lax.axis_index("track") % 2).astype(jnp.int32).reshape(1)
    parts = OWN // CHUNK

    flat = volume.reshape(channels * OWN, depth)
    near = near_swap(flat)
    far = far_swap(flat)
    cols = jnp.swapaxes(
        jnp.concatenate(
            [conv_taps.reshape(2, 3 * TAPS, channels), norm_gain[:, None], layer_scale[:, None]], axis=1
        ), 1, 2,
    )
    b_in = bias_in.T
    head = jnp.zeros((ROWS, channels), BF16).at[:classes].set(head_weight)
    head_b = jnp.full((ROWS,), -1e30, F32).at[:classes].set(head_bias)[:, None]
    flat_labels = labels.reshape(parts, 1, CHUNK * depth)

    low = shape((OWN, channels, depth), BF16)
    full = shape((OWN, channels, depth))
    half = shape((channels + PAIR, hidden))
    s_full = pltpu.VMEM((OWN, channels, depth), F32)
    s_wide = pltpu.VMEM((channels * OWN, depth), F32)
    s_sums = pltpu.VMEM((2, channels + PAIR, hidden), F32)
    k_full = pinned((OWN, channels, depth))
    k_half = pinned((channels + PAIR, hidden))
    k_stat = pinned((channels, LANES))

    small = (cols, b_in, weight_in, weight_out, head, head_b, flat_labels)
    (tables, cols, b_in, w_in, w_in_t, w_out, w_out_t, head, head_t, head_b, flat_labels, select) = call(
        tables_kernel, "tables", small,
        [pinned((2, 4 * TAPS, channels, LANES)), pinned(cols.shape), pinned(b_in.shape),
         pinned(weight_in.shape, BF16), pinned(weight_out.shape, BF16), pinned(weight_out.shape, BF16),
         pinned(weight_in.shape, BF16), pinned(head.shape, BF16), pinned((channels, ROWS), BF16),
         pinned(head_b.shape), pinned(flat_labels.shape, jnp.int32),
         pinned((3 * TAPS * LANES, LANES), BF16)],
    )
    part, own_kept, near_kept = call(
        start_kernel, "start_one", (par, flat, near, tables), [k_full, k_full, k_full], [s_wide],
    )
    mid, mixed_one, far_kept, mx_one, mxy_one = call(
        forward_kernel, "forward_one", (par, far, part, own_kept, cols, tables, w_in, b_in, w_out),
        [low, k_full, k_full, k_full, k_full], [s_wide], 8,
    )
    near = near_swap(mid)
    far = far_swap(mid)
    normed, normal, inverse, act, slope = call(
        save_kernel, "save_one", (mixed_one, cols, w_in, b_in),
        [pinned((OWN, channels, depth), BF16), k_full, pinned((parts, 1, CHUNK * depth)),
         pinned((parts, hidden, CHUNK * depth), BF16), pinned((parts, hidden, CHUNK * depth))],
        (), 16,
    )
    (part,) = call(
        middle_kernel, "start_two", (par, mid, near, tables), [k_full], (), 4, after=(inverse,)
    )
    k_taps = pinned((TAPS, channels, LANES))
    s_taps = pltpu.VMEM((2 * TAPS, channels, LANES), F32)
    (rim_far, mx, z_sums, cross, along, dmixed, base, keep, send,
     acc_gain, acc_scale, head_cols, head_lanes) = call(
        turn_kernel, "turn_two",
        (par, far, part, mid, flat_labels, cols, tables, w_in, w_in_t, b_in, w_out, w_out_t,
         head, head_t, head_b),
        [low, k_full, k_taps, k_full, k_full, k_full, k_full, k_half, half, k_stat, k_stat, pinned((channels, ROWS)),
         pinned((ROWS, LANES))],
        [s_full, s_full, s_sums], 24,
    )
    rim_far = far_swap(rim_far)
    got = near_swap(send)
    stats, inner, rim_near = call(
        taps_two_kernel, "taps_two",
        (par, mid, near, far, mx, cross, along, z_sums, select, base, tables, acc_gain, acc_scale, head_cols,
         head_lanes),
        [k_stat, k_full, low], [s_taps], 8, after=(got,),
    )
    rim_near = near_swap(rim_near)
    tall = shape((channels + PAIR + ROWS, hidden))
    k_tall = pinned(tall.shape)
    tall_low = shape((channels + 2 * PAIR, hidden), BF16)
    two, two_low = call(
        pack_kernel, "pack_two", (keep, got, stats), [k_tall, tall_low], (), 4, after=(inner,)
    )
    got = [bit_swap(two_low, step) for step in (4, 8, 12)]
    base, g_norm, keep, send, gs_scale = call(
        point_back_kernel, "point_back_one",
        (par, inner, rim_near, rim_far, act, slope, normed, cols, w_in_t, w_out, w_out_t),
        [k_full, k_full, k_half, half, pinned((channels, 1))], [s_sums], 8,
    )
    got_two, got = got, near_swap(send)
    rim_far, z_sums, cross, along, acc_gain = call(
        conv_back_kernel, "conv_back_one", (par, g_norm, normal, inverse, mxy_one, cols, tables),
        [low, k_taps, k_full, k_full, k_stat], [s_full], 8,
    )
    rim_far = far_swap(rim_far)
    half_low = shape((channels + PAIR, hidden), BF16)
    (two,) = call(
        spread_two_kernel, "sums_two", (two, *got_two), [k_tall], (), 4, after=(along,), flops=4 * 10**10
    )
    one, one_low = call(first_kernel, "sums_one_a", (keep, got), [k_half, half_low], (), 4, after=(two,))
    got = [bit_swap(one_low, step) for step in (4, 8, 12)]
    (stats,) = call(
        taps_one_kernel, "taps_one",
        (par, own_kept, near_kept, far_kept, mx_one, cross, along, z_sums, select, acc_gain, gs_scale),
        [k_stat], [s_taps], 8, after=(two,),
    )
    (one,) = call(spread_kernel, "sums_one_b", (one, *got), [k_half], (), 4, after=(stats,), flops=4 * 10**9)
    stats, stats_low = call(
        stats_pack_kernel, "pack_stats", (stats,), [pinned((ROWS, hidden)), shape((PAIR, hidden), BF16)], (), 4
    )
    got_stats = [bit_swap(stats_low, step) for step in (4, 8, 12)]
    inner, rim_near = call(
        inside_kernel, "inside_one", (par, along, base, tables), [k_full, low], (), 4
    )
    rim_near = near_swap(rim_near)
    both_shape = (2 * tall.shape[0], hidden)
    both, both_low = call(
        spread_one_kernel, "sums_one", (one, stats, *got_stats, two),
        [pinned(both_shape), shape((2 * tall_low.shape[0], hidden), BF16)], (), 4, after=(inner,),
    )
    got = bit_swap(both_low, 2)
    grad, token = call(
        last_kernel, "last", (inner, rim_near, rim_far),
        [shape((channels * OWN, depth)), pinned((ROWS, LANES))], [s_full], 4,
        after=(both,),
    )
    (both,) = call(joined_kernel, "sums_last", (both, got), [shape(both_shape)], (), 4, after=(token,))
    step = 16
    while step < devices:
        both = both + bit_swap(both, step)
        step *= 2
    g_in_t, g_bias, g_out, g_taps, g_gain, g_scale, g_head, g_head_b = call(
        functools.partial(final_kernel, share), "final", (par, both, near_swap(both)),
        [shape((2, channels, hidden)), shape((2, hidden)), shape((2, channels, hidden)),
         shape((3, TAPS, 2, channels)), shape((2, channels)), shape((2, channels)),
         shape((classes, channels)), shape((1, classes))],
    )
    return (
        grad.reshape(volume.shape), jnp.moveaxis(g_taps, 2, 0), g_gain, jnp.swapaxes(g_in_t, 1, 2), g_bias, g_out, g_scale,
        g_head, g_head_b.reshape(classes),
    )


def solution(mesh):
    placed = (
        P(None, ("groups", "track"), None, None),
        P(("groups", "track"), None, None),
        P(), P(), P(), P(), P(), P(), P(), P(),
    )
    return jax.shard_map(
        on_device,
        mesh=mesh,
        in_specs=placed,
        out_specs=(
            P(None, ("groups", "track"), None, None),
            P("groups", None, None, None),
            P("groups", None),
            P("groups", None, None),
            P("groups", None),
            P("groups", None, None),
            P("groups", None),
            P("groups", None),
            P("groups"),
        ),
        check_vma=False,
    )
```
